32 devices in a mesh: dp: 2 (over x), aa: 4 (over y, core), ba: 4 (over z).
Axes of the slice: x: 2, y: 2, z: 4, core: 2. Of those that a mesh axis runs over, the one named last changes fastest.
Arguments:
- inputs: bfloat16 [33856, 768], P(('dp', 'aa', 'ba')), may hold values from -6 to 6
- cotangent: bfloat16 [33856, 768], P(('dp', 'aa', 'ba')), may hold values from -6 to 6
- split_at: int32 [64], P(('dp', 'aa', 'ba')), may hold values from 264 to 529, as said below
- ln1_gain: bfloat16 [768], P(('aa', 'ba')), may hold values from 0.25 to 1.75
- ln1_bias: bfloat16 [768], P(('aa', 'ba')), may hold values from -3 to 3
- w_qkv: bfloat16 [768, 3, 768], P('ba', None, 'aa'), may hold values from -0.21875 to 0.21875
- q_bias: bfloat16 [768], P(('aa', 'ba')), may hold values from -4 to 4
- v_bias: bfloat16 [768], P(('aa', 'ba')), may hold values from -4 to 4
- w_out: bfloat16 [768, 768], P('aa', 'ba'), may hold values from -0.875 to 0.875
- o_bias: bfloat16 [768], P(('aa', 'ba')), may hold values from -4 to 4
- ln2_gain: bfloat16 [768], P(('aa', 'ba')), may hold values from 0.25 to 1.75
- ln2_bias: bfloat16 [768], P(('aa', 'ba')), may hold values from -3 to 3
- w_up: bfloat16 [768, 3072], P('ba', 'aa'), may hold values from -0.21875 to 0.21875
- up_bias: bfloat16 [3072], P(('aa', 'ba')), may hold values from -4 to 4
- w_down: bfloat16 [3072, 768], P('aa', 'ba'), may hold values from -0.109375 to 0.109375
- down_bias: bfloat16 [768], P(('aa', 'ba')), may hold values from -4 to 4
Outputs:
- output: bfloat16 [33856, 768], P(('dp', 'aa', 'ba'))
- grad_inputs: bfloat16 [33856, 768], P(('dp', 'aa', 'ba'))
- grad_ln1_gain: float32 [768], P(('aa', 'ba'))
- grad_ln1_bias: float32 [768], P(('aa', 'ba'))
- grad_w_qkv: float32 [768, 3, 768], P('ba', None, 'aa')
- grad_q_bias: float32 [768], P(('aa', 'ba'))
- grad_v_bias: float32 [768], P(('aa', 'ba'))
- grad_w_out: float32 [768, 768], P('aa', 'ba')
- grad_o_bias: float32 [768], P(('aa', 'ba'))
- grad_ln2_gain: float32 [768], P(('aa', 'ba'))
- grad_ln2_bias: float32 [768], P(('aa', 'ba'))
- grad_w_up: float32 [768, 3072], P('ba', 'aa')
- grad_up_bias: float32 [3072], P(('aa', 'ba'))
- grad_w_down: float32 [3072, 768], P('aa', 'ba')
- grad_down_bias: float32 [768], P(('aa', 'ba'))
The draws below stay inside these ranges and needn't reach their ends.
Inputs may be any that keep to these rules, and one draw needn't show every extreme that they name: `split_at`: each slot of 529 patches holds either one full strip (entry 529) or two half strips, the first of 264 patches (entry 264); the first slot is a full strip and the second a pair.
All inputs are finite; a program needn't handle non-finite values.
Results may differ from the reference program's by a relative error of at most 0.02.
Values may be sent and summed in bfloat16 or wider, within the bound.
A program may use at most 256 MiB of HBM per device.

```python
import math
import jax
import jax.numpy as jnp
from jax import lax

D = 768
HEADS = 12
HEAD_DIM = 64
FF = 3072
SLOT = 529
SLOTS = 64
TOKENS = 33856


def draw_split_at(key, part):
    key = jax.random.fold_in(key, 7)
    coins = jax.random.randint(key, (SLOTS,), 0, 2)
    coins = coins.at[0].set(0).at[1].set(1)
    return jnp.where(coins == 0, SLOT, SLOT // 2).astype(jnp.int32)


def block_levels(stream_key, shape, shards, least, high):
    loudness = 1.0
    for dim, parts in shards:
        steps = jax.random.uniform(jax.random.fold_in(jax.random.fold_in(stream_key, 6), dim), (parts,), jnp.float32, least / len(shards), high / len(shards))
        loudness = loudness * jnp.repeat(jnp.exp(steps), shape[dim] // parts).reshape((-1,) + (1,) * (len(shape) - 1 - dim))
    return loudness


def noise(own_key, dims, width, most, shards=(), held_as=jnp.bfloat16):
    array = width * jax.random.normal(own_key, dims, jnp.float32)
    if shards:
        array = array * block_levels(own_key, dims, shards, -0.22, 0.18)
    return jnp.clip(array, -most, most).astype(held_as)


def setup_inputs(seed: int = 0) -> dict:
    keys = jax.random.split(jax.random.key(seed), 17)
    inputs = noise(keys[0], (TOKENS, D), 1.0, 6.0, ((0, 32),))
    cotangent = noise(keys[1], (TOKENS, D), 1.0, 6.0, ((0, 32),))
    split_at = draw_split_at(jax.random.fold_in(keys[16], 71), 0)
    ln1_gain = jnp.clip(1.0 + 0.15 * jax.random.normal(keys[3], (D,), jnp.float32), 0.25, 1.75).astype(jnp.bfloat16)
    ln1_bias = noise(keys[4], (D,), 0.3, 3.0, ((0, 16),))
    w_qkv = noise(keys[5], (D, 3, D), D ** -0.5, 0.21875, ((0, 4), (2, 4)))
    q_bias = noise(keys[6], (D,), 0.5, 4.0, ((0, 16),))
    v_bias = noise(keys[7], (D,), 0.5, 4.0, ((0, 16),))
    w_out = noise(keys[8], (D, D), (D // 16) ** -0.5, 0.875, ((0, 4), (1, 4)))
    o_bias = noise(keys[9], (D,), 0.5, 4.0, ((0, 16),))
    ln2_gain = jnp.clip(1.0 + 0.15 * jax.random.normal(keys[10], (D,), jnp.float32), 0.25, 1.75).astype(jnp.bfloat16)
    ln2_bias = noise(keys[11], (D,), 0.3, 3.0, ((0, 16),))
    w_up = noise(keys[12], (D, FF), D ** -0.5, 0.21875, ((0, 4), (1, 4)))
    up_bias = noise(keys[13], (FF,), 0.5, 4.0, ((0, 16),))
    w_down = noise(keys[14], (FF, D), FF ** -0.5, 0.109375, ((0, 4), (1, 4)))
    down_bias = noise(keys[15], (D,), 0.5, 4.0, ((0, 16),))
    return dict(inputs=inputs, cotangent=cotangent, split_at=split_at, ln1_gain=ln1_gain, ln1_bias=ln1_bias, w_qkv=w_qkv, q_bias=q_bias, v_bias=v_bias, w_out=w_out, o_bias=o_bias, ln2_gain=ln2_gain, ln2_bias=ln2_bias, w_up=w_up, up_bias=up_bias, w_down=w_down, down_bias=down_bias)


@jax.custom_vjp
def low(v):
    return lax.optimization_barrier(v.astype(jnp.bfloat16)).astype(jnp.float32)

@jax.custom_vjp
def low_back(v):
    return v

def low_keep(v):
    return (low(v), None)

def low_pass(kept, grad):
    return (grad,)

def back_keep(v):
    return (v, None)

def back_low(kept, grad):
    return (low(grad),)
low.defvjp(low_keep, low_pass)
low_back.defvjp(back_keep, back_low)

def layer_norm(values, gains, offset):
    centre = lax.optimization_barrier(jnp.mean(values, axis=-1, keepdims=True))
    shifted = values - centre
    spread = lax.optimization_barrier(jnp.mean(shifted * shifted, axis=-1, keepdims=True))
    return shifted * lax.rsqrt(spread + 1e-06) * gains + offset

def product(left, right):
    return jnp.dot(left, right, precision=lax.Precision.HIGHEST)

def segment_mask(split_one):
    places = jnp.arange(SLOT)
    first_part = places < split_one
    return first_part[:, None] == first_part[None, :]

def slot_attention(members):
    queries, keys_in, values_in, split_one = members
    scores = jnp.einsum('qhd,khd->hqk', queries, keys_in, precision=lax.Precision.HIGHEST)
    scores = low_back(scores * (1.0 / math.sqrt(HEAD_DIM)))
    scores = jnp.where(segment_mask(split_one)[None], scores, -1e+30)
    softmax_w = low(jax.nn.softmax(scores, axis=-1))
    return jnp.einsum('hqk,khd->qhd', softmax_w, values_in, precision=lax.Precision.HIGHEST)

def forward(inputs, ln1_gain, ln1_bias, w_qkv, q_bias, v_bias, w_out, o_bias, ln2_gain, ln2_bias, w_up, up_bias, w_down, down_bias, split_at):
    normed = low(layer_norm(inputs, ln1_gain, ln1_bias))
    mixed = jnp.einsum('td,dkc->tkc', normed, w_qkv, precision=lax.Precision.HIGHEST)
    queries = low_back(low(mixed[:, 0] + q_bias))
    keys_all = low_back(low(mixed[:, 1]))
    values_all = low_back(low(mixed[:, 2] + v_bias))
    slot_shape = (-1, SLOT, HEADS, HEAD_DIM)
    attended = lax.map(jax.checkpoint(slot_attention), (queries.reshape(slot_shape), keys_all.reshape(slot_shape), values_all.reshape(slot_shape), split_at))
    attended = low_back(low(attended.reshape(-1, D)))
    branch = low_back(product(attended, w_out) + o_bias)
    middle = inputs + branch
    normed_two = low(layer_norm(middle, ln2_gain, ln2_bias))
    hidden = low_back(product(normed_two, w_up) + up_bias)
    activated = low(jax.nn.gelu(hidden, approximate=False))
    return middle + product(activated, w_down) + down_bias

def reference(inputs, cotangent, split_at, ln1_gain, ln1_bias, w_qkv, q_bias, v_bias, w_out, o_bias, ln2_gain, ln2_bias, w_up, up_bias, w_down, down_bias):
    floats = tuple((member.astype(jnp.float32) for member in (inputs, ln1_gain, ln1_bias, w_qkv, q_bias, v_bias, w_out, o_bias, ln2_gain, ln2_bias, w_up, up_bias, w_down, down_bias)))

    def apply_layer(*members):
        return forward(*members, split_at)
    output, pullback = jax.vjp(apply_layer, *floats)
    grads = pullback(cotangent.astype(jnp.float32))
    return (output.astype(jnp.bfloat16), grads[0].astype(jnp.bfloat16), grads[1], grads[2], grads[3], grads[4], grads[5], grads[6], grads[7], grads[8], grads[9], grads[10], grads[11], grads[12], grads[13])
```

```python
import functools
import math

import jax
import jax.numpy as jnp
from jax import lax
from jax.experimental import pallas as pl
from jax.experimental.pallas import tpu as pltpu
from jax.sharding import PartitionSpec as P

D = 768
HEADS = 12
HEAD_DIM = 64
SLOT = 529
PAD = 544
ROWS = 2 * PAD
GROUP = 192
BIG = 1e30
MESH = pl.DeviceIdType.MESH
F32 = jnp.float32
BF16 = jnp.bfloat16
MIB = 1 << 20

NT = (((1,), (1,)), ((), ()))
NN = (((1,), (0,)), ((), ()))
TN = (((0,), (0,)), ((), ()))

TAIL = (
    0.11962926248861097,
    0.12075451364069298,
    0.09991001218129214,
    0.12857310923328652,
    -0.0537053561953165,
    0.20637712218096793,
    -0.15721681637037743,
    0.03567808025645831,
)


def dot(left, right, dims=NN):
    return lax.dot_general(left, right, dims, preferred_element_type=F32)


def exact_dot(left, right, dims=NN):
    return lax.dot_general(
        left, right, dims, preferred_element_type=F32, precision=lax.Precision.HIGHEST
    )


def place():
    dp, aa, ba = lax.axis_index("dp"), lax.axis_index("aa"), lax.axis_index("ba")
    half, core = lax.rem(dp, 2), lax.rem(aa, 2)
    peers = {
        "x": (dp + 1 - 2 * half, aa, ba),
        "y": (dp, lax.rem(aa + 2, 4), ba),
        "c": (dp, aa + 1 - 2 * core, ba),
        "z1": (dp, aa, lax.rem(ba + 1, 4)),
        "z2": (dp, aa, lax.rem(ba + 2, 4)),
        "z3": (dp, aa, lax.rem(ba + 3, 4)),
    }
    return dp, aa, ba, half, core, peers


def greet(peers):
    barrier = pltpu.get_barrier_semaphore()
    for peer in peers.values():
        pl.semaphore_signal(barrier, inc=1, device_id=peer, device_id_type=MESH)
    pl.semaphore_wait(barrier, len(peers))


class Sends:
    def __init__(self, send_sem, recv_sem, peers):
        self.send_sem, self.recv_sem, self.peers = send_sem, recv_sem, peers
        self.made = {}

    def start(self, name, src, dst, peer):
        at = len(self.made)
        copy = pltpu.make_async_remote_copy(
            src_ref=src,
            dst_ref=dst,
            send_sem=self.send_sem.at[at],
            recv_sem=self.recv_sem.at[at],
            device_id=self.peers[peer],
            device_id_type=MESH,
        )
        copy.start()
        self.made[name] = copy

    def arrived(self, *names):
        for name in names:
            self.made[name].wait_recv()

    def finish(self):
        for copy in self.made.values():
            copy.wait_send()


def sixteen(value):
    return pl.multiple_of(value, 16)


def gather_kernel(pa, pb, pc, slab, wa, wb, wc, vv, send_sem, recv_sem, own_sem):
    dp, aa, ba, half, core, peers = place()
    greet(peers)
    sends = Sends(send_sem, recv_sem, peers)
    ay = lax.rem(aa + 2, 4)
    other = [lax.rem(ba + j, 4) for j in (1, 2, 3)]
    big = pl.ds(sixteen(64 * half), 64)
    big_not = pl.ds(sixteen(64 - 64 * half), 64)
    small = pl.ds(sixteen(128 + 32 * half), 32)
    rest = pl.ds(128, 64)
    own = [
        pltpu.make_async_copy(part, whole.at[aa, ba], own_sem.at[i])
        for i, (part, whole) in enumerate(((pa, wa), (pb, wb), (pc, wc), (slab, vv)))
    ]
    for copy in own:
        copy.start()
    every = (("a", pa, wa), ("b", pb, wb), ("c", pc, wc))
    for j in (1, 2, 3):
        sends.start(("v", j), slab, vv.at[aa, ba], f"z{j}")
    for n, part, w in every:
        for j in (1, 2, 3):
            sends.start((n, "z", j), part.at[big], w.at[aa, ba, big], f"z{j}")
        sends.start((n, "y"), part.at[small], w.at[aa, ba, small], "y")
        for j in (1, 2, 3):
            sends.start((n, "zs", j), part.at[small], w.at[aa, ba, small], f"z{j}")
    for copy in own:
        copy.wait()
    sends.arrived(*[("v", j) for j in (1, 2, 3)])
    sends.start(("v", "y"), vv.at[aa], vv.at[aa], "y")
    sends.start(("v", "c"), vv.at[aa], vv.at[aa], "c")
    for n, part, w in every:
        sends.arrived(*[(n, "z", j) for j in (1, 2, 3)])
        for j, z in zip((1, 2, 3), other):
            sends.start((n, "x", j), w.at[aa, z, big], w.at[aa, z, big], "x")
        sends.start((n, "yb"), w.at[aa, :, big], w.at[aa, :, big], "y")
        sends.arrived((n, "y"))
        for j in (1, 2, 3):
            sends.start((n, "zy", j), w.at[ay, ba, small], w.at[ay, ba, small], f"z{j}")
        sends.arrived(*[(n, "zs", j) for j in (1, 2, 3)])
        for j, z in zip((1, 2, 3), other):
            sends.start((n, "xs", j), w.at[aa, z, small], w.at[aa, z, small], "x")
        sends.start((n, "c0"), w.at[aa, :, big], w.at[aa, :, big], "c")
    sends.arrived(("v", "y"), ("v", "c"))
    sends.start(("v", "cy"), vv.at[ay], vv.at[ay], "c")
    for n, part, w in every:
        sends.arrived(*[(n, "x", j) for j in (1, 2, 3)])
        sends.start((n, "yn"), w.at[aa, :, big_not], w.at[aa, :, big_not], "y")
        sends.arrived(*[(n, "zy", j) for j in (1, 2, 3)])
        sends.start((n, "xy"), w.at[ay, :, small], w.at[ay, :, small], "x")
        sends.arrived((n, "yb"))
        sends.start((n, "c1"), w.at[aa, :, big_not], w.at[aa, :, big_not], "c")
        sends.start((n, "c2"), w.at[ay, :, big], w.at[ay, :, big], "c")
    for n, part, w in every:
        sends.arrived(*[(n, "xs", j) for j in (1, 2, 3)])
        sends.start((n, "c3"), w.at[aa, :, rest], w.at[aa, :, rest], "c")
        sends.arrived((n, "yn"))
        sends.start((n, "c4"), w.at[ay, :, big_not], w.at[ay, :, big_not], "c")
        sends.arrived((n, "xy"))
        sends.start((n, "c5"), w.at[ay, :, rest], w.at[ay, :, rest], "c")
    sends.arrived(("v", "cy"))
    for n, part, w in every:
        sends.arrived(*[(n, f"c{i}") for i in range(6)])
    sends.finish()


def gather(pa, pb, pc, slab):
    whole = jax.ShapeDtypeStruct((4, 4, GROUP, D), BF16)
    count = 3 * 26 + 6
    return pl.pallas_call(
        gather_kernel,
        out_shape=(whole, whole, whole, jax.ShapeDtypeStruct((4, 4, 16, 128), BF16)),
        in_specs=[pl.BlockSpec(memory_space=pl.ANY)] * 4,
        out_specs=[pl.BlockSpec(memory_space=pl.ANY)] * 4,
        scratch_shapes=[
            pltpu.SemaphoreType.DMA((count,)),
            pltpu.SemaphoreType.DMA((count,)),
            pltpu.SemaphoreType.DMA((4,)),
        ],
        compiler_params=pltpu.CompilerParams(
            collective_id=0, has_side_effects=True, vmem_limit_bytes=48 * MIB
        ),
    )(pa, pb, pc, slab)


LINES = 16 * 8


def add_into(acc, at, more, more_at, lines):
    acc[at] = (acc[at].astype(F32) + more[more_at].astype(F32)).astype(BF16)


def scatter_kernel(ga, gb, gc, gv, oa, ob, oc, ov, *scratch):
    parts = []
    for i in range(3):
        parts.append(scratch[12 * i : 12 * i + 12])
    vh, vc, vy, vz, vx, send_sem, recv_sem, own_sem = scratch[36:]
    dp, aa, ba, half, core, peers = place()
    greet(peers)
    sends = Sends(send_sem, recv_sem, peers)
    yy = aa // 2
    yn = 1 - yy
    other = [lax.rem(ba + j, 4) for j in (1, 2, 3)]
    mine = sixteen(64 * half)
    theirs = sixteen(64 - 64 * half)
    smine = sixteen(128 + 32 * half)
    stheirs = sixteen(160 - 32 * half)
    every = list(zip("abc", (ga, gb, gc), (oa, ob, oc), parts))
    own = []
    for i, (n, g, o, p) in enumerate(every):
        for y in (0, 1):
            own.append(
                pltpu.make_async_copy(g.at[2 * y + core], p[0].at[y], own_sem.at[2 * i + y])
            )
            own[-1].start()
            sends.start((n, "c", y), g.at[2 * y + 1 - core], p[1].at[y], "c")
    for y in (0, 1):
        own.append(pltpu.make_async_copy(gv.at[2 * y + core], vh.at[y], own_sem.at[6 + y]))
        own[-1].start()
        sends.start(("v", "c", y), gv.at[2 * y + 1 - core], vc.at[y], "c")
    for copy in own:
        copy.wait()
    for y in (0, 1):
        sends.arrived(("v", "c", y))
    vh[...] = vh[...] + vc[...]
    sends.start(("v", "y"), vh.at[yn], vy, "y")
    for n, g, o, (h, rc, ry, rx, rz, rf, sx, sz, sy, sf, f0, f1) in every:
        for y in (0, 1):
            sends.arrived((n, "c", y))

        @pl.loop(0, 8)
        def _(i):
            y, z = i // 4, lax.rem(i, 4)
            h[y, z] = (h[y, z].astype(F32) + rc[y, z].astype(F32)).astype(BF16)

        sends.start((n, "y"), h.at[yn, :, pl.ds(0, 128)], ry, "y")
        sends.start((n, "x"), h.at[:, :, pl.ds(stheirs, 32)], sx, "x")
    sends.arrived(("v", "y"))
    vh[yy] = vh[yy] + vy[...]
    for j, z in zip((1, 2, 3), other):
        sends.start(("v", "z", j), vh.at[yy, z], vz.at[j - 1], f"z{j}")
    for n, g, o, (h, rc, ry, rx, rz, rf, sx, sz, sy, sf, f0, f1) in every:
        sends.arrived((n, "y"))

        @pl.loop(0, 4)
        def _(z):
            rows = pl.ds(0, 128)
            h[yy, z, rows] = (h[yy, z, rows].astype(F32) + ry[z].astype(F32)).astype(BF16)

        sends.start((n, "x2"), h.at[yy, :, pl.ds(theirs, 64)], rx, "x")
        sends.arrived((n, "x"))

        @pl.loop(0, 8)
        def _(i):
            y, z = i // 4, lax.rem(i, 4)
            rows = pl.ds(smine, 32)
            h[y, z, rows] = (h[y, z, rows].astype(F32) + sx[y, z].astype(F32)).astype(BF16)

        for j, z in zip((1, 2, 3), other):
            sends.start((n, "zs", j), h.at[:, z, pl.ds(smine, 32)], sz.at[j - 1], f"z{j}")
    for j in (1, 2, 3):
        sends.arrived(("v", "z", j))
    vh[yy, ba] = vh[yy, ba] + (vz[0] + vz[1] + vz[2])
    sends.start(("v", "x"), vh.at[yy, ba], vx, "x")
    for n, g, o, (h, rc, ry, rx, rz, rf, sx, sz, sy, sf, f0, f1) in every:
        sends.arrived((n, "x2"))

        @pl.loop(0, 4)
        def _(z):
            rows = pl.ds(mine, 64)
            h[yy, z, rows] = (h[yy, z, rows].astype(F32) + rx[z].astype(F32)).astype(BF16)

        for j, z in zip((1, 2, 3), other):
            sends.start((n, "z", j), h.at[yy, z, pl.ds(mine, 64)], rz.at[j - 1], f"z{j}")
        for j in (1, 2, 3):
            sends.arrived((n, "zs", j))
        for y in (0, 1):
            rows = pl.ds(smine, 32)
            total = h[y, ba, rows].astype(F32)
            for j in range(3):
                total = total + sz[j, y].astype(F32)
            h[y, ba, rows] = total.astype(BF16)
        sends.start((n, "ys"), h.at[yn, ba, pl.ds(smine, 32)], sy, "y")
    for n, g, o, (h, rc, ry, rx, rz, rf, sx, sz, sy, sf, f0, f1) in every:
        for j in (1, 2, 3):
            sends.arrived((n, "z", j))
        total = h[yy, ba, pl.ds(mine, 64)].astype(F32)
        for j in range(3):
            total = total + rz[j].astype(F32)
        f0[...] = total.astype(BF16)
        sends.start((n, "f0"), f0, rf, "x")
        sends.arrived((n, "ys"))
        f1[...] = (h[yy, ba, pl.ds(smine, 32)].astype(F32) + sy[...].astype(F32)).astype(BF16)
        sends.start((n, "f1"), f1, sf, "x")
    sends.arrived(("v", "x"))
    ov[...] = vh[yy, ba] + vx[...]
    for n, g, o, (h, rc, ry, rx, rz, rf, sx, sz, sy, sf, f0, f1) in every:
        o[pl.ds(mine, 64)] = f0[...].astype(F32)
        o[pl.ds(smine, 32)] = f1[...].astype(F32)
        sends.arrived((n, "f0"), (n, "f1"))
        o[pl.ds(theirs, 64)] = rf[...].astype(F32)
        o[pl.ds(stheirs, 32)] = sf[...].astype(F32)
    sends.finish()


def scatter(ga, gb, gc, gv):
    out = jax.ShapeDtypeStruct((GROUP, D), F32)
    one = [
        pltpu.VMEM((2, 4, GROUP, D), BF16),
        pltpu.VMEM((2, 4, GROUP, D), BF16),
        pltpu.VMEM((4, 128, D), BF16),
        pltpu.VMEM((4, 64, D), BF16),
        pltpu.VMEM((3, 64, D), BF16),
        pltpu.VMEM((64, D), BF16),
        pltpu.VMEM((2, 4, 32, D), BF16),
        pltpu.VMEM((3, 2, 32, D), BF16),
        pltpu.VMEM((32, D), BF16),
        pltpu.VMEM((32, D), BF16),
        pltpu.VMEM((64, D), BF16),
        pltpu.VMEM((32, D), BF16),
    ]
    vectors = [
        pltpu.VMEM((2, 4, 16, 128), F32),
        pltpu.VMEM((2, 4, 16, 128), F32),
        pltpu.VMEM((4, 16, 128), F32),
        pltpu.VMEM((3, 16, 128), F32),
        pltpu.VMEM((16, 128), F32),
    ]
    count = 3 * 14 + 7
    return pl.pallas_call(
        scatter_kernel,
        out_shape=(out, out, out, jax.ShapeDtypeStruct((16, 128), F32)),
        in_specs=[pl.BlockSpec(memory_space=pl.ANY)] * 4,
        out_specs=[pl.BlockSpec(memory_space=pltpu.VMEM)] * 4,
        scratch_shapes=one * 3
        + vectors
        + [
            pltpu.SemaphoreType.DMA((count,)),
            pltpu.SemaphoreType.DMA((count,)),
            pltpu.SemaphoreType.DMA((8,)),
        ],
        compiler_params=pltpu.CompilerParams(
            collective_id=1, has_side_effects=True, vmem_limit_bytes=48 * MIB
        ),
    )(ga, gb, gc, gv)


def slab_maps():
    lane = lax.broadcasted_iota(jnp.int32, (128, D), 0)
    column = lax.broadcasted_iota(jnp.int32, (128, D), 1)
    spread = (lax.rem(column, 48) == lane).astype(F32)
    line = lax.broadcasted_iota(jnp.int32, (256, D), 0)
    block = lax.broadcasted_iota(jnp.int32, (256, D), 1) // 48
    device, kind = line // 16, lax.rem(line, 16)
    wanted = jnp.where(kind < 8, device, 4 * lax.rem(device, 4) + kind - 8)
    keep = jnp.where((wanted == block) & (kind < 12), 1.0, 0.0).astype(F32)
    line = lax.broadcasted_iota(jnp.int32, (16, 256), 1)
    out = lax.broadcasted_iota(jnp.int32, (16, 256), 0)
    device, kind = line // 16, lax.rem(line, 16)
    choose = (jnp.where(kind < 8, kind, 8 + device // 4) == out).astype(F32)
    return spread, keep, choose


def norm_parts(value):
    centre = jnp.mean(value, axis=-1, keepdims=True)
    shifted = value - centre
    spread = jnp.mean(shifted * shifted, axis=-1, keepdims=True)
    return shifted, lax.rsqrt(spread + 1e-6)


def mask_columns(split, keys):
    place_ = lax.broadcasted_iota(jnp.int32, (PAD, HEAD_DIM), 0)
    column = lax.broadcasted_iota(jnp.int32, (PAD, HEAD_DIM), 1)
    first = jnp.where(place_ < split, 1.0, 0.0)
    has = jnp.where(column == 0, first, jnp.where(column == 1, 1.0 - first, 0.0))
    if keys:
        allowed = jnp.where(place_ < SLOT, has, 0.0)
        return jnp.where(column < 2, (allowed - 1.0) * BIG, 0.0).astype(BF16)
    return has.astype(BF16)


def attend_kernel(
    split, x, wa, vv, e, xp, n1, m, att, wo, lt, xs, lacc, qmask, kmask, qb
):
    spread, keep, choose = slab_maps()
    wide = dot(vv[...], spread.astype(BF16))
    e[...] = exact_dot(choose, wide * keep)
    xs[0:1056] = x[0:1056].astype(F32)
    xs[1056:ROWS] = jnp.zeros((ROWS - 1056, D), F32)
    xs[1056:1058] = x[1056:1058].astype(F32)
    gain, offset = e[0:1], e[1:2]
    for slot in range(2):
        qmask[slot] = mask_columns(split[slot], False)
        kmask[slot] = mask_columns(split[slot], True)
        for part in range(2):
            source = SLOT * slot + 272 * part
            target = slice(PAD * slot + 272 * part, PAD * slot + 272 * part + 272)
            value = xs[source : source + 272]
            xp[target] = value.astype(BF16)
            shifted, rate = norm_parts(value)
            n1[target] = (shifted * rate * gain + offset).astype(BF16)
    zero = jnp.zeros((1, GROUP), F32)
    for group in range(4):
        lanes = slice(GROUP * group, GROUP * group + GROUP)
        qb[group] = jnp.concatenate((e[2:3, lanes], zero, e[3:4, lanes]), axis=1)

    def one_group(group, carry):
        weights = wa[group]
        wo[group] = weights[:, 3 * GROUP :]
        for part in range(4):
            rows = slice(272 * part, 272 * part + 272)
            mixed = dot(n1[rows], weights[:, : 3 * GROUP]) + qb[group]
            m[group, rows] = mixed.astype(BF16)
        for slot in range(2):
            rows = slice(PAD * slot, PAD * slot + PAD)
            for head in range(3):
                cols = slice(HEAD_DIM * head, HEAD_DIM * head + HEAD_DIM)
                both = m[group, rows]
                q = both[:, HEAD_DIM * head : HEAD_DIM * (head + 1)] * 0.125
                k = both[:, GROUP + HEAD_DIM * head : GROUP + HEAD_DIM * (head + 1)]
                v = both[:, 2 * GROUP + HEAD_DIM * head : 2 * GROUP + HEAD_DIM * (head + 1)]
                qx = jnp.concatenate((q.astype(BF16), qmask[slot]), axis=1)
                kx = jnp.concatenate((k, kmask[slot]), axis=1)
                scores = dot(qx, kx, NT)
                top = jnp.max(scores, axis=1, keepdims=True)
                terms = jnp.exp(scores - top)
                total = jnp.sum(terms, axis=1, keepdims=True)
                mixed = dot(terms.astype(BF16), v) / total
                att[group, rows, cols] = mixed.astype(BF16)
                lane = lax.broadcasted_iota(jnp.int32, (PAD, 128), 1)
                lacc[slot] = jnp.where(
                    lane == 3 * group + head, top + jnp.log(total), lacc[slot]
                )
        return carry

    lacc[...] = jnp.zeros_like(lacc)
    lax.fori_loop(0, 4, one_group, 0)
    row = lax.broadcasted_iota(jnp.int32, (16, 128), 0)
    eye = (row == lax.broadcasted_iota(jnp.int32, (16, 128), 1)).astype(F32)
    for slot in range(2):
        lt[slot] = exact_dot(eye, lacc[slot], NT)


def attend(split_at, inputs, wa, vv):
    vm = pl.BlockSpec(memory_space=pltpu.VMEM)
    return pl.pallas_call(
        attend_kernel,
        out_shape=(
            jax.ShapeDtypeStruct((16, D), F32),
            jax.ShapeDtypeStruct((ROWS, D), BF16),
            jax.ShapeDtypeStruct((ROWS, D), BF16),
            jax.ShapeDtypeStruct((4, ROWS, 3 * GROUP), BF16),
            jax.ShapeDtypeStruct((4, ROWS, GROUP), BF16),
            jax.ShapeDtypeStruct((4, D, GROUP), BF16),
            jax.ShapeDtypeStruct((2, 16, PAD), F32),
        ),
        in_specs=[pl.BlockSpec(memory_space=pltpu.SMEM), vm, vm, vm],
        out_specs=[vm] * 7,
        scratch_shapes=[
            pltpu.VMEM((ROWS, D), F32),
            pltpu.VMEM((2, PAD, 128), F32),
            pltpu.VMEM((2, PAD, HEAD_DIM), BF16),
            pltpu.VMEM((2, PAD, HEAD_DIM), BF16),
            pltpu.VMEM((4, 1, 3 * GROUP), F32),
        ],
        compiler_params=pltpu.CompilerParams(vmem_limit_bytes=56 * MIB),
    )(split_at, inputs, wa, vv)


def gelu_parts(hidden):
    size = jnp.abs(hidden)
    t = 1.0 / (1.0 + 0.3 * size)
    bell = jnp.exp(hidden * hidden * -0.5)
    poly = jnp.full_like(t, TAIL[-1])
    for factor in TAIL[-2::-1]:
        poly = poly * t + factor
    tail = poly * t * bell
    phi = jnp.where(hidden < 0, tail, 1.0 - tail)
    return hidden * phi, phi + hidden * bell * (1.0 / math.sqrt(2 * math.pi))


def feed_kernel(
    e, xp, dy, att, wo, wb, wc,
    out, gm, gatt, gwo, gb, gc, gvec,
    middle, acc, back, n2, n2t, dyp, dyt, act, gh, gbr,
):
    step = pl.program_id(0)

    @pl.when(step == 0)
    def _():
        acc[0:1056] = dy[0:1056].astype(F32)
        acc[1056:ROWS] = jnp.zeros((ROWS - 1056, D), F32)
        acc[1056:1058] = dy[1056:1058].astype(F32)
        line = lax.broadcasted_iota(jnp.int32, (272, D), 0)
        total = jnp.zeros((1, D), F32)
        for slot in range(2):
            for part in range(2):
                source = SLOT * slot + 272 * part
                target = slice(PAD * slot + 272 * part, PAD * slot + 272 * part + 272)
                value = acc[source : source + 272]
                if part == 1:
                    value = jnp.where(line < SLOT - 272, value, 0.0)
                total = total + jnp.sum(value, axis=0, keepdims=True)
                dyp[target] = value.astype(BF16)
        gvec[...] = jnp.zeros_like(gvec)
        gvec[7:8] = total
        dyt[...] = dyp[...].T
        for part in range(4):
            rows = slice(272 * part, 272 * part + 272)
            value = xp[rows].astype(F32) + e[4:5]
            for group in range(4):
                value = value + dot(att[group, rows], wo[group], NT)
            middle[rows] = value
            shifted, rate = norm_parts(value)
            n2[rows] = (shifted * rate * e[5:6] + e[6:7]).astype(BF16)
            acc[rows] = value + e[7:8]
            back[rows] = jnp.zeros((272, D), F32)
        n2t[...] = n2[...].T

    offset = e[pl.ds(8 + step, 1)]

    def chunk(part, total):
        rows = pl.ds(sixteen(part * 272), 272)
        hidden = dot(n2[rows], wb[0]) + offset
        forward, slope = gelu_parts(hidden)
        low = forward.astype(BF16)
        act[rows] = low
        grad = (dot(dyp[rows], wc[0]) * slope).astype(BF16)
        gh[rows] = grad
        acc[rows] = acc[rows] + dot(low, wc[0], NT)
        back[rows] = back[rows] + dot(grad, wb[0], NT)
        return total + jnp.sum(grad.astype(F32), axis=0, keepdims=True)

    total = lax.fori_loop(0, 4, chunk, jnp.zeros((1, D), F32))
    gvec[pl.ds(8 + step, 1)] = total
    gc[0] = dot(dyt[...], act[...]).astype(BF16)
    gb[0] = dot(n2t[...], gh[...]).astype(BF16)

    @pl.when(step == 3)
    def _():
        sums = [jnp.zeros((1, D), F32)] * 3
        for part in range(4):
            rows = slice(272 * part, 272 * part + 272)
            shifted, rate = norm_parts(middle[rows])
            hat = shifted * rate
            grad = back[rows]
            inner = grad * e[5:6]
            mean = jnp.mean(inner, axis=-1, keepdims=True)
            along = jnp.mean(inner * hat, axis=-1, keepdims=True)
            total = dyp[rows].astype(F32) + rate * (inner - mean - hat * along)
            gm[rows] = total
            branch = total.astype(BF16)
            gbr[rows] = branch
            for i, value in enumerate((grad * hat, grad, branch.astype(F32))):
                sums[i] = sums[i] + jnp.sum(value, axis=0, keepdims=True)
            for group in range(4):
                gatt[group, rows] = dot(branch, wo[group]).astype(BF16)
        gvec[5:6] = sums[0]
        gvec[6:7] = sums[1]
        gvec[4:5] = sums[2]
        turned = gbr[...].T
        for group in range(4):
            gwo[group] = dot(turned, att[group]).astype(BF16)
        line = lax.broadcasted_iota(jnp.int32, (16, D), 0)
        out[0:528] = acc[0:528].astype(BF16)
        out[528:544] = jnp.where(line == 0, acc[528:544], acc[543:559]).astype(BF16)
        out[544:1056] = acc[559:1071].astype(BF16)
        out[1056:1058] = acc[1071:1073].astype(BF16)


def feed(e, xp, cotangent, att, wo, wb, wc):
    def whole(*shape):
        return pl.BlockSpec(shape, lambda i: (0,) * len(shape), pipeline_mode=pl.Buffered(1))

    block = pl.BlockSpec((1, D, D), lambda i: (i, 0, 0))
    local = cotangent.shape[0]
    return pl.pallas_call(
        feed_kernel,
        grid=(4,),
        out_shape=(
            jax.ShapeDtypeStruct((local, D), BF16),
            jax.ShapeDtypeStruct((ROWS, D), F32),
            jax.ShapeDtypeStruct((4, ROWS, GROUP), BF16),
            jax.ShapeDtypeStruct((4, D, GROUP), BF16),
            jax.ShapeDtypeStruct((4, D, D), BF16),
            jax.ShapeDtypeStruct((4, D, D), BF16),
            jax.ShapeDtypeStruct((16, D), F32),
        ),
        in_specs=[
            whole(16, D), whole(ROWS, D), whole(local, D), whole(4, ROWS, GROUP),
            whole(4, D, GROUP), block, block,
        ],
        out_specs=[
            whole(local, D), whole(ROWS, D), whole(4, ROWS, GROUP), whole(4, D, GROUP),
            block, block, whole(16, D),
        ],
        scratch_shapes=[
            pltpu.VMEM((ROWS, D), F32),
            pltpu.VMEM((ROWS, D), F32),
            pltpu.VMEM((ROWS, D), F32),
            pltpu.VMEM((ROWS, D), BF16),
            pltpu.VMEM((D, ROWS), BF16),
            pltpu.VMEM((ROWS, D), BF16),
            pltpu.VMEM((D, ROWS), BF16),
            pltpu.VMEM((ROWS, D), BF16),
            pltpu.VMEM((ROWS, D), BF16),
            pltpu.VMEM((ROWS, D), BF16),
        ],
        compiler_params=pltpu.CompilerParams(
            vmem_limit_bytes=60 * MIB, dimension_semantics=("arbitrary",)
        ),
    )(e, xp, cotangent, att, wo, wb, wc)


def unattend_kernel(
    split, e, xp, n1, m, gatt, lt, wa, gm, gwo, gvec,
    gin, ga, gv, n1t, gmix, back, sums, qmask, kmask,
):
    for slot in range(2):
        qmask[slot] = mask_columns(split[slot], False)
        kmask[slot] = mask_columns(split[slot], True)
    n1t[...] = n1[...].T
    back[...] = jnp.zeros_like(back)

    def one_group(group, carry):
        for slot in range(2):
            rows = slice(PAD * slot, PAD * slot + PAD)
            for head in range(3):
                both = m[group, rows]
                q = (both[:, HEAD_DIM * head : HEAD_DIM * (head + 1)] * 0.125).astype(BF16)
                k = both[:, GROUP + HEAD_DIM * head : GROUP + HEAD_DIM * (head + 1)]
                v = both[:, 2 * GROUP + HEAD_DIM * head : 2 * GROUP + HEAD_DIM * (head + 1)]
                go = gatt[group, rows][:, HEAD_DIM * head : HEAD_DIM * (head + 1)]
                qx = jnp.concatenate((q, qmask[slot]), axis=1)
                kx = jnp.concatenate((k, kmask[slot]), axis=1)
                scores = dot(kx, qx, NT)
                probs = jnp.exp(scores - lt[slot, pl.ds(3 * group + head, 1)])
                gprobs = dot(v, go, NT)
                both_ = probs * gprobs
                delta = jnp.sum(both_, axis=0, keepdims=True)
                gs = (both_ - probs * delta).astype(BF16)
                gq = dot(gs, k, TN) * 0.125
                gk = dot(gs, q)
                gval = dot(probs.astype(BF16), go)
                for i, value in enumerate((gq, gk, gval)):
                    at = GROUP * i + HEAD_DIM * head
                    gmix[rows, at : at + HEAD_DIM] = value.astype(BF16)
        weights = wa[group][:, : 3 * GROUP]
        total = jnp.zeros((1, 3 * GROUP), F32)
        for part in range(4):
            rows = slice(272 * part, 272 * part + 272)
            total = total + jnp.sum(gmix[rows].astype(F32), axis=0, keepdims=True)
            back[rows] = back[rows] + dot(gmix[rows], weights, NT)
        sums[group] = total
        ga[group, :, 0 : 3 * GROUP] = dot(n1t[...], gmix[...]).astype(BF16)
        ga[group, :, 3 * GROUP :] = gwo[group]
        return carry

    lax.fori_loop(0, 4, one_group, 0)
    tot_gain, tot_bias = jnp.zeros((1, D), F32), jnp.zeros((1, D), F32)
    for part in range(4):
        rows = slice(272 * part, 272 * part + 272)
        shifted, rate = norm_parts(xp[rows].astype(F32))
        hat = shifted * rate
        grad = back[rows]
        inner = grad * e[0:1]
        mean = jnp.mean(inner, axis=-1, keepdims=True)
        along = jnp.mean(inner * hat, axis=-1, keepdims=True)
        tot_gain = tot_gain + jnp.sum(grad * hat, axis=0, keepdims=True)
        tot_bias = tot_bias + jnp.sum(grad, axis=0, keepdims=True)
        back[rows] = gm[rows] + rate * (inner - mean - hat * along)
    line = lax.broadcasted_iota(jnp.int32, (16, D), 0)
    gin[0:528] = back[0:528].astype(BF16)
    gin[528:544] = jnp.where(line == 0, back[528:544], back[543:559]).astype(BF16)
    gin[544:1056] = back[559:1071].astype(BF16)
    gin[1056:1058] = back[1071:1073].astype(BF16)
    q_row = jnp.concatenate([sums[i][:, :GROUP] for i in range(4)], axis=1)
    v_row = jnp.concatenate([sums[i][:, 2 * GROUP :] for i in range(4)], axis=1)
    rows = jnp.where(line == 0, tot_gain, jnp.where(line == 1, tot_bias, gvec[...]))
    rows = jnp.where(line == 2, q_row, jnp.where(line == 3, v_row, rows))
    spread, keep, choose = slab_maps()
    wide = exact_dot(choose, rows, TN) * keep
    gv[...] = exact_dot(wide, spread, NT)


def unattend(split_at, e, xp, n1, m, gatt, lt, wa, gm, gwo, gvec, local):
    vm = pl.BlockSpec(memory_space=pltpu.VMEM)
    return pl.pallas_call(
        unattend_kernel,
        out_shape=(
            jax.ShapeDtypeStruct((local, D), BF16),
            jax.ShapeDtypeStruct((4, D, D), BF16),
            jax.ShapeDtypeStruct((256, 128), F32),
        ),
        in_specs=[pl.BlockSpec(memory_space=pltpu.SMEM)] + [vm] * 10,
        out_specs=[vm] * 3,
        scratch_shapes=[
            pltpu.VMEM((D, ROWS), BF16),
            pltpu.VMEM((ROWS, 3 * GROUP), BF16),
            pltpu.VMEM((ROWS, D), F32),
            pltpu.VMEM((4, 1, 3 * GROUP), F32),
            pltpu.VMEM((2, PAD, HEAD_DIM), BF16),
            pltpu.VMEM((2, PAD, HEAD_DIM), BF16),
        ],
        compiler_params=pltpu.CompilerParams(vmem_limit_bytes=60 * MIB),
    )(split_at, e, xp, n1, m, gatt, lt, wa, gm, gwo, gvec)


def on_device(
    inputs, cotangent, split_at, ln1_gain, ln1_bias, w_qkv, q_bias, v_bias, w_out, o_bias,
    ln2_gain, ln2_bias, w_up, up_bias, w_down, down_bias,
):
    pa = jnp.concatenate((w_qkv.reshape(GROUP, 3 * GROUP), w_out.T), axis=1)
    vectors = jnp.stack(
        (ln1_gain, ln1_bias, q_bias, v_bias, o_bias, ln2_gain, ln2_bias, down_bias)
        + tuple(up_bias[48 * i : 48 * i + 48] for i in range(4))
    )
    slab = jnp.pad(vectors, ((0, 4), (0, 80)))
    wa, wb, wc, vv = gather(pa, w_up, w_down.T, slab)
    wa, wb, wc = (w.reshape(4, D, D) for w in (wa, wb, wc))
    e, xp, n1, m, att, wo, lt = attend(split_at, inputs, wa, vv.reshape(256, 128))
    output, gm, gatt, gwo, gb, gc, gvec = feed(e, xp, cotangent, att, wo, wb, wc)
    gin, ga, gv = unattend(
        split_at, e, xp, n1, m, gatt, lt, wa, gm, gwo, gvec, inputs.shape[0]
    )
    ga, gb, gc = (g.reshape(4, 4, GROUP, D) for g in (ga, gb, gc))
    oa, ob, oc, ov = scatter(ga, gb, gc, gv.reshape(4, 4, 16, 128))
    if lax.axis_size("dp") > 2:
        oa, ob, oc, ov = (lax.psum(v, "dp") * 0.5 for v in (oa, ob, oc, ov))
    rows = [ov[i, :48] for i in range(8)]
    return (
        output,
        gin,
        rows[0],
        rows[1],
        oa[:, : 3 * GROUP].reshape(w_qkv.shape),
        rows[2],
        rows[3],
        oa[:, 3 * GROUP :].T,
        rows[4],
        rows[5],
        rows[6],
        ob,
        ov[8:12, :48].reshape(192),
        oc.T,
        rows[7],
    )


def solution(mesh):
    rows = P(("dp", "aa", "ba"), None)
    vec = P(("aa", "ba"))
    grid_qkv, first, second = P("ba", None, "aa"), P("aa", "ba"), P("ba", "aa")
    params = (vec, vec, grid_qkv, vec, vec, first, vec, vec, vec, second, vec, first, vec)
    return jax.shard_map(
        on_device,
        mesh=mesh,
        in_specs=(rows, rows, P(("dp", "aa", "ba"))) + params,
        out_specs=(rows, rows) + params,
        check_vma=False,
    )
```

```python
import functools
import math

import jax
import jax.numpy as jnp
from jax import lax
from jax.experimental import pallas as pl
from jax.experimental.pallas import tpu as pltpu
from jax.sharding import PartitionSpec as P

D = 768
HEADS = 12
HEAD_DIM = 64
SLOT = 529
PAD = 544
ROWS = 2 * PAD
GROUP = 192
BIG = 1e30
MESH = pl.DeviceIdType.MESH
F32 = jnp.float32
BF16 = jnp.bfloat16
MIB = 1 << 20

NT = (((1,), (1,)), ((), ()))
NN = (((1,), (0,)), ((), ()))
TN = (((0,), (0,)), ((), ()))

TAIL = (
    0.11962926248861097,
    0.12075451364069298,
    0.09991001218129214,
    0.12857310923328652,
    -0.0537053561953165,
    0.20637712218096793,
    -0.15721681637037743,
    0.03567808025645831,
)


def dot(left, right, dims=NN):
    return lax.dot_general(left, right, dims, preferred_element_type=F32)


def exact_dot(left, right, dims=NN):
    return lax.dot_general(
        left, right, dims, preferred_element_type=F32, precision=lax.Precision.HIGHEST
    )


def place():
    dp, aa, ba = lax.axis_index("dp"), lax.axis_index("aa"), lax.axis_index("ba")
    half, core = lax.rem(dp, 2), lax.rem(aa, 2)
    peers = {
        "x": (dp + 1 - 2 * half, aa, ba),
        "y": (dp, lax.rem(aa + 2, 4), ba),
        "c": (dp, aa + 1 - 2 * core, ba),
        "z1": (dp, aa, lax.rem(ba + 1, 4)),
        "z2": (dp, aa, lax.rem(ba + 2, 4)),
        "z3": (dp, aa, lax.rem(ba + 3, 4)),
    }
    return dp, aa, ba, half, core, peers


def greet(peers):
    barrier = pltpu.get_barrier_semaphore()
    for peer in peers.values():
        pl.semaphore_signal(barrier, inc=1, device_id=peer, device_id_type=MESH)
    pl.semaphore_wait(barrier, len(peers))


class Sends:
    def __init__(self, send_sem, recv_sem, peers):
        self.send_sem, self.recv_sem, self.peers = send_sem, recv_sem, peers
        self.made = {}

    def start(self, name, src, dst, peer):
        at = len(self.made)
        copy = pltpu.make_async_remote_copy(
            src_ref=src,
            dst_ref=dst,
            send_sem=self.send_sem.at[at],
            recv_sem=self.recv_sem.at[at],
            device_id=self.peers[peer],
            device_id_type=MESH,
        )
        copy.start()
        self.made[name] = copy

    def arrived(self, *names):
        for name in names:
            self.made[name].wait_recv()

    def finish(self):
        for copy in self.made.values():
            copy.wait_send()


def sixteen(value):
    return pl.multiple_of(value, 16)


class Gather:
    def __init__(self, name, sends, where, part, whole, row):
        self.name, self.sends, self.part, self.whole = name, sends, part, whole
        self.aa, self.ba, self.half = where
        self.ay = lax.rem(self.aa + 2, 4)
        self.other = [(j, lax.rem(self.ba + j, 4)) for j in (1, 2, 3)]
        self.big = pl.ds(sixteen(row + 32 * self.half), 32)
        self.big_not = pl.ds(sixteen(row + 32 - 32 * self.half), 32)
        self.small = pl.ds(sixteen(row + 64 + 16 * self.half), 16)
        self.rest = pl.ds(row + 64, 32)

    def send(self, key, src, dst, peer):
        self.sends.start((self.name,) + key, src, dst, peer)

    def move(self, key, at, peer):
        self.send(key, self.whole.at[at], self.whole.at[at], peer)

    def got(self, *keys):
        self.sends.arrived(*[(self.name,) + key for key in keys])

    def first(self):
        w, aa, ba = self.whole, self.aa, self.ba
        for j in (1, 2, 3):
            self.send(("z", j), self.part.at[self.big], w.at[aa, ba, self.big], f"z{j}")
        self.send(("y",), self.part.at[self.small], w.at[aa, ba, self.small], "y")
        for j in (1, 2, 3):
            self.send(("zs", j), self.part.at[self.small], w.at[aa, ba, self.small], f"z{j}")

    def second(self):
        self.got(("z", 1), ("z", 2), ("z", 3))
        for j, z in self.other:
            self.move(("x", j), (self.aa, z, self.big), "x")
        self.move(("yb",), (self.aa, slice(None), self.big), "y")
        self.got(("y",))
        for j in (1, 2, 3):
            self.move(("zy", j), (self.ay, self.ba, self.small), f"z{j}")
        self.got(("zs", 1), ("zs", 2), ("zs", 3))
        for j, z in self.other:
            self.move(("xs", j), (self.aa, z, self.small), "x")
        self.move(("c0",), (self.aa, slice(None), self.big), "c")

    def third(self):
        every = slice(None)
        self.got(("x", 1), ("x", 2), ("x", 3))
        self.move(("yn",), (self.aa, every, self.big_not), "y")
        self.got(("zy", 1), ("zy", 2), ("zy", 3))
        self.move(("xy",), (self.ay, every, self.small), "x")
        self.got(("yb",))
        self.move(("c1",), (self.aa, every, self.big_not), "c")
        self.move(("c2",), (self.ay, every, self.big), "c")

    def fourth(self):
        every = slice(None)
        self.got(("xs", 1), ("xs", 2), ("xs", 3))
        self.move(("c3",), (self.aa, every, self.rest), "c")
        self.got(("yn",))
        self.move(("c4",), (self.ay, every, self.big_not), "c")
        self.got(("xy",))
        self.move(("c5",), (self.ay, every, self.rest), "c")

    def last(self):
        self.got(*[(f"c{i}",) for i in range(6)])


class Scatter:
    def __init__(self, name, sends, where, given, held, out, row, bufs):
        self.name, self.sends, self.given, self.held, self.out, self.row = (
            name, sends, given, held, out, row,
        )
        self.aa, self.ba, self.half = where
        self.yy = self.aa // 2
        self.yn = 1 - self.yy
        self.other = [(j, lax.rem(self.ba + j, 4)) for j in (1, 2, 3)]
        self.rc, self.ry, self.rx, self.rz, self.rf, self.sx, self.sz, self.sy, self.sf, self.f0, self.f1 = bufs
        self.mine = pl.ds(sixteen(row + 32 * self.half), 32)
        self.theirs = pl.ds(sixteen(row + 32 - 32 * self.half), 32)
        self.smine = pl.ds(sixteen(row + 64 + 16 * self.half), 16)
        self.stheirs = pl.ds(sixteen(row + 80 - 16 * self.half), 16)

    def send(self, key, src, dst, peer):
        self.sends.start((self.name,) + key, src, dst, peer)

    def got(self, *keys):
        self.sends.arrived(*[(self.name,) + key for key in keys])

    @staticmethod
    def scratch():
        return [
            pltpu.VMEM((2, 4, 96, D), BF16),
            pltpu.VMEM((4, 64, D), BF16),
            pltpu.VMEM((4, 32, D), BF16),
            pltpu.VMEM((3, 32, D), BF16),
            pltpu.VMEM((32, D), BF16),
            pltpu.VMEM((2, 4, 16, D), BF16),
            pltpu.VMEM((3, 2, 16, D), BF16),
            pltpu.VMEM((16, D), BF16),
            pltpu.VMEM((16, D), BF16),
            pltpu.VMEM((32, D), BF16),
            pltpu.VMEM((16, D), BF16),
        ]

    def cores(self):
        for y in (0, 1):
            self.send(("c", y), self.given(y).at[:, pl.ds(self.row, 96)], self.rc.at[y], "c")

    def first(self):
        self.got(("c", 0), ("c", 1))
        rows = pl.ds(self.row, 96)
        for y in (0, 1):
            h, rc = self.held(y), self.rc.at[y]

            @pl.loop(0, 4)
            def _(z):
                h[z, rows] = (h[z, rows].astype(F32) + rc[z].astype(F32)).astype(BF16)

        self.send(("y",), self.held(self.yn).at[:, pl.ds(self.row, 64)], self.ry, "y")
        for y in (0, 1):
            self.send(("x", y), self.held(y).at[:, self.stheirs], self.sx.at[y], "x")

    def second(self):
        self.got(("y",))
        h, rows = self.held(self.yy), pl.ds(self.row, 64)

        @pl.loop(0, 4)
        def _(z):
            h[z, rows] = (h[z, rows].astype(F32) + self.ry[z].astype(F32)).astype(BF16)

        self.send(("x2",), h.at[:, self.theirs], self.rx, "x")
        self.got(("x", 0), ("x", 1))
        rows = self.smine
        for y in (0, 1):
            g = self.held(y)
            for z in range(4):
                g[z, rows] = (g[z, rows].astype(F32) + self.sx[y, z].astype(F32)).astype(BF16)
            for j, z in self.other:
                self.send(("zs", j, y), g.at[z, rows], self.sz.at[j - 1, y], f"z{j}")

    def third(self):
        self.got(("x2",))
        h, rows = self.held(self.yy), self.mine

        @pl.loop(0, 4)
        def _(z):
            h[z, rows] = (h[z, rows].astype(F32) + self.rx[z].astype(F32)).astype(BF16)

        for j, z in self.other:
            self.send(("z", j), h.at[z, rows], self.rz.at[j - 1], f"z{j}")
        rows = self.smine
        for y in (0, 1):
            self.got(*[("zs", j, y) for j in (1, 2, 3)])
            g = self.held(y)
            total = g[self.ba, rows].astype(F32)
            for j in range(3):
                total = total + self.sz[j, y].astype(F32)
            g[self.ba, rows] = total.astype(BF16)
        self.send(("ys",), self.held(self.yn).at[self.ba, rows], self.sy, "y")

    def fourth(self):
        self.got(("z", 1), ("z", 2), ("z", 3))
        h = self.held(self.yy)
        total = h[self.ba, self.mine].astype(F32)
        for j in range(3):
            total = total + self.rz[j].astype(F32)
        self.f0[...] = total.astype(BF16)
        self.send(("f0",), self.f0, self.rf, "x")
        self.got(("ys",))
        self.f1[...] = (h[self.ba, self.smine].astype(F32) + self.sy[...].astype(F32)).astype(BF16)
        self.send(("f1",), self.f1, self.sf, "x")

    def last(self):
        self.out[self.mine] = self.f0[...].astype(F32)
        self.out[self.smine] = self.f1[...].astype(F32)
        self.got(("f0",), ("f1",))
        self.out[self.theirs] = self.rf[...].astype(F32)
        self.out[self.stheirs] = self.sf[...].astype(F32)


def slab_maps():
    lane = lax.broadcasted_iota(jnp.int32, (128, D), 0)
    column = lax.broadcasted_iota(jnp.int32, (128, D), 1)
    spread = (lax.rem(column, 48) == lane).astype(F32)
    line = lax.broadcasted_iota(jnp.int32, (256, D), 0)
    block = lax.broadcasted_iota(jnp.int32, (256, D), 1) // 48
    device, kind = line // 16, lax.rem(line, 16)
    wanted = jnp.where(kind < 8, device, 4 * lax.rem(device, 4) + kind - 8)
    keep = jnp.where((wanted == block) & (kind < 12), 1.0, 0.0).astype(F32)
    line = lax.broadcasted_iota(jnp.int32, (16, 256), 1)
    out = lax.broadcasted_iota(jnp.int32, (16, 256), 0)
    device, kind = line // 16, lax.rem(line, 16)
    choose = (jnp.where(kind < 8, kind, 8 + device // 4) == out).astype(F32)
    return spread, keep, choose


def norm_parts(value):
    centre = jnp.mean(value, axis=-1, keepdims=True)
    shifted = value - centre
    spread = jnp.mean(shifted * shifted, axis=-1, keepdims=True)
    return shifted, lax.rsqrt(spread + 1e-6)


def mask_columns(split, keys):
    place_ = lax.broadcasted_iota(jnp.int32, (PAD, HEAD_DIM), 0)
    column = lax.broadcasted_iota(jnp.int32, (PAD, HEAD_DIM), 1)
    first = jnp.where(place_ < split, 1.0, 0.0)
    has = jnp.where(column == 0, first, jnp.where(column == 1, 1.0 - first, 0.0))
    if keys:
        allowed = jnp.where(place_ < SLOT, has, 0.0)
        return jnp.where(column < 2, (allowed - 1.0) * BIG, 0.0).astype(BF16)
    return has.astype(BF16)


def shift_in(source, wide):
    wide[0:1056] = source[0:1056].astype(F32)
    wide[1056:ROWS] = jnp.zeros((ROWS - 1056, D), F32)
    wide[1056:1058] = source[1056:1058].astype(F32)


def halves():
    for slot in range(2):
        for part in range(2):
            start = PAD * slot + 272 * part
            yield SLOT * slot + 272 * part, slice(start, start + 272), part


def attend_kernel(
    split, pa, pb, pc, slab, x, dy,
    wa_out, wb, wc, e_out, xp_out, n1t_out, dyp_out, dyt_out, m_out, att_out, wo_out, lt_out,
    wa, vv, xs, n1, e, xp, n1t, dyp, dyt, m, att, wo, lt, lacc, qmask, kmask, qb,
    send_sem, recv_sem, own_sem, out_sem,
):
    dp, aa, ba, half, core, peers = place()
    greet(peers)
    sends = Sends(send_sem, recv_sem, peers)
    where = (aa, ba, half)
    own = [
        pltpu.make_async_copy(part, whole.at[aa, ba], own_sem.at[i])
        for i, (part, whole) in enumerate(((pa, wa), (pb, wb), (pc, wc), (slab, vv)))
    ]
    for copy in own:
        copy.start()
    for j in (1, 2, 3):
        sends.start(("v", j), slab, vv.at[aa, ba], f"z{j}")
    a0, a1, b0, b1, c0, c1 = (
        Gather(f"{name}{i}", sends, where, part, whole, 96 * i)
        for name, part, whole in (("a", pa, wa), ("b", pb, wb), ("c", pc, wc))
        for i in (0, 1)
    )
    outs = []

    def put(source, target):
        copy = pltpu.make_async_copy(source, target, out_sem.at[len(outs)])
        copy.start()
        outs.append(copy)

    a0.first()
    a1.first()
    shift_in(dy, xs)
    line = lax.broadcasted_iota(jnp.int32, (272, D), 0)
    total = jnp.zeros((1, D), F32)
    for source, target, part in halves():
        value = xs[source : source + 272]
        if part == 1:
            value = jnp.where(line < SLOT - 272, value, 0.0)
        total = total + jnp.sum(value, axis=0, keepdims=True)
        dyp[target] = value.astype(BF16)
    put(dyp, dyp_out)
    for copy in own:
        copy.wait()
    a0.second()
    sends.arrived(*[("v", j) for j in (1, 2, 3)])
    sends.start(("v", "y"), vv.at[aa], vv.at[aa], "y")
    sends.start(("v", "c"), vv.at[aa], vv.at[aa], "c")
    a1.second()
    shift_in(x, xs)
    for source, target, part in halves():
        xp[target] = xs[source : source + 272].astype(BF16)
    put(xp, xp_out)
    sends.arrived(("v", "y"), ("v", "c"))
    sends.start(("v", "cy"), vv.at[lax.rem(aa + 2, 4)], vv.at[lax.rem(aa + 2, 4)], "c")
    a0.third()
    a1.third()
    b0.first()
    dyt[...] = dyp[...].T
    put(dyt, dyt_out)
    sends.arrived(("v", "cy"))
    spread, keep, choose = slab_maps()
    wide = dot(vv[...].reshape(256, 128), spread.astype(BF16))
    e[...] = exact_dot(choose, wide * keep)
    e[12:13] = total
    put(e, e_out)
    gain, offset = e[0:1], e[1:2]
    for source, target, part in halves():
        shifted, rate = norm_parts(xs[source : source + 272])
        n1[target] = (shifted * rate * gain + offset).astype(BF16)
    a0.fourth()
    a1.fourth()
    b1.first()
    n1t[...] = n1[...].T
    put(n1t, n1t_out)
    for slot in range(2):
        qmask[slot] = mask_columns(split[slot], False)
        kmask[slot] = mask_columns(split[slot], True)
    zero = jnp.zeros((1, GROUP), F32)
    for group in range(4):
        lanes = slice(GROUP * group, GROUP * group + GROUP)
        qb[group] = jnp.concatenate((e[2:3, lanes], zero, e[3:4, lanes]), axis=1)
    lacc[...] = jnp.zeros_like(lacc)
    a0.last()
    a1.last()
    put(wa, wa_out)

    def project(group):
        weights = wa[group].reshape(D, D)
        wo[group] = weights[:, 3 * GROUP :]
        for part in range(4):
            rows = slice(272 * part, 272 * part + 272)
            mixed = dot(n1[rows], weights[:, : 3 * GROUP]) + qb[group]
            m[group, rows] = mixed.astype(BF16)

    def look(group, slot):
        rows = slice(PAD * slot, PAD * slot + PAD)
        for head in range(3):
            cols = slice(HEAD_DIM * head, HEAD_DIM * head + HEAD_DIM)
            both = m[group, rows]
            q = both[:, HEAD_DIM * head : HEAD_DIM * (head + 1)] * 0.125
            k = both[:, GROUP + HEAD_DIM * head : GROUP + HEAD_DIM * (head + 1)]
            v = both[:, 2 * GROUP + HEAD_DIM * head : 2 * GROUP + HEAD_DIM * (head + 1)]
            qx = jnp.concatenate((q.astype(BF16), qmask[slot]), axis=1)
            kx = jnp.concatenate((k, kmask[slot]), axis=1)
            scores = dot(qx, kx, NT)
            top = jnp.max(scores, axis=1, keepdims=True)
            terms = jnp.exp(scores - top)
            total = jnp.sum(terms, axis=1, keepdims=True)
            mixed = dot(terms.astype(BF16), v) / total
            att[group, rows, cols] = mixed.astype(BF16)
            lane = lax.broadcasted_iota(jnp.int32, (PAD, 128), 1)
            lacc[slot] = jnp.where(lane == 3 * group + head, top + jnp.log(total), lacc[slot])

    pumps = (
        (b0.second, c0.first),
        (b1.second, c1.first),
        (b0.third, c0.second),
        (b1.third, c1.second),
        (b0.fourth, c0.third),
        (b1.fourth, c1.third),
        (b0.last, c0.fourth),
        (b1.last, c1.fourth),
    )
    for group in range(4):
        project(group)
        put(m.at[group], m_out.at[group])
        for slot in range(2):
            look(group, slot)
            for step in pumps[2 * group + slot]:
                step()
    put(wo, wo_out)
    put(att, att_out)
    row = lax.broadcasted_iota(jnp.int32, (16, 128), 0)
    eye = (row == lax.broadcasted_iota(jnp.int32, (16, 128), 1)).astype(F32)
    for slot in range(2):
        lt[slot] = exact_dot(eye, lacc[slot], NT)
    put(lt, lt_out)
    c0.last()
    c1.last()
    sends.finish()
    for copy in outs:
        copy.wait()


def attend(split_at, pa, pb, pc, slab, inputs, cotangent):
    vm = pl.BlockSpec(memory_space=pltpu.VMEM)
    hbm = pl.BlockSpec(memory_space=pl.ANY)
    whole = (4, 4, GROUP, D)
    shapes = [
        (whole, BF16), (whole, BF16), (whole, BF16), ((16, D), F32), ((ROWS, D), BF16),
        ((D, ROWS), BF16), ((ROWS, D), BF16), ((D, ROWS), BF16), ((4, ROWS, 3 * GROUP), BF16),
        ((4, ROWS, GROUP), BF16), ((4, D, GROUP), BF16), ((2, 16, PAD), F32),
    ]
    count = 6 * 26 + 6
    return pl.pallas_call(
        attend_kernel,
        out_shape=tuple(jax.ShapeDtypeStruct(*shape) for shape in shapes),
        in_specs=[pl.BlockSpec(memory_space=pltpu.SMEM)] + [hbm] * 4 + [vm] * 2,
        out_specs=[hbm] * len(shapes),
        scratch_shapes=[
            pltpu.VMEM(whole, BF16),
            pltpu.VMEM((4, 4, 16, 128), BF16),
            pltpu.VMEM((ROWS, D), F32),
            pltpu.VMEM((ROWS, D), BF16),
        ]
        + [pltpu.VMEM(*shape) for shape in shapes[3:]]
        + [
            pltpu.VMEM((2, PAD, 128), F32),
            pltpu.VMEM((2, PAD, HEAD_DIM), BF16),
            pltpu.VMEM((2, PAD, HEAD_DIM), BF16),
            pltpu.VMEM((4, 1, 3 * GROUP), F32),
            pltpu.SemaphoreType.DMA((count,)),
            pltpu.SemaphoreType.DMA((count,)),
            pltpu.SemaphoreType.DMA((4,)),
            pltpu.SemaphoreType.DMA((16,)),
        ],
        compiler_params=pltpu.CompilerParams(
            collective_id=0, has_side_effects=True, vmem_limit_bytes=58 * MIB
        ),
    )(split_at, pa, pb, pc, slab, inputs, cotangent)


def gelu_parts(hidden):
    size = jnp.abs(hidden)
    t = 1.0 / (1.0 + 0.3 * size)
    bell = jnp.exp(hidden * hidden * -0.5)
    poly = jnp.full_like(t, TAIL[-1])
    for factor in TAIL[-2::-1]:
        poly = poly * t + factor
    tail = poly * t * bell
    phi = jnp.where(hidden < 0, tail, 1.0 - tail)
    return hidden * phi, phi + hidden * bell * (1.0 / math.sqrt(2 * math.pi))


def feed_kernel(
    e, xp, dyp, dyt, att, wo, wb, wc,
    out, gm, gatt, gwo, gb, gc, gvec,
    middle, acc, back, n2, n2t, act, gh, gbr,
):
    step = pl.program_id(0)

    @pl.when(step == 0)
    def _():
        gvec[...] = jnp.zeros_like(gvec)
        gvec[7:8] = e[12:13]
        for part in range(4):
            rows = slice(272 * part, 272 * part + 272)
            value = xp[rows].astype(F32) + e[4:5]
            for group in range(4):
                value = value + dot(att[group, rows], wo[group], NT)
            middle[rows] = value
            shifted, rate = norm_parts(value)
            n2[rows] = (shifted * rate * e[5:6] + e[6:7]).astype(BF16)
            acc[rows] = value + e[7:8]
            back[rows] = jnp.zeros((272, D), F32)
        n2t[...] = n2[...].T

    offset = e[pl.ds(8 + step, 1)]

    def chunk(part, total):
        rows = pl.ds(sixteen(part * 272), 272)
        hidden = dot(n2[rows], wb[0]) + offset
        forward, slope = gelu_parts(hidden)
        low = forward.astype(BF16)
        act[rows] = low
        grad = (dot(dyp[rows], wc[0]) * slope).astype(BF16)
        gh[rows] = grad
        acc[rows] = acc[rows] + dot(low, wc[0], NT)
        back[rows] = back[rows] + dot(grad, wb[0], NT)
        return total + jnp.sum(grad.astype(F32), axis=0, keepdims=True)

    total = lax.fori_loop(0, 4, chunk, jnp.zeros((1, D), F32))
    gvec[pl.ds(8 + step, 1)] = total
    gc[0] = dot(dyt[...], act[...]).astype(BF16)
    gb[0] = dot(n2t[...], gh[...]).astype(BF16)

    @pl.when(step == 3)
    def _():
        sums = [jnp.zeros((1, D), F32)] * 3
        for part in range(4):
            rows = slice(272 * part, 272 * part + 272)
            shifted, rate = norm_parts(middle[rows])
            hat = shifted * rate
            grad = back[rows]
            inner = grad * e[5:6]
            mean = jnp.mean(inner, axis=-1, keepdims=True)
            along = jnp.mean(inner * hat, axis=-1, keepdims=True)
            total = dyp[rows].astype(F32) + rate * (inner - mean - hat * along)
            gm[rows] = total
            branch = total.astype(BF16)
            gbr[rows] = branch
            for i, value in enumerate((grad * hat, grad, branch.astype(F32))):
                sums[i] = sums[i] + jnp.sum(value, axis=0, keepdims=True)
            for group in range(4):
                gatt[group, rows] = dot(branch, wo[group]).astype(BF16)
        gvec[5:6] = sums[0]
        gvec[6:7] = sums[1]
        gvec[4:5] = sums[2]
        turned = gbr[...].T
        for group in range(4):
            gwo[group] = dot(turned, att[group]).astype(BF16)
        line = lax.broadcasted_iota(jnp.int32, (16, D), 0)
        out[0:528] = acc[0:528].astype(BF16)
        out[528:544] = jnp.where(line == 0, acc[528:544], acc[543:559]).astype(BF16)
        out[544:1056] = acc[559:1071].astype(BF16)
        out[1056:1058] = acc[1071:1073].astype(BF16)


def feed(e, xp, dyp, dyt, att, wo, wb, wc, local):
    def whole(*shape):
        return pl.BlockSpec(shape, lambda i: (0,) * len(shape), pipeline_mode=pl.Buffered(1))

    block = pl.BlockSpec((1, D, D), lambda i: (i, 0, 0))
    return pl.pallas_call(
        feed_kernel,
        grid=(4,),
        out_shape=(
            jax.ShapeDtypeStruct((local, D), BF16),
            jax.ShapeDtypeStruct((ROWS, D), F32),
            jax.ShapeDtypeStruct((4, ROWS, GROUP), BF16),
            jax.ShapeDtypeStruct((4, D, GROUP), BF16),
            jax.ShapeDtypeStruct((4, D, D), BF16),
            jax.ShapeDtypeStruct((4, D, D), BF16),
            jax.ShapeDtypeStruct((16, D), F32),
        ),
        in_specs=[
            whole(16, D), whole(ROWS, D), whole(ROWS, D), whole(D, ROWS), whole(4, ROWS, GROUP),
            whole(4, D, GROUP), block, block,
        ],
        out_specs=[
            whole(local, D), whole(ROWS, D), whole(4, ROWS, GROUP), whole(4, D, GROUP),
            block, block, whole(16, D),
        ],
        scratch_shapes=[
            pltpu.VMEM((ROWS, D), F32),
            pltpu.VMEM((ROWS, D), F32),
            pltpu.VMEM((ROWS, D), F32),
            pltpu.VMEM((ROWS, D), BF16),
            pltpu.VMEM((D, ROWS), BF16),
            pltpu.VMEM((ROWS, D), BF16),
            pltpu.VMEM((ROWS, D), BF16),
            pltpu.VMEM((ROWS, D), BF16),
        ],
        compiler_params=pltpu.CompilerParams(
            vmem_limit_bytes=60 * MIB, dimension_semantics=("arbitrary",)
        ),
    )(e, xp, dyp, dyt, att, wo, wb, wc)


def unattend_kernel(
    split, e, lt, gvec, xp_in, n1t_in, m_in, gatt_in, wa_in, gm_in, gwo_in, gb, gc,
    gin, oa, ob, oc, ov,
    xp, n1t, m, gatt, ga, gm, gwo, hb, hc, gmix, back, sums, gv, qmask, kmask,
    vh, vc, vy, vz, vx, *more,
):
    bufs, (send_sem, recv_sem, own_sem, in_sem) = more[:66], more[66:]
    dp, aa, ba, half, core, peers = place()
    loads = {}
    for name, source, target in (
        ("n1t", n1t_in, n1t), ("m", m_in, m), ("gatt", gatt_in, gatt), ("wa", wa_in, ga),
        ("gwo", gwo_in, gwo), ("xp", xp_in, xp), ("gm", gm_in, gm),
    ):
        loads[name] = pltpu.make_async_copy(source, target, in_sem.at[len(loads)])
        loads[name].start()
    own = []
    for g, h in ((gb, hb), (gc, hc)):
        for y in (0, 1):
            own.append(pltpu.make_async_copy(g.at[2 * y + core], h.at[y], own_sem.at[len(own)]))
            own[-1].start()
    greet(peers)
    sends = Sends(send_sem, recv_sem, peers)
    where = (aa, ba, half)
    made = []
    for n, given, held, out in (
        ("a", ga, None, oa), ("b", gb, hb, ob), ("c", gc, hc, oc),
    ):
        for i in (0, 1):
            at = 11 * len(made)
            made.append(
                Scatter(
                    f"{n}{i}", sends, where,
                    lambda y, given=given: given.at[2 * y + 1 - core],
                    (lambda y: ga.at[2 * y + core]) if held is None else (lambda y, held=held: held.at[y]),
                    out, 96 * i, bufs[at : at + 11],
                )
            )
    a0, a1, b0, b1, c0, c1 = made
    for batch in (b0, b1, c0, c1):
        batch.cores()
    for slot in range(2):
        qmask[slot] = mask_columns(split[slot], False)
        kmask[slot] = mask_columns(split[slot], True)
    back[...] = jnp.zeros_like(back)
    for name in ("m", "gatt", "n1t", "wa", "gwo"):
        loads[name].wait()

    def look(group, slot):
        rows = slice(PAD * slot, PAD * slot + PAD)
        for head in range(3):
            both = m[group, rows]
            q = (both[:, HEAD_DIM * head : HEAD_DIM * (head + 1)] * 0.125).astype(BF16)
            k = both[:, GROUP + HEAD_DIM * head : GROUP + HEAD_DIM * (head + 1)]
            v = both[:, 2 * GROUP + HEAD_DIM * head : 2 * GROUP + HEAD_DIM * (head + 1)]
            go = gatt[group, rows][:, HEAD_DIM * head : HEAD_DIM * (head + 1)]
            qx = jnp.concatenate((q, qmask[slot]), axis=1)
            kx = jnp.concatenate((k, kmask[slot]), axis=1)
            scores = dot(kx, qx, NT)
            probs = jnp.exp(scores - lt[slot, pl.ds(3 * group + head, 1)])
            gprobs = dot(v, go, NT)
            both_ = probs * gprobs
            delta = jnp.sum(both_, axis=0, keepdims=True)
            gs = (both_ - probs * delta).astype(BF16)
            gq = dot(gs, k, TN) * 0.125
            gk = dot(gs, q)
            gval = dot(probs.astype(BF16), go)
            for i, value in enumerate((gq, gk, gval)):
                at = GROUP * i + HEAD_DIM * head
                gmix[rows, at : at + HEAD_DIM] = value.astype(BF16)

    def fold(group):
        weights = ga[group].reshape(D, D)[:, : 3 * GROUP]
        total = jnp.zeros((1, 3 * GROUP), F32)
        for part in range(4):
            rows = slice(272 * part, 272 * part + 272)
            total = total + jnp.sum(gmix[rows].astype(F32), axis=0, keepdims=True)
            back[rows] = back[rows] + dot(gmix[rows], weights, NT)
        sums[group] = total
        grad = dot(n1t[...], gmix[...]).astype(BF16)
        ga[group, :, :, 0 : 3 * GROUP] = grad.reshape(4, GROUP, 3 * GROUP)
        ga[group, :, :, 3 * GROUP :] = gwo[group].reshape(4, GROUP, GROUP)

    pumps = (
        (b0.first,),
        (b0.second, b1.first),
        (b0.third, b1.second, c0.first),
        (b0.fourth, b1.third, c0.second, c1.first),
        (b0.last, b1.fourth, c0.third, c1.second),
        (b1.last, c0.fourth, c1.third),
        (c0.last, c1.fourth),
        (c1.last,),
    )
    for copy in own:
        copy.wait()
    for group in range(4):
        for slot in range(2):
            look(group, slot)
            for step in pumps[2 * group + slot]:
                step()
        fold(group)
    a0.cores()
    a1.cores()
    loads["xp"].wait()
    loads["gm"].wait()
    tot_gain, tot_bias = jnp.zeros((1, D), F32), jnp.zeros((1, D), F32)
    for part in range(4):
        rows = slice(272 * part, 272 * part + 272)
        shifted, rate = norm_parts(xp[rows].astype(F32))
        hat = shifted * rate
        grad = back[rows]
        inner = grad * e[0:1]
        mean = jnp.mean(inner, axis=-1, keepdims=True)
        along = jnp.mean(inner * hat, axis=-1, keepdims=True)
        tot_gain = tot_gain + jnp.sum(grad * hat, axis=0, keepdims=True)
        tot_bias = tot_bias + jnp.sum(grad, axis=0, keepdims=True)
        back[rows] = gm[rows] + rate * (inner - mean - hat * along)
        if part == 0:
            a0.first()
            a1.first()
    line = lax.broadcasted_iota(jnp.int32, (16, D), 0)
    q_row = jnp.concatenate([sums[i][:, :GROUP] for i in range(4)], axis=1)
    v_row = jnp.concatenate([sums[i][:, 2 * GROUP :] for i in range(4)], axis=1)
    rows = jnp.where(line == 0, tot_gain, jnp.where(line == 1, tot_bias, gvec[...]))
    rows = jnp.where(line == 2, q_row, jnp.where(line == 3, v_row, rows))
    spread, keep, choose = slab_maps()
    wide = exact_dot(choose, rows, TN) * keep
    gv[...] = exact_dot(wide, spread, NT).reshape(4, 4, 16, 128)
    yy = aa // 2
    for y in (0, 1):
        sends.start(("v", "c", y), gv.at[2 * y + 1 - core], vc.at[y], "c")
    a0.second()
    for y in (0, 1):
        sends.arrived(("v", "c", y))
        vh[y] = gv[2 * y + core] + vc[y]
    sends.start(("v", "y"), vh.at[1 - yy], vy, "y")
    gin[0:528] = back[0:528].astype(BF16)
    gin[528:544] = jnp.where(line == 0, back[528:544], back[543:559]).astype(BF16)
    gin[544:1056] = back[559:1071].astype(BF16)
    gin[1056:1058] = back[1071:1073].astype(BF16)
    a1.second()
    sends.arrived(("v", "y"))
    vh[yy] = vh[yy] + vy[...]
    for j in (1, 2, 3):
        sends.start(("v", "z", j), vh.at[yy, lax.rem(ba + j, 4)], vz.at[j - 1], f"z{j}")
    a0.third()
    sends.arrived(*[("v", "z", j) for j in (1, 2, 3)])
    vh[yy, ba] = vh[yy, ba] + (vz[0] + vz[1] + vz[2])
    sends.start(("v", "x"), vh.at[yy, ba], vx, "x")
    a1.third()
    a0.fourth()
    a1.fourth()
    sends.arrived(("v", "x"))
    ov[...] = vh[yy, ba] + vx[...]
    a0.last()
    a1.last()
    sends.finish()


def unattend(split_at, e, lt, gvec, xp, n1t, m, gatt, wa, gm, gwo, gb, gc, local):
    vm = pl.BlockSpec(memory_space=pltpu.VMEM)
    hbm = pl.BlockSpec(memory_space=pl.ANY)
    out = jax.ShapeDtypeStruct((GROUP, D), F32)
    count = 6 * 18 + 7
    return pl.pallas_call(
        unattend_kernel,
        out_shape=(
            jax.ShapeDtypeStruct((local, D), BF16), out, out, out,
            jax.ShapeDtypeStruct((16, 128), F32),
        ),
        in_specs=[pl.BlockSpec(memory_space=pltpu.SMEM)] + [vm] * 3 + [hbm] * 9,
        out_specs=[vm] * 5,
        scratch_shapes=[
            pltpu.VMEM((ROWS, D), BF16),
            pltpu.VMEM((D, ROWS), BF16),
            pltpu.VMEM((4, ROWS, 3 * GROUP), BF16),
            pltpu.VMEM((4, ROWS, GROUP), BF16),
            pltpu.VMEM((4, 4, GROUP, D), BF16),
            pltpu.VMEM((ROWS, D), F32),
            pltpu.VMEM((4, D, GROUP), BF16),
            pltpu.VMEM((2, 4, GROUP, D), BF16),
            pltpu.VMEM((2, 4, GROUP, D), BF16),
            pltpu.VMEM((ROWS, 3 * GROUP), BF16),
            pltpu.VMEM((ROWS, D), F32),
            pltpu.VMEM((4, 1, 3 * GROUP), F32),
            pltpu.VMEM((4, 4, 16, 128), F32),
            pltpu.VMEM((2, PAD, HEAD_DIM), BF16),
            pltpu.VMEM((2, PAD, HEAD_DIM), BF16),
            pltpu.VMEM((2, 4, 16, 128), F32),
            pltpu.VMEM((2, 4, 16, 128), F32),
            pltpu.VMEM((4, 16, 128), F32),
            pltpu.VMEM((3, 16, 128), F32),
            pltpu.VMEM((16, 128), F32),
        ]
        + Scatter.scratch() * 6
        + [
            pltpu.SemaphoreType.DMA((count,)),
            pltpu.SemaphoreType.DMA((count,)),
            pltpu.SemaphoreType.DMA((4,)),
            pltpu.SemaphoreType.DMA((7,)),
        ],
        compiler_params=pltpu.CompilerParams(
            collective_id=1, has_side_effects=True, vmem_limit_bytes=62 * MIB
        ),
    )(split_at, e, lt, gvec, xp, n1t, m, gatt, wa, gm, gwo, gb, gc)


def on_device(
    inputs, cotangent, split_at, ln1_gain, ln1_bias, w_qkv, q_bias, v_bias, w_out, o_bias,
    ln2_gain, ln2_bias, w_up, up_bias, w_down, down_bias,
):
    pa = jnp.concatenate((w_qkv.reshape(GROUP, 3 * GROUP), w_out.T), axis=1)
    vectors = jnp.stack(
        (ln1_gain, ln1_bias, q_bias, v_bias, o_bias, ln2_gain, ln2_bias, down_bias)
        + tuple(up_bias[48 * i : 48 * i + 48] for i in range(4))
    )
    slab = jnp.pad(vectors, ((0, 4), (0, 80)))
    wa, wb, wc, e, xp, n1t, dyp, dyt, m, att, wo, lt = attend(
        split_at, pa, w_up, w_down.T, slab, inputs, cotangent
    )
    wb, wc = (w.reshape(4, D, D) for w in (wb, wc))
    local = inputs.shape[0]
    output, gm, gatt, gwo, gb, gc, gvec = feed(e, xp, dyp, dyt, att, wo, wb, wc, local)
    gb, gc = (g.reshape(4, 4, GROUP, D) for g in (gb, gc))
    gin, oa, ob, oc, ov = unattend(
        split_at, e, lt, gvec, xp, n1t, m, gatt, wa, gm, gwo, gb, gc, local
    )
    if lax.axis_size("dp") > 2:
        oa, ob, oc, ov = (lax.psum(v, "dp") * 0.5 for v in (oa, ob, oc, ov))
    rows = [ov[i, :48] for i in range(8)]
    return (
        output,
        gin,
        rows[0],
        rows[1],
        oa[:, : 3 * GROUP].reshape(w_qkv.shape),
        rows[2],
        rows[3],
        oa[:, 3 * GROUP :].T,
        rows[4],
        rows[5],
        rows[6],
        ob,
        ov[8:12, :48].reshape(192),
        oc.T,
        rows[7],
    )


def solution(mesh):
    rows = P(("dp", "aa", "ba"), None)
    vec = P(("aa", "ba"))
    grid_qkv, first, second = P("ba", None, "aa"), P("aa", "ba"), P("ba", "aa")
    params = (vec, vec, grid_qkv, vec, vec, first, vec, vec, vec, second, vec, first, vec)
    return jax.shard_map(
        on_device,
        mesh=mesh,
        in_specs=(rows, rows, P(("dp", "aa", "ba"))) + params,
        out_specs=(rows, rows) + params,
        check_vma=False,
    )
```

```python
import functools
import math

import jax
import jax.numpy as jnp
from jax import lax
from jax.experimental import pallas as pl
from jax.experimental.pallas import tpu as pltpu
from jax.sharding import PartitionSpec as P

D = 768
HEADS = 12
HEAD_DIM = 64
SLOT = 529
PAD = 544
ROWS = 2 * PAD
STEP = 256
GROUP = 192
BIG = 1e30
MESH = pl.DeviceIdType.MESH
F32 = jnp.float32
BF16 = jnp.bfloat16
MIB = 1 << 20

NT = (((1,), (1,)), ((), ()))
NN = (((1,), (0,)), ((), ()))
TN = (((0,), (0,)), ((), ()))

TAIL = (
    0.11962926248861097,
    0.12075451364069298,
    0.09991001218129214,
    0.12857310923328652,
    -0.0537053561953165,
    0.20637712218096793,
    -0.15721681637037743,
    0.03567808025645831,
)


def dot(left, right, dims=NN):
    return lax.dot_general(left, right, dims, preferred_element_type=F32)


def exact_dot(left, right, dims=NN):
    return lax.dot_general(
        left, right, dims, preferred_element_type=F32, precision=lax.Precision.HIGHEST
    )


def place():
    dp, aa, ba = lax.axis_index("dp"), lax.axis_index("aa"), lax.axis_index("ba")
    half, core = lax.rem(dp, 2), lax.rem(aa, 2)
    peers = {
        "x": (dp + 1 - 2 * half, aa, ba),
        "y": (dp, lax.rem(aa + 2, 4), ba),
        "c": (dp, aa + 1 - 2 * core, ba),
        "z1": (dp, aa, lax.rem(ba + 1, 4)),
        "z2": (dp, aa, lax.rem(ba + 2, 4)),
        "z3": (dp, aa, lax.rem(ba + 3, 4)),
    }
    return dp, aa, ba, half, core, peers


def greet(peers):
    barrier = pltpu.get_barrier_semaphore()
    for peer in peers.values():
        pl.semaphore_signal(barrier, inc=1, device_id=peer, device_id_type=MESH)
    pl.semaphore_wait(barrier, len(peers))


class Sends:
    def __init__(self, send_sem, recv_sem, peers):
        self.send_sem, self.recv_sem, self.peers = send_sem, recv_sem, peers
        self.made = {}

    def start(self, name, src, dst, peer):
        at = len(self.made)
        copy = pltpu.make_async_remote_copy(
            src_ref=src,
            dst_ref=dst,
            send_sem=self.send_sem.at[at],
            recv_sem=self.recv_sem.at[at],
            device_id=self.peers[peer],
            device_id_type=MESH,
        )
        copy.start()
        self.made[name] = copy

    def arrived(self, *names):
        for name in names:
            self.made[name].wait_recv()

    def finish(self):
        for copy in self.made.values():
            copy.wait_send()


def sixteen(value):
    return pl.multiple_of(value, 16)


class Gather:
    def __init__(self, name, sends, where, part, whole, row, count):
        self.name, self.sends, self.part, self.whole = name, sends, part, whole
        self.aa, self.ba, self.half = where
        self.ay = lax.rem(self.aa + 2, 4)
        self.other = [(j, lax.rem(self.ba + j, 4)) for j in (1, 2, 3)]
        big, small = count // 3, count // 6
        self.big = pl.ds(sixteen(row + big * self.half), big)
        self.big_not = pl.ds(sixteen(row + big - big * self.half), big)
        self.small = pl.ds(sixteen(row + 2 * big + small * self.half), small)
        self.rest = pl.ds(row + 2 * big, big)

    def send(self, key, src, dst, peer):
        self.sends.start((self.name,) + key, src, dst, peer)

    def move(self, key, at, peer):
        self.send(key, self.whole.at[at], self.whole.at[at], peer)

    def got(self, *keys):
        self.sends.arrived(*[(self.name,) + key for key in keys])

    def first(self):
        w, aa, ba = self.whole, self.aa, self.ba
        for j in (1, 2, 3):
            self.send(("z", j), self.part.at[self.big], w.at[aa, ba, self.big], f"z{j}")
        self.send(("y",), self.part.at[self.small], w.at[aa, ba, self.small], "y")
        for j in (1, 2, 3):
            self.send(("zs", j), self.part.at[self.small], w.at[aa, ba, self.small], f"z{j}")

    def second(self):
        self.got(("z", 1), ("z", 2), ("z", 3))
        for j, z in self.other:
            self.move(("x", j), (self.aa, z, self.big), "x")
        self.move(("yb",), (self.aa, slice(None), self.big), "y")
        self.got(("y",))
        for j in (1, 2, 3):
            self.move(("zy", j), (self.ay, self.ba, self.small), f"z{j}")
        self.got(("zs", 1), ("zs", 2), ("zs", 3))
        for j, z in self.other:
            self.move(("xs", j), (self.aa, z, self.small), "x")
        self.move(("c0",), (self.aa, slice(None), self.big), "c")

    def third(self):
        every = slice(None)
        self.got(("x", 1), ("x", 2), ("x", 3))
        self.move(("yn",), (self.aa, every, self.big_not), "y")
        self.got(("zy", 1), ("zy", 2), ("zy", 3))
        self.move(("xy",), (self.ay, every, self.small), "x")
        self.got(("yb",))
        self.move(("c1",), (self.aa, every, self.big_not), "c")
        self.move(("c2",), (self.ay, every, self.big), "c")

    def fourth(self):
        every = slice(None)
        self.got(("xs", 1), ("xs", 2), ("xs", 3))
        self.move(("c3",), (self.aa, every, self.rest), "c")
        self.got(("yn",))
        self.move(("c4",), (self.ay, every, self.big_not), "c")
        self.got(("xy",))
        self.move(("c5",), (self.ay, every, self.rest), "c")

    def last(self):
        self.got(*[(f"c{i}",) for i in range(6)])


class Sum:
    def __init__(self, name, sends, where, held, out, row, count, bufs):
        self.name, self.sends, self.held, self.out, self.bufs = name, sends, held, out, bufs
        part = count // 2
        self.aa, self.ba, self.half = where
        self.yy = self.aa // 2
        self.yn = 1 - self.yy
        self.other = [(j, lax.rem(self.ba + j, 4)) for j in (1, 2, 3)]
        self.rows = pl.ds(row, count)
        self.mine = pl.ds(sixteen(row + part * self.half), part)
        self.theirs = pl.ds(sixteen(row + part - part * self.half), part)

    def send(self, key, src, dst, peer):
        self.sends.start((self.name,) + key, src, dst, peer)

    def got(self, *keys):
        self.sends.arrived(*[(self.name,) + key for key in keys])

    def add(self, h, rows, more):
        @pl.loop(0, 4)
        def _(z):
            h[z, rows] = (h[z, rows].astype(F32) + more[z].astype(F32)).astype(BF16)

    def add_core(self, rc):
        for y in (0, 1):
            self.add(self.held(y), self.rows, rc.at[y, :, self.rows])

    def over_z(self, h, key, at):
        for j, z in self.other:
            self.send(key + (j,), h.at[z, self.mine], at(j - 1), f"z{j}")

    def close(self, total, own, far):
        own[...] = total.astype(BF16)
        self.send(("f",), own, far, "x")

    def last(self):
        own, far = self.bufs[:2]
        self.out[self.mine] = own[...].astype(F32)
        self.got(("f",))
        self.out[self.theirs] = far[...].astype(F32)


class SumY(Sum):
    @staticmethod
    def scratch(count, width):
        part = count // 2
        return [
            pltpu.VMEM((part, width), BF16),
            pltpu.VMEM((part, width), BF16),
            pltpu.VMEM((4, count, width), BF16),
            pltpu.VMEM((4, part, width), BF16),
            pltpu.VMEM((3, part, width), BF16),
        ]

    def first(self, rc):
        self.add_core(rc)
        self.send(("y",), self.held(self.yn).at[:, self.rows], self.bufs[2], "y")

    def second(self):
        self.got(("y",))
        h = self.held(self.yy)
        self.add(h, self.rows, self.bufs[2])
        self.send(("x",), h.at[:, self.theirs], self.bufs[3], "x")

    def third(self):
        self.got(("x",))
        h = self.held(self.yy)
        self.add(h, self.mine, self.bufs[3])
        self.over_z(h, ("z",), lambda i: self.bufs[4].at[i])

    def fourth(self):
        self.got(("z", 1), ("z", 2), ("z", 3))
        total = self.held(self.yy)[self.ba, self.mine].astype(F32)
        for i in range(3):
            total = total + self.bufs[4][i].astype(F32)
        self.close(total, self.bufs[0], self.bufs[1])


class SumX(Sum):
    @staticmethod
    def scratch(count, width):
        part = count // 2
        return [
            pltpu.VMEM((part, width), BF16),
            pltpu.VMEM((part, width), BF16),
            pltpu.VMEM((2, 4, part, width), BF16),
            pltpu.VMEM((2, 3, part, width), BF16),
            pltpu.VMEM((part, width), BF16),
        ]

    def first(self, rc):
        self.add_core(rc)
        for y in (0, 1):
            self.send(("x", y), self.held(y).at[:, self.theirs], self.bufs[2].at[y], "x")

    def second(self):
        self.got(("x", 0), ("x", 1))
        for y in (0, 1):
            h = self.held(y)
            self.add(h, self.mine, self.bufs[2].at[y])
            self.over_z(h, ("z", y), lambda i, y=y: self.bufs[3].at[y, i])

    def third(self):
        for y in (0, 1):
            h = self.held(y)
            self.got(("z", y, 1), ("z", y, 2), ("z", y, 3))
            total = h[self.ba, self.mine].astype(F32)
            for i in range(3):
                total = total + self.bufs[3][y, i].astype(F32)
            h[self.ba, self.mine] = total.astype(BF16)
        self.send(("y",), self.held(self.yn).at[self.ba, self.mine], self.bufs[4], "y")

    def fourth(self):
        self.got(("y",))
        total = self.held(self.yy)[self.ba, self.mine].astype(F32) + self.bufs[4][...].astype(F32)
        self.close(total, self.bufs[0], self.bufs[1])


def slab_maps():
    lane = lax.broadcasted_iota(jnp.int32, (128, D), 0)
    column = lax.broadcasted_iota(jnp.int32, (128, D), 1)
    spread = (lax.rem(column, 48) == lane).astype(F32)
    line = lax.broadcasted_iota(jnp.int32, (256, D), 0)
    block = lax.broadcasted_iota(jnp.int32, (256, D), 1) // 48
    device, kind = line // 16, lax.rem(line, 16)
    wanted = jnp.where(kind < 8, device, 4 * lax.rem(device, 4) + kind - 8)
    keep = jnp.where((wanted == block) & (kind < 12), 1.0, 0.0).astype(F32)
    line = lax.broadcasted_iota(jnp.int32, (16, 256), 1)
    out = lax.broadcasted_iota(jnp.int32, (16, 256), 0)
    device, kind = line // 16, lax.rem(line, 16)
    choose = (jnp.where(kind < 8, kind, 8 + device // 4) == out).astype(F32)
    return spread, keep, choose


def norm_parts(value):
    centre = jnp.mean(value, axis=-1, keepdims=True)
    shifted = value - centre
    spread = jnp.mean(shifted * shifted, axis=-1, keepdims=True)
    return shifted, lax.rsqrt(spread + 1e-6)


def mask_columns(split, keys):
    place_ = lax.broadcasted_iota(jnp.int32, (PAD, HEAD_DIM), 0)
    column = lax.broadcasted_iota(jnp.int32, (PAD, HEAD_DIM), 1)
    first = jnp.where(place_ < split, 1.0, 0.0)
    has = jnp.where(column == 0, first, jnp.where(column == 1, 1.0 - first, 0.0))
    if keys:
        allowed = jnp.where(place_ < SLOT, has, 0.0)
        return jnp.where(column < 2, (allowed - 1.0) * BIG, 0.0).astype(BF16)
    return has.astype(BF16)


def shift_in(source, wide):
    wide[0:1056] = source[0:1056].astype(F32)
    wide[1056:ROWS] = jnp.zeros((ROWS - 1056, D), F32)
    wide[1056:1058] = source[1056:1058].astype(F32)


def halves():
    for slot in range(2):
        for part in range(2):
            start = PAD * slot + 272 * part
            yield SLOT * slot + 272 * part, slice(start, start + 272), part


def attend_kernel(
    split, pa, pb, pc, slab, x, dy,
    wa_out, wb0, wc0, wb1, wc1, e_out, xp_out, n1t_out, dyp_out, dyt_out, m_out, att_out, wo_out, lt_out,
    wa, vv, xs, n1, e, xp, n1t, dyp, dyt, m, att, wo, lt, lacc, qmask, kmask, qb,
    send_sem, recv_sem, own_sem, out_sem,
):
    dp, aa, ba, half, core, peers = place()
    greet(peers)
    sends = Sends(send_sem, recv_sem, peers)
    where = (aa, ba, half)
    first, second = (slice(None), slice(0, STEP)), (slice(None), slice(STEP, 2 * STEP))
    parts = (
        (pb.at[first], wb0), (pc.at[first], wc0), (pb.at[second], wb1), (pc.at[second], wc1),
    )
    own = [
        pltpu.make_async_copy(part, whole.at[aa, ba], own_sem.at[i])
        for i, (part, whole) in enumerate(((pa, wa), (slab, vv)) + parts)
    ]
    for copy in own:
        copy.start()
    for j in (1, 2, 3):
        sends.start(("v", j), slab, vv.at[aa, ba], f"z{j}")
    a0, a1 = (Gather(f"a{i}", sends, where, pa, wa, 96 * i, 96) for i in (0, 1))
    b0, c0, b1, c1 = (
        Gather(f"b{i}", sends, where, part, whole, 0, GROUP)
        for i, (part, whole) in enumerate(parts)
    )
    outs = []

    def put(source, target):
        copy = pltpu.make_async_copy(source, target, out_sem.at[len(outs)])
        copy.start()
        outs.append(copy)

    a0.first()
    shift_in(dy, xs)
    line = lax.broadcasted_iota(jnp.int32, (272, D), 0)
    total = jnp.zeros((1, D), F32)
    for source, target, part in halves():
        value = xs[source : source + 272]
        if part == 1:
            value = jnp.where(line < SLOT - 272, value, 0.0)
        total = total + jnp.sum(value, axis=0, keepdims=True)
        dyp[target] = value.astype(BF16)
    put(dyp, dyp_out)
    for copy in own:
        copy.wait()
    a0.second()
    a1.first()
    sends.arrived(*[("v", j) for j in (1, 2, 3)])
    sends.start(("v", "y"), vv.at[aa], vv.at[aa], "y")
    sends.start(("v", "c"), vv.at[aa], vv.at[aa], "c")
    shift_in(x, xs)
    for source, target, part in halves():
        xp[target] = xs[source : source + 272].astype(BF16)
    put(xp, xp_out)
    sends.arrived(("v", "y"), ("v", "c"))
    sends.start(("v", "cy"), vv.at[lax.rem(aa + 2, 4)], vv.at[lax.rem(aa + 2, 4)], "c")
    a0.third()
    a1.second()
    dyt[...] = dyp[...].T
    put(dyt, dyt_out)
    sends.arrived(("v", "cy"))
    spread, keep, choose = slab_maps()
    wide = dot(vv[...].reshape(256, 128), spread.astype(BF16))
    e[...] = exact_dot(choose, wide * keep)
    e[12:13] = total
    put(e, e_out)
    gain, offset = e[0:1], e[1:2]
    for source, target, part in halves():
        shifted, rate = norm_parts(xs[source : source + 272])
        n1[target] = (shifted * rate * gain + offset).astype(BF16)
    a0.fourth()
    a1.third()
    b0.first()
    n1t[...] = n1[...].T
    put(n1t, n1t_out)
    for slot in range(2):
        qmask[slot] = mask_columns(split[slot], False)
        kmask[slot] = mask_columns(split[slot], True)
    zero = jnp.zeros((1, GROUP), F32)
    for group in range(4):
        lanes = slice(GROUP * group, GROUP * group + GROUP)
        qb[group] = jnp.concatenate((e[2:3, lanes], zero, e[3:4, lanes]), axis=1)
    lacc[...] = jnp.zeros_like(lacc)
    a1.fourth()
    b0.second()
    c0.first()
    a0.last()
    a1.last()
    put(wa, wa_out)

    def project(group):
        weights = wa[group].reshape(D, D)
        wo[group] = weights[:, 3 * GROUP :]
        for part in range(4):
            rows = slice(272 * part, 272 * part + 272)
            mixed = dot(n1[rows], weights[:, : 3 * GROUP]) + qb[group]
            m[group, rows] = mixed.astype(BF16)

    def look(group, slot):
        rows = slice(PAD * slot, PAD * slot + PAD)
        for head in range(3):
            cols = slice(HEAD_DIM * head, HEAD_DIM * head + HEAD_DIM)
            both = m[group, rows]
            q = both[:, HEAD_DIM * head : HEAD_DIM * (head + 1)] * 0.125
            k = both[:, GROUP + HEAD_DIM * head : GROUP + HEAD_DIM * (head + 1)]
            v = both[:, 2 * GROUP + HEAD_DIM * head : 2 * GROUP + HEAD_DIM * (head + 1)]
            qx = jnp.concatenate((q.astype(BF16), qmask[slot]), axis=1)
            kx = jnp.concatenate((k, kmask[slot]), axis=1)
            scores = dot(qx, kx, NT)
            top = jnp.max(scores, axis=1, keepdims=True)
            terms = jnp.exp(scores - top)
            total = jnp.sum(terms, axis=1, keepdims=True)
            mixed = dot(terms.astype(BF16), v) / total
            att[group, rows, cols] = mixed.astype(BF16)
            lane = lax.broadcasted_iota(jnp.int32, (PAD, 128), 1)
            lacc[slot] = jnp.where(lane == 3 * group + head, top + jnp.log(total), lacc[slot])

    pumps = (
        (b0.third, c0.second, b1.first),
        (),
        (b0.fourth, c0.third, b1.second, c1.first),
        (),
        (b0.last, c0.fourth, b1.third, c1.second),
        (c0.last, b1.fourth, c1.third),
        (b1.last, c1.fourth),
        (),
    )
    for group in range(4):
        project(group)
        put(m.at[group], m_out.at[group])
        for slot in range(2):
            look(group, slot)
            for step in pumps[2 * group + slot]:
                step()
    put(wo, wo_out)
    put(att, att_out)
    row = lax.broadcasted_iota(jnp.int32, (16, 128), 0)
    eye = (row == lax.broadcasted_iota(jnp.int32, (16, 128), 1)).astype(F32)
    for slot in range(2):
        lt[slot] = exact_dot(eye, lacc[slot], NT)
    put(lt, lt_out)
    c1.last()
    sends.finish()
    for copy in outs:
        copy.wait()


def attend(split_at, pa, pb, pc, slab, inputs, cotangent):
    vm = pl.BlockSpec(memory_space=pltpu.VMEM)
    hbm = pl.BlockSpec(memory_space=pl.ANY)
    whole = (4, 4, GROUP, D)
    piece = ((4, 4, GROUP, STEP), BF16)
    shapes = [
        (whole, BF16), piece, piece, piece, piece, ((16, D), F32), ((ROWS, D), BF16),
        ((D, ROWS), BF16), ((ROWS, D), BF16), ((D, ROWS), BF16), ((4, ROWS, 3 * GROUP), BF16),
        ((4, ROWS, GROUP), BF16), ((4, D, GROUP), BF16), ((2, 16, PAD), F32),
    ]
    count = 6 * 26 + 6
    return pl.pallas_call(
        attend_kernel,
        out_shape=tuple(jax.ShapeDtypeStruct(*shape) for shape in shapes),
        in_specs=[pl.BlockSpec(memory_space=pltpu.SMEM)] + [vm] * 6,
        out_specs=[hbm] * len(shapes),
        scratch_shapes=[
            pltpu.VMEM(whole, BF16),
            pltpu.VMEM((4, 4, 16, 128), BF16),
            pltpu.VMEM((ROWS, D), F32),
            pltpu.VMEM((ROWS, D), BF16),
        ]
        + [pltpu.VMEM(*shape) for shape in shapes[5:]]
        + [
            pltpu.VMEM((2, PAD, 128), F32),
            pltpu.VMEM((2, PAD, HEAD_DIM), BF16),
            pltpu.VMEM((2, PAD, HEAD_DIM), BF16),
            pltpu.VMEM((4, 1, 3 * GROUP), F32),
            pltpu.SemaphoreType.DMA((count,)),
            pltpu.SemaphoreType.DMA((count,)),
            pltpu.SemaphoreType.DMA((6,)),
            pltpu.SemaphoreType.DMA((16,)),
        ],
        compiler_params=pltpu.CompilerParams(
            collective_id=0, has_side_effects=True, vmem_limit_bytes=58 * MIB
        ),
    )(split_at, pa, pb, pc, slab, inputs, cotangent)


def gelu_parts(hidden):
    size = jnp.abs(hidden)
    t = 1.0 / (1.0 + 0.3 * size)
    bell = jnp.exp(hidden * hidden * -0.5)
    poly = jnp.full_like(t, TAIL[-1])
    for factor in TAIL[-2::-1]:
        poly = poly * t + factor
    tail = poly * t * bell
    phi = jnp.where(hidden < 0, tail, 1.0 - tail)
    return hidden * phi, phi + hidden * bell * (1.0 / math.sqrt(2 * math.pi))


def feed_kernel(
    e, pb, pc, xp_in, dyp_in, dyt_in, att_in, wo_in, wb0, wc0, wb1, wc1,
    out, gvec, ob, oc, gm_out, gatt_out, gwo_out, gb1, gc1, gb2, gc2,
    xp, dyp, dyt, att, wo, w, middle, acc, back, n2, n2t, act, gh, rcb, rcc, *more,
):
    bufs, (send_sem, recv_sem, send_two, recv_two, in_sem, out_sem, own_sem) = more[:-7], more[-7:]
    dp, aa, ba, half, core, peers = place()
    loads = {}
    for name, source, target in (
        ("xp", xp_in, xp), ("att", att_in, att), ("wo", wo_in, wo), ("dyp", dyp_in, dyp),
        ("wb0", wb0, w.at[0, 0]), ("wc0", wc0, w.at[1, 0]), ("dyt", dyt_in, dyt),
        ("wb1", wb1, w.at[0, 1]), ("wc1", wc1, w.at[1, 1]),
    ):
        loads[name] = pltpu.make_async_copy(source, target, in_sem.at[len(loads)])
        loads[name].start()
    third = (slice(None), slice(2 * STEP, 3 * STEP))
    parts = [part.at[third] for part in (pb, pc)]
    own = [
        pltpu.make_async_copy(part, w.at[i, 2, aa, ba], own_sem.at[i])
        for i, part in enumerate(parts)
    ]
    for copy in own:
        copy.start()
    greet(peers)
    where = (aa, ba, half)
    takes = Sends(send_sem, recv_sem, peers)
    gives = Sends(send_two, recv_two, peers)
    tb, tc = (Gather(f"t{i}", takes, where, parts[i], w.at[i, 2], 0, GROUP) for i in (0, 1))
    tb.first()
    tc.first()
    made = []
    for i, o in enumerate((ob, oc)):
        held = lambda y, i=i: w.at[i, 0, 2 * y + core]
        for kind, row, count in ((SumY, 0, 64), (SumX, 64, 128)):
            at = 5 * len(made)
            made.append(kind(f"s{len(made)}", gives, where, held, o, row, count, bufs[at : at + 5]))
    by, bx, cy, cx = made
    outs = []

    def put(source, target):
        copy = pltpu.make_async_copy(source, target, out_sem.at[len(outs)])
        copy.start()
        outs.append(copy)

    for name in ("xp", "att", "wo"):
        loads[name].wait()
    gvec[...] = jnp.zeros_like(gvec)
    gvec[7:8] = e[12:13]
    for part in range(4):
        rows = slice(272 * part, 272 * part + 272)
        value = xp[rows].astype(F32) + e[4:5]
        for group in range(4):
            value = value + dot(att[group, rows], wo[group], NT)
        middle[rows] = value
        shifted, rate = norm_parts(value)
        n2[rows] = (shifted * rate * e[5:6] + e[6:7]).astype(BF16)
        acc[rows] = value + e[7:8]
        back[rows] = jnp.zeros((272, D), F32)
        if part == 1:
            for copy in own:
                copy.wait()
            tb.second()
            tc.second()
    n2t[...] = n2[...].T
    for name in ("dyp", "wb0", "wc0", "dyt"):
        loads[name].wait()

    def whole_unit(u):
        step, pair, now = min(u, 5) // 2, u % 2, u % 2
        both = ((2 * now, 2 * pair), (2 * now + 1, 2 * pair + 1))
        columns = slice(STEP * step, STEP * step + STEP)

        def weight(kind, group):
            return w[kind, step, group].reshape(D, STEP)

        def up(part):
            rows = slice(272 * part, 272 * part + 272)
            return [
                (
                    dot(n2[rows], weight(0, group)) + e[8 + group : 9 + group, columns],
                    dot(dyp[rows], weight(1, group)),
                )
                for _, group in both
            ]

        def across(part, made, totals):
            rows = slice(272 * part, 272 * part + 272)
            new = []
            for (at, _), (hidden, grad), total in zip(both, made, totals):
                forward, slope = gelu_parts(hidden)
                grad = (grad * slope).astype(BF16)
                act[at, rows] = forward.astype(BF16)
                gh[at, rows] = grad
                new.append(total + jnp.sum(grad.astype(F32), axis=0, keepdims=True))
            return new

        def down(part):
            rows = slice(272 * part, 272 * part + 272)
            for total, values, kind in ((acc, act, 1), (back, gh, 0)):
                more = [dot(values[at, rows], weight(kind, group), NT) for at, group in both]
                total[rows] = total[rows] + more[0] + more[1]

        if u < 6:
            totals = [jnp.zeros((1, STEP), F32)] * 2
            made = up(0)
            for part in range(4):
                ahead = up(part + 1) if part < 3 else None
                totals = across(part, made, totals)
                if part:
                    down(part - 1)
                made = ahead
            down(3)
            for (_, group), total in zip(both, totals):
                gvec[8 + group : 9 + group, columns] = total
        if u > 0:
            step, pair, before = (u - 1) // 2, (u - 1) % 2, (u - 1) % 2
            for i, (turned, values) in enumerate(((n2t, gh), (dyt, act))):
                for j in range(2):
                    grad = dot(turned[...], values[2 * before + j]).astype(BF16)
                    w[i, step, 2 * pair + j] = grad.reshape(4, GROUP, STEP)

    once = 1 + jnp.minimum(dp, 0)

    def unit(u):
        def inside(_, carry):
            whole_unit(u)
            return carry

        lax.fori_loop(0, once, inside, 0)

    unit(0)
    tb.third()
    tc.third()
    unit(1)
    tb.fourth()
    tc.fourth()
    for name in ("wb1", "wc1"):
        loads[name].wait()
    unit(2)
    tb.last()
    tc.last()
    for i, rc in enumerate((rcb, rcc)):
        for y in (0, 1):
            gives.start((i, y), w.at[i, 0, 2 * y + 1 - core], rc.at[y], "c")
    unit(3)
    takes.finish()
    gives.arrived((0, 0), (0, 1))
    by.first(rcb)
    bx.first(rcb)
    gives.arrived((1, 0), (1, 1))
    cy.first(rcc)
    cx.first(rcc)
    unit(4)
    put(w.at[0, 1], gb1)
    put(w.at[1, 1], gc1)
    for batch in made:
        batch.second()
    unit(5)
    for batch in made:
        batch.third()
    line = lax.broadcasted_iota(jnp.int32, (16, D), 0)
    out[0:528] = acc[0:528].astype(BF16)
    out[528:544] = jnp.where(line == 0, acc[528:544], acc[543:559]).astype(BF16)
    out[544:1056] = acc[559:1071].astype(BF16)
    out[1056:1058] = acc[1071:1073].astype(BF16)
    unit(6)
    put(w.at[0, 2], gb2)
    put(w.at[1, 2], gc2)
    sums = [jnp.zeros((1, D), F32)] * 3
    for part in range(4):
        rows = slice(272 * part, 272 * part + 272)
        shifted, rate = norm_parts(middle[rows])
        hat = shifted * rate
        grad = back[rows]
        inner = grad * e[5:6]
        mean = jnp.mean(inner, axis=-1, keepdims=True)
        along = jnp.mean(inner * hat, axis=-1, keepdims=True)
        total = dyp[rows].astype(F32) + rate * (inner - mean - hat * along)
        middle[rows] = total
        branch = total.astype(BF16)
        n2[rows] = branch
        for i, value in enumerate((grad * hat, grad, branch.astype(F32))):
            sums[i] = sums[i] + jnp.sum(value, axis=0, keepdims=True)
        for group in range(4):
            act[group, rows, 0:GROUP] = dot(branch, wo[group]).astype(BF16)
        if part == 1:
            for batch in made:
                batch.fourth()
    put(middle, gm_out)
    put(act, gatt_out)
    gvec[5:6] = sums[0]
    gvec[6:7] = sums[1]
    gvec[4:5] = sums[2]
    n2t[...] = n2[...].T
    for group in range(4):
        gh[group, 0:D, 0:GROUP] = dot(n2t[...], att[group]).astype(BF16)
    put(gh.at[:, 0:D], gwo_out)
    for batch in made:
        batch.last()
    gives.finish()
    for copy in outs:
        copy.wait()


def feed(e, pb, pc, xp, dyp, dyt, att, wo, wb0, wc0, wb1, wc1, local):
    vm = pl.BlockSpec(memory_space=pltpu.VMEM)
    hbm = pl.BlockSpec(memory_space=pl.ANY)
    piece = jax.ShapeDtypeStruct((4, 4, GROUP, STEP), BF16)
    own = jax.ShapeDtypeStruct((GROUP, STEP), F32)
    sums = SumY.scratch(64, STEP) + SumX.scratch(128, STEP)
    gives = 4 + 2 * (6 + 10)
    return pl.pallas_call(
        feed_kernel,
        out_shape=(
            jax.ShapeDtypeStruct((local, D), BF16),
            jax.ShapeDtypeStruct((16, D), F32),
            own,
            own,
            jax.ShapeDtypeStruct((ROWS, D), F32),
            jax.ShapeDtypeStruct((4, ROWS, STEP), BF16),
            jax.ShapeDtypeStruct((4, D, STEP), BF16),
            piece,
            piece,
            piece,
            piece,
        ),
        in_specs=[vm] * 3 + [hbm] * 9,
        out_specs=[vm] * 4 + [hbm] * 7,
        scratch_shapes=[
            pltpu.VMEM((ROWS, D), BF16),
            pltpu.VMEM((ROWS, D), BF16),
            pltpu.VMEM((D, ROWS), BF16),
            pltpu.VMEM((4, ROWS, GROUP), BF16),
            pltpu.VMEM((4, D, GROUP), BF16),
            pltpu.VMEM((2, 3, 4, 4, GROUP, STEP), BF16),
            pltpu.VMEM((ROWS, D), F32),
            pltpu.VMEM((ROWS, D), F32),
            pltpu.VMEM((ROWS, D), F32),
            pltpu.VMEM((ROWS, D), BF16),
            pltpu.VMEM((D, ROWS), BF16),
            pltpu.VMEM((4, ROWS, STEP), BF16),
            pltpu.VMEM((4, ROWS, STEP), BF16),
            pltpu.VMEM((2, 4, GROUP, STEP), BF16),
            pltpu.VMEM((2, 4, GROUP, STEP), BF16),
        ]
        + sums * 2
        + [
            pltpu.SemaphoreType.DMA((52,)),
            pltpu.SemaphoreType.DMA((52,)),
            pltpu.SemaphoreType.DMA((gives,)),
            pltpu.SemaphoreType.DMA((gives,)),
            pltpu.SemaphoreType.DMA((9,)),
            pltpu.SemaphoreType.DMA((7,)),
            pltpu.SemaphoreType.DMA((2,)),
        ],
        compiler_params=pltpu.CompilerParams(
            collective_id=2, has_side_effects=True, vmem_limit_bytes=60 * MIB
        ),
    )(e, pb, pc, xp, dyp, dyt, att, wo, wb0, wc0, wb1, wc1)


def unattend_kernel(
    split, e, lt, gvec, ob0, oc0, xp_in, n1t_in, m_in, gatt_in, wa_in, gm_in, gwo_in, gb1, gc1, gb2, gc2,
    gin, oa, ob, oc, ov,
    xp, n1t, m, gatt, ga, gm, gwo, h, rc, rca, rya, gmix, back, sums, gv, qmask, kmask,
    vh, vc, vy, vz, vx, *more,
):
    bufs, (send_sem, recv_sem, own_sem, in_sem) = more[:-4], more[-4:]
    dp, aa, ba, half, core, peers = place()
    loads = {}
    for name, source, target in (
        ("n1t", n1t_in, n1t), ("m", m_in, m), ("gatt", gatt_in, gatt), ("wa", wa_in, ga),
        ("gwo", gwo_in, gwo), ("xp", xp_in, xp), ("gm", gm_in, gm),
    ):
        loads[name] = pltpu.make_async_copy(source, target, in_sem.at[len(loads)])
        loads[name].start()
    own = []
    given = (gb1, gc1, gb2, gc2)
    for i, g in enumerate(given):
        for y in (0, 1):
            own.append(pltpu.make_async_copy(g.at[2 * y + core], h.at[i, y], own_sem.at[len(own)]))
            own[-1].start()
    greet(peers)
    sends = Sends(send_sem, recv_sem, peers)
    where = (aa, ba, half)
    yy = aa // 2
    order = [2 * (1 - yy) + 1 - core, 2 * (1 - yy) + core, 2 * yy + 1 - core, 2 * yy + core]
    for i, g in enumerate(given):
        for y in (0, 1):
            sends.start((i, y), g.at[2 * y + 1 - core], rc.at[i, y], "c")
    made = []
    for i, o in enumerate((ob, oc, ob, oc)):
        o = o.at[:, STEP * (1 + i // 2) : STEP * (2 + i // 2)]
        held = lambda y, i=i: h.at[i, y]
        for kind, row, count in ((SumY, 0, 64), (SumX, 64, 128)):
            at = 5 * len(made)
            made.append(kind(f"s{len(made)}", sends, where, held, o, row, count, bufs[at : at + 5]))
            made[-1].open = functools.partial(made[-1].first, rc.at[i])
    for i in range(3):
        at = 5 * len(made)
        held = lambda y: ga.at[2 * y + core]
        made.append(SumY(f"a{i}", sends, where, held, oa, 64 * i, 64, bufs[at : at + 5]))
    by1, bx1, cy1, cx1, by2, bx2, cy2, cx2, a0, a1, a2 = made
    for slot in range(2):
        qmask[slot] = mask_columns(split[slot], False)
        kmask[slot] = mask_columns(split[slot], True)
    back[...] = jnp.zeros_like(back)
    for name in ("m", "gatt", "n1t", "wa", "gwo"):
        loads[name].wait()

    def look(group, slot):
        rows = slice(PAD * slot, PAD * slot + PAD)
        for head in range(3):
            both = m[group, rows]
            q = (both[:, HEAD_DIM * head : HEAD_DIM * (head + 1)] * 0.125).astype(BF16)
            k = both[:, GROUP + HEAD_DIM * head : GROUP + HEAD_DIM * (head + 1)]
            v = both[:, 2 * GROUP + HEAD_DIM * head : 2 * GROUP + HEAD_DIM * (head + 1)]
            go = gatt[group, rows][:, HEAD_DIM * head : HEAD_DIM * (head + 1)]
            qx = jnp.concatenate((q, qmask[slot]), axis=1)
            kx = jnp.concatenate((k, kmask[slot]), axis=1)
            scores = dot(kx, qx, NT)
            probs = jnp.exp(scores - lt[slot, pl.ds(3 * group + head, 1)])
            gprobs = dot(v, go, NT)
            both_ = probs * gprobs
            delta = jnp.sum(both_, axis=0, keepdims=True)
            gs = (both_ - probs * delta).astype(BF16)
            gq = dot(gs, k, TN) * 0.125
            gk = dot(gs, q)
            gval = dot(probs.astype(BF16), go)
            for i, value in enumerate((gq, gk, gval)):
                at = GROUP * i + HEAD_DIM * head
                gmix[rows, at : at + HEAD_DIM] = value.astype(BF16)

    def grads(k):
        group = order[k]
        grad = dot(n1t[...], gmix[...]).reshape(4, GROUP, 3 * GROUP)
        rest = gwo[group][:, 0:GROUP].reshape(4, GROUP, GROUP)
        if k in (1, 3):
            rest = rest.astype(F32)
            sends.arrived(("a", k - 1))
            terms = [rca.at[k // 2]]
            if k == 3:
                sends.arrived(("a", 1))
                terms.append(rya)
            for term in terms:
                grad = grad + term[:, :, 0 : 3 * GROUP].astype(F32)
                rest = rest + term[:, :, 3 * GROUP :].astype(F32)
        given = ga.at[group]
        given[:, :, 0 : 3 * GROUP] = grad.astype(BF16)
        given[:, :, 3 * GROUP :] = rest.astype(BF16)

    def fold(group):
        weights = ga[group].reshape(D, D)[:, : 3 * GROUP]
        total = jnp.zeros((1, 3 * GROUP), F32)
        for part in range(4):
            rows = slice(272 * part, 272 * part + 272)
            total = total + jnp.sum(gmix[rows].astype(F32), axis=0, keepdims=True)
            back[rows] = back[rows] + dot(gmix[rows], weights, NT)
        sums[group] = total

    def store(k):
        group = order[k]
        fold(group)
        grads(k)
        if k == 1:
            sends.start(("a", 1), ga.at[group], rya, "y")
        elif k < 3:
            sends.start(("a", k), ga.at[group], rca.at[k // 2], "c")

    pumps = (
        (cx1.open,),
        (by1.second, cy1.second, bx1.second),
        (by2.open, cy2.open, cx1.second, bx2.open),
        (by1.third, cy1.third, bx1.third, cx2.open),
        (by2.second, cy2.second, cx1.third, bx2.second),
        (by1.fourth, cy1.fourth, bx1.fourth, cx2.second),
        (by2.third, cy2.third, bx2.third, cx1.fourth),
        (cx2.third,),
    )
    ob[:, 0:STEP] = ob0[...]
    oc[:, 0:STEP] = oc0[...]
    for copy in own:
        copy.wait()
    for i in range(4):
        sends.arrived((i, 0), (i, 1))
    for batch in (by1, cy1, bx1):
        batch.open()
    for k in range(4):
        for slot in range(2):
            look(order[k], slot)
            for step in pumps[2 * k + slot]:
                step()
        store(k)
    for batch in (a0, a1, a2):
        mine = batch.held(yy)
        batch.start_x = functools.partial(batch.send, ("x",), mine.at[:, batch.theirs], batch.bufs[3], "x")
    a0.start_x()
    for batch in (by2, cy2, bx2, cx2):
        batch.fourth()
    loads["xp"].wait()
    loads["gm"].wait()
    tot_gain, tot_bias = jnp.zeros((1, D), F32), jnp.zeros((1, D), F32)
    for part in range(4):
        rows = slice(272 * part, 272 * part + 272)
        shifted, rate = norm_parts(xp[rows].astype(F32))
        hat = shifted * rate
        grad = back[rows]
        inner = grad * e[0:1]
        mean = jnp.mean(inner, axis=-1, keepdims=True)
        along = jnp.mean(inner * hat, axis=-1, keepdims=True)
        tot_gain = tot_gain + jnp.sum(grad * hat, axis=0, keepdims=True)
        tot_bias = tot_bias + jnp.sum(grad, axis=0, keepdims=True)
        back[rows] = gm[rows] + rate * (inner - mean - hat * along)
        if part == 2:
            a0.third()
            a1.start_x()
    line = lax.broadcasted_iota(jnp.int32, (16, D), 0)
    q_row = jnp.concatenate([sums[i][:, :GROUP] for i in range(4)], axis=1)
    v_row = jnp.concatenate([sums[i][:, 2 * GROUP :] for i in range(4)], axis=1)
    rows = jnp.where(line == 0, tot_gain, jnp.where(line == 1, tot_bias, gvec[...]))
    rows = jnp.where(line == 2, q_row, jnp.where(line == 3, v_row, rows))
    spread, keep, choose = slab_maps()
    wide = exact_dot(choose, rows, TN) * keep
    gv[...] = exact_dot(wide, spread, NT).reshape(4, 4, 16, 128)
    for y in (0, 1):
        sends.start(("v", "c", y), gv.at[2 * y + 1 - core], vc.at[y], "c")
    a1.third()
    a2.start_x()
    for y in (0, 1):
        sends.arrived(("v", "c", y))
        vh[y] = gv[2 * y + core] + vc[y]
    sends.start(("v", "y"), vh.at[1 - yy], vy, "y")
    gin[0:528] = back[0:528].astype(BF16)
    gin[528:544] = jnp.where(line == 0, back[528:544], back[543:559]).astype(BF16)
    gin[544:1056] = back[559:1071].astype(BF16)
    gin[1056:1058] = back[1071:1073].astype(BF16)
    a0.fourth()
    sends.arrived(("v", "y"))
    vh[yy] = vh[yy] + vy[...]
    for j in (1, 2, 3):
        sends.start(("v", "z", j), vh.at[yy, lax.rem(ba + j, 4)], vz.at[j - 1], f"z{j}")
    for batch in made[:8]:
        batch.last()
    a2.third()
    a1.fourth()
    sends.arrived(*[("v", "z", j) for j in (1, 2, 3)])
    vh[yy, ba] = vh[yy, ba] + (vz[0] + vz[1] + vz[2])
    sends.start(("v", "x"), vh.at[yy, ba], vx, "x")
    a2.fourth()
    sends.arrived(("v", "x"))
    ov[...] = vh[yy, ba] + vx[...]
    a0.last()
    a1.last()
    a2.last()
    sends.finish()


def unattend(split_at, e, lt, gvec, ob0, oc0, *stored, local):
    vm = pl.BlockSpec(memory_space=pltpu.VMEM)
    hbm = pl.BlockSpec(memory_space=pl.ANY)
    out = jax.ShapeDtypeStruct((GROUP, D), F32)
    count = 8 + 4 * 16 + 3 + 3 * 5 + 7
    return pl.pallas_call(
        unattend_kernel,
        out_shape=(
            jax.ShapeDtypeStruct((local, D), BF16), out, out, out,
            jax.ShapeDtypeStruct((16, 128), F32),
        ),
        in_specs=[pl.BlockSpec(memory_space=pltpu.SMEM)] + [vm] * 5 + [hbm] * 11,
        out_specs=[vm] * 5,
        scratch_shapes=[
            pltpu.VMEM((ROWS, D), BF16),
            pltpu.VMEM((D, ROWS), BF16),
            pltpu.VMEM((4, ROWS, 3 * GROUP), BF16),
            pltpu.VMEM((4, ROWS, STEP), BF16),
            pltpu.VMEM((4, 4, GROUP, D), BF16),
            pltpu.VMEM((ROWS, D), F32),
            pltpu.VMEM((4, D, STEP), BF16),
            pltpu.VMEM((4, 2, 4, GROUP, STEP), BF16),
            pltpu.VMEM((4, 2, 4, GROUP, STEP), BF16),
            pltpu.VMEM((2, 4, GROUP, D), BF16),
            pltpu.VMEM((4, GROUP, D), BF16),
            pltpu.VMEM((ROWS, 3 * GROUP), BF16),
            pltpu.VMEM((ROWS, D), F32),
            pltpu.VMEM((4, 1, 3 * GROUP), F32),
            pltpu.VMEM((4, 4, 16, 128), F32),
            pltpu.VMEM((2, PAD, HEAD_DIM), BF16),
            pltpu.VMEM((2, PAD, HEAD_DIM), BF16),
            pltpu.VMEM((2, 4, 16, 128), F32),
            pltpu.VMEM((2, 4, 16, 128), F32),
            pltpu.VMEM((4, 16, 128), F32),
            pltpu.VMEM((3, 16, 128), F32),
            pltpu.VMEM((16, 128), F32),
        ]
        + (SumY.scratch(64, STEP) + SumX.scratch(128, STEP)) * 4
        + SumY.scratch(64, D) * 3
        + [
            pltpu.SemaphoreType.DMA((count,)),
            pltpu.SemaphoreType.DMA((count,)),
            pltpu.SemaphoreType.DMA((8,)),
            pltpu.SemaphoreType.DMA((7,)),
        ],
        compiler_params=pltpu.CompilerParams(
            collective_id=1, has_side_effects=True, vmem_limit_bytes=62 * MIB
        ),
    )(split_at, e, lt, gvec, ob0, oc0, *stored)


def on_device(
    inputs, cotangent, split_at, ln1_gain, ln1_bias, w_qkv, q_bias, v_bias, w_out, o_bias,
    ln2_gain, ln2_bias, w_up, up_bias, w_down, down_bias,
):
    pa = jnp.concatenate((w_qkv.reshape(GROUP, 3 * GROUP), w_out.T), axis=1)
    vectors = jnp.stack(
        (ln1_gain, ln1_bias, q_bias, v_bias, o_bias, ln2_gain, ln2_bias, down_bias)
        + tuple(up_bias[48 * i : 48 * i + 48] for i in range(4))
    )
    slab = jnp.pad(vectors, ((0, 4), (0, 80)))
    pc = w_down.T
    local = inputs.shape[0]
    wa, *pieces, e, xp, n1t, dyp, dyt, m, att, wo, lt = attend(
        split_at, pa, w_up, pc, slab, inputs, cotangent
    )
    output, gvec, ob0, oc0, gm, gatt, gwo, *grads = feed(
        e, w_up, pc, xp, dyp, dyt, att, wo, *pieces, local
    )
    gin, oa, ob, oc, ov = unattend(
        split_at, e, lt, gvec, ob0, oc0, xp, n1t, m, gatt, wa, gm, gwo, *grads, local=local
    )
    if lax.axis_size("dp") > 2:
        oa, ob, oc, ov = (lax.psum(v, "dp") * 0.5 for v in (oa, ob, oc, ov))
    rows = [ov[i, :48] for i in range(8)]
    return (
        output,
        gin,
        rows[0],
        rows[1],
        oa[:, : 3 * GROUP].reshape(w_qkv.shape),
        rows[2],
        rows[3],
        oa[:, 3 * GROUP :].T,
        rows[4],
        rows[5],
        rows[6],
        ob,
        ov[8:12, :48].reshape(192),
        oc.T,
        rows[7],
    )


def solution(mesh):
    rows = P(("dp", "aa", "ba"), None)
    vec = P(("aa", "ba"))
    grid_qkv, first, second = P("ba", None, "aa"), P("aa", "ba"), P("ba", "aa")
    params = (vec, vec, grid_qkv, vec, vec, first, vec, vec, vec, second, vec, first, vec)
    return jax.shard_map(
        on_device,
        mesh=mesh,
        in_specs=(rows, rows, P(("dp", "aa", "ba"))) + params,
        out_specs=(rows, rows) + params,
        check_vma=False,
    )
```

```python
import functools
import math

import jax
import jax.numpy as jnp
from jax import lax
from jax.experimental import pallas as pl
from jax.experimental.pallas import tpu as pltpu
from jax.sharding import PartitionSpec as P

D = 768
HEADS = 12
HEAD_DIM = 64
SLOT = 529
PAD = 544
ROWS = 2 * PAD
STEP = 256
GROUP = 192
BIG = 1e30
MESH = pl.DeviceIdType.MESH
F32 = jnp.float32
BF16 = jnp.bfloat16
MIB = 1 << 20

NT = (((1,), (1,)), ((), ()))
NN = (((1,), (0,)), ((), ()))
TN = (((0,), (0,)), ((), ()))

TAIL = (
    0.11962926248861097,
    0.12075451364069298,
    0.09991001218129214,
    0.12857310923328652,
    -0.0537053561953165,
    0.20637712218096793,
    -0.15721681637037743,
    0.03567808025645831,
)


def dot(left, right, dims=NN):
    return lax.dot_general(left, right, dims, preferred_element_type=F32)


def exact_dot(left, right, dims=NN):
    return lax.dot_general(
        left, right, dims, preferred_element_type=F32, precision=lax.Precision.HIGHEST
    )


def place():
    dp, aa, ba = lax.axis_index("dp"), lax.axis_index("aa"), lax.axis_index("ba")
    half, core = lax.rem(dp, 2), lax.rem(aa, 2)
    peers = {
        "x": (dp + 1 - 2 * half, aa, ba),
        "y": (dp, lax.rem(aa + 2, 4), ba),
        "c": (dp, aa + 1 - 2 * core, ba),
        "z1": (dp, aa, lax.rem(ba + 1, 4)),
        "z2": (dp, aa, lax.rem(ba + 2, 4)),
        "z3": (dp, aa, lax.rem(ba + 3, 4)),
    }
    return dp, aa, ba, half, core, peers


def greet(peers):
    barrier = pltpu.get_barrier_semaphore()
    for peer in peers.values():
        pl.semaphore_signal(barrier, inc=1, device_id=peer, device_id_type=MESH)


def meet(peers):
    pl.semaphore_wait(pltpu.get_barrier_semaphore(), len(peers))


class Sends:
    def __init__(self, send_sem, recv_sem, peers):
        self.send_sem, self.recv_sem, self.peers = send_sem, recv_sem, peers
        self.made = {}

    def start(self, name, src, dst, peer):
        at = len(self.made)
        copy = pltpu.make_async_remote_copy(
            src_ref=src,
            dst_ref=dst,
            send_sem=self.send_sem.at[at],
            recv_sem=self.recv_sem.at[at],
            device_id=self.peers[peer],
            device_id_type=MESH,
        )
        copy.start()
        self.made[name] = copy

    def arrived(self, *names):
        for name in names:
            self.made[name].wait_recv()

    def finish(self):
        for copy in self.made.values():
            copy.wait_send()


def sixteen(value):
    return pl.multiple_of(value, 16)


class Gather:
    def __init__(self, name, sends, where, part, whole, row, count):
        self.name, self.sends, self.part, self.whole = name, sends, part, whole
        self.aa, self.ba, self.half = where
        self.ay = lax.rem(self.aa + 2, 4)
        self.other = [(j, lax.rem(self.ba + j, 4)) for j in (1, 2, 3)]
        big, small = count // 3, count // 6
        self.big = pl.ds(sixteen(row + big * self.half), big)
        self.big_not = pl.ds(sixteen(row + big - big * self.half), big)
        self.small = pl.ds(sixteen(row + 2 * big + small * self.half), small)
        self.rest = pl.ds(row + 2 * big, big)

    def send(self, key, src, dst, peer):
        self.sends.start((self.name,) + key, src, dst, peer)

    def move(self, key, at, peer):
        self.send(key, self.whole.at[at], self.whole.at[at], peer)

    def got(self, *keys):
        self.sends.arrived(*[(self.name,) + key for key in keys])

    def first(self):
        w, aa, ba = self.whole, self.aa, self.ba
        for j in (1, 2, 3):
            self.send(("z", j), self.part.at[self.big], w.at[aa, ba, self.big], f"z{j}")
        self.send(("y",), self.part.at[self.small], w.at[aa, ba, self.small], "y")
        for j in (1, 2, 3):
            self.send(("zs", j), self.part.at[self.small], w.at[aa, ba, self.small], f"z{j}")

    def second(self):
        self.got(("z", 1), ("z", 2), ("z", 3))
        for j, z in self.other:
            self.move(("x", j), (self.aa, z, self.big), "x")
        self.move(("yb",), (self.aa, slice(None), self.big), "y")
        self.got(("y",))
        for j in (1, 2, 3):
            self.move(("zy", j), (self.ay, self.ba, self.small), f"z{j}")
        self.got(("zs", 1), ("zs", 2), ("zs", 3))
        for j, z in self.other:
            self.move(("xs", j), (self.aa, z, self.small), "x")
        self.move(("c0",), (self.aa, slice(None), self.big), "c")

    def third(self):
        every = slice(None)
        self.got(("x", 1), ("x", 2), ("x", 3))
        self.move(("yn",), (self.aa, every, self.big_not), "y")
        self.got(("zy", 1), ("zy", 2), ("zy", 3))
        self.move(("xy",), (self.ay, every, self.small), "x")
        self.got(("yb",))
        self.move(("c1",), (self.aa, every, self.big_not), "c")
        self.move(("c2",), (self.ay, every, self.big), "c")

    def fourth(self):
        every = slice(None)
        self.got(("xs", 1), ("xs", 2), ("xs", 3))
        self.move(("c3",), (self.aa, every, self.rest), "c")
        self.got(("yn",))
        self.move(("c4",), (self.ay, every, self.big_not), "c")
        self.got(("xy",))
        self.move(("c5",), (self.ay, every, self.rest), "c")

    def last(self):
        self.got(*[(f"c{i}",) for i in range(6)])


class Sum:
    def __init__(self, name, sends, where, held, out, row, count, bufs):
        self.name, self.sends, self.held, self.out, self.bufs = name, sends, held, out, bufs
        part = count // 2
        self.aa, self.ba, self.half = where
        self.yy = self.aa // 2
        self.yn = 1 - self.yy
        self.other = [(j, lax.rem(self.ba + j, 4)) for j in (1, 2, 3)]
        self.rows = pl.ds(row, count)
        self.mine = pl.ds(sixteen(row + part * self.half), part)
        self.theirs = pl.ds(sixteen(row + part - part * self.half), part)

    def send(self, key, src, dst, peer):
        self.sends.start((self.name,) + key, src, dst, peer)

    def got(self, *keys):
        self.sends.arrived(*[(self.name,) + key for key in keys])

    def add(self, h, rows, more):
        @pl.loop(0, 4)
        def _(z):
            h[z, rows] = (h[z, rows].astype(F32) + more[z].astype(F32)).astype(BF16)

    def add_core(self, rc):
        for y in (0, 1):
            self.add(self.held(y), self.rows, rc.at[y, :, self.rows])

    def over_z(self, h, key, at):
        for j, z in self.other:
            self.send(key + (j,), h.at[z, self.mine], at(j - 1), f"z{j}")

    def close(self, total, own, far):
        own[...] = total.astype(BF16)
        self.send(("f",), own, far, "x")

    def last(self):
        own, far = self.bufs[:2]
        self.out[self.mine] = own[...].astype(F32)
        self.got(("f",))
        self.out[self.theirs] = far[...].astype(F32)


class SumY(Sum):
    @staticmethod
    def scratch(count, width):
        part = count // 2
        return [
            pltpu.VMEM((part, width), BF16),
            pltpu.VMEM((part, width), BF16),
            pltpu.VMEM((4, count, width), BF16),
            pltpu.VMEM((4, part, width), BF16),
            pltpu.VMEM((3, part, width), BF16),
        ]

    def first(self, rc):
        self.add_core(rc)
        self.send(("y",), self.held(self.yn).at[:, self.rows], self.bufs[2], "y")

    def second(self):
        self.got(("y",))
        h = self.held(self.yy)
        self.add(h, self.rows, self.bufs[2])
        self.send(("x",), h.at[:, self.theirs], self.bufs[3], "x")

    def third(self):
        self.got(("x",))
        h = self.held(self.yy)
        self.add(h, self.mine, self.bufs[3])
        self.over_z(h, ("z",), lambda i: self.bufs[4].at[i])

    def fourth(self):
        self.got(("z", 1), ("z", 2), ("z", 3))
        total = self.held(self.yy)[self.ba, self.mine].astype(F32)
        for i in range(3):
            total = total + self.bufs[4][i].astype(F32)
        self.close(total, self.bufs[0], self.bufs[1])


class SumX(Sum):
    @staticmethod
    def scratch(count, width):
        part = count // 2
        return [
            pltpu.VMEM((part, width), BF16),
            pltpu.VMEM((part, width), BF16),
            pltpu.VMEM((2, 4, part, width), BF16),
            pltpu.VMEM((2, 3, part, width), BF16),
            pltpu.VMEM((part, width), BF16),
        ]

    def first(self, rc):
        self.add_core(rc)
        for y in (0, 1):
            self.send(("x", y), self.held(y).at[:, self.theirs], self.bufs[2].at[y], "x")

    def second(self):
        self.got(("x", 0), ("x", 1))
        for y in (0, 1):
            h = self.held(y)
            self.add(h, self.mine, self.bufs[2].at[y])
            self.over_z(h, ("z", y), lambda i, y=y: self.bufs[3].at[y, i])

    def third(self):
        for y in (0, 1):
            h = self.held(y)
            self.got(("z", y, 1), ("z", y, 2), ("z", y, 3))
            total = h[self.ba, self.mine].astype(F32)
            for i in range(3):
                total = total + self.bufs[3][y, i].astype(F32)
            h[self.ba, self.mine] = total.astype(BF16)
        self.send(("y",), self.held(self.yn).at[self.ba, self.mine], self.bufs[4], "y")

    def fourth(self):
        self.got(("y",))
        total = self.held(self.yy)[self.ba, self.mine].astype(F32) + self.bufs[4][...].astype(F32)
        self.close(total, self.bufs[0], self.bufs[1])


def slab_maps():
    lane = lax.broadcasted_iota(jnp.int32, (128, D), 0)
    column = lax.broadcasted_iota(jnp.int32, (128, D), 1)
    spread = (lax.rem(column, 48) == lane).astype(F32)
    line = lax.broadcasted_iota(jnp.int32, (256, D), 0)
    block = lax.broadcasted_iota(jnp.int32, (256, D), 1) // 48
    device, kind = line // 16, lax.rem(line, 16)
    wanted = jnp.where(kind < 8, device, 4 * lax.rem(device, 4) + kind - 8)
    keep = jnp.where((wanted == block) & (kind < 12), 1.0, 0.0).astype(F32)
    line = lax.broadcasted_iota(jnp.int32, (16, 256), 1)
    out = lax.broadcasted_iota(jnp.int32, (16, 256), 0)
    device, kind = line // 16, lax.rem(line, 16)
    choose = (jnp.where(kind < 8, kind, 8 + device // 4) == out).astype(F32)
    return spread, keep, choose


def norm_parts(value):
    centre = jnp.mean(value, axis=-1, keepdims=True)
    shifted = value - centre
    spread = jnp.mean(shifted * shifted, axis=-1, keepdims=True)
    return shifted, lax.rsqrt(spread + 1e-6)


def mask_columns(split, keys):
    place_ = lax.broadcasted_iota(jnp.int32, (PAD, HEAD_DIM), 0)
    column = lax.broadcasted_iota(jnp.int32, (PAD, HEAD_DIM), 1)
    first = jnp.where(place_ < split, 1.0, 0.0)
    has = jnp.where(column == 0, first, jnp.where(column == 1, 1.0 - first, 0.0))
    if keys:
        allowed = jnp.where(place_ < SLOT, has, 0.0)
        return jnp.where(column < 2, (allowed - 1.0) * BIG, 0.0).astype(BF16)
    return has.astype(BF16)


def shift_in(source, wide):
    wide[0:1056] = source[0:1056].astype(F32)
    wide[1056:ROWS] = jnp.zeros((ROWS - 1056, D), F32)
    wide[1056:1058] = source[1056:1058].astype(F32)


def halves():
    for slot in range(2):
        for part in range(2):
            start = PAD * slot + 272 * part
            yield SLOT * slot + 272 * part, slice(start, start + 272), part


def attend_kernel(
    split, pa, pb, pc, slab, x, dy,
    wa_out, wb0, wc0, wb1, wc1, e_out, xp_out, n1t_out, dyp_out, dyt_out, m_out, att_out, wo_out, lt_out,
    wa, vv, xs, n1, e, xp, n1t, dyp, dyt, m, att, wo, lt, lacc, qmask, kmask, qb,
    send_sem, recv_sem, own_sem, out_sem,
):
    dp, aa, ba, half, core, peers = place()
    greet(peers)
    meet(peers)
    sends = Sends(send_sem, recv_sem, peers)
    where = (aa, ba, half)
    first, second = (slice(None), slice(0, STEP)), (slice(None), slice(STEP, 2 * STEP))
    parts = (
        (pb.at[first], wb0), (pc.at[first], wc0), (pb.at[second], wb1), (pc.at[second], wc1),
    )
    own = [
        pltpu.make_async_copy(part, whole.at[aa, ba], own_sem.at[i])
        for i, (part, whole) in enumerate(((pa, wa), (slab, vv)) + parts)
    ]
    for copy in own:
        copy.start()
    for j in (1, 2, 3):
        sends.start(("v", j), slab, vv.at[aa, ba], f"z{j}")
    a0, a1 = (Gather(f"a{i}", sends, where, pa, wa, 96 * i, 96) for i in (0, 1))
    b0, c0, b1, c1 = (
        Gather(f"b{i}", sends, where, part, whole, 0, GROUP)
        for i, (part, whole) in enumerate(parts)
    )
    outs = []

    def put(source, target):
        copy = pltpu.make_async_copy(source, target, out_sem.at[len(outs)])
        copy.start()
        outs.append(copy)

    a0.first()
    shift_in(dy, xs)
    line = lax.broadcasted_iota(jnp.int32, (272, D), 0)
    total = jnp.zeros((1, D), F32)
    for source, target, part in halves():
        value = xs[source : source + 272]
        if part == 1:
            value = jnp.where(line < SLOT - 272, value, 0.0)
        total = total + jnp.sum(value, axis=0, keepdims=True)
        dyp[target] = value.astype(BF16)
    put(dyp, dyp_out)
    for copy in own:
        copy.wait()
    a0.second()
    a1.first()
    sends.arrived(*[("v", j) for j in (1, 2, 3)])
    sends.start(("v", "y"), vv.at[aa], vv.at[aa], "y")
    sends.start(("v", "c"), vv.at[aa], vv.at[aa], "c")
    shift_in(x, xs)
    for source, target, part in halves():
        xp[target] = xs[source : source + 272].astype(BF16)
    put(xp, xp_out)
    sends.arrived(("v", "y"), ("v", "c"))
    sends.start(("v", "cy"), vv.at[lax.rem(aa + 2, 4)], vv.at[lax.rem(aa + 2, 4)], "c")
    a0.third()
    a1.second()
    dyt[...] = dyp[...].T
    put(dyt, dyt_out)
    sends.arrived(("v", "cy"))
    spread, keep, choose = slab_maps()
    wide = dot(vv[...].reshape(256, 128), spread.astype(BF16))
    e[...] = exact_dot(choose, wide * keep)
    e[12:13] = total
    put(e, e_out)
    gain, offset = e[0:1], e[1:2]
    for source, target, part in halves():
        shifted, rate = norm_parts(xs[source : source + 272])
        n1[target] = (shifted * rate * gain + offset).astype(BF16)
    a0.fourth()
    a1.third()
    b0.first()
    n1t[...] = n1[...].T
    put(n1t, n1t_out)
    for slot in range(2):
        qmask[slot] = mask_columns(split[slot], False)
        kmask[slot] = mask_columns(split[slot], True)
    zero = jnp.zeros((1, GROUP), F32)
    for group in range(4):
        lanes = slice(GROUP * group, GROUP * group + GROUP)
        qb[group] = jnp.concatenate((e[2:3, lanes], zero, e[3:4, lanes]), axis=1)
    lacc[...] = jnp.zeros_like(lacc)
    a1.fourth()
    b0.second()
    c0.first()
    a0.last()
    a1.last()
    put(wa, wa_out)

    def project(group):
        weights = wa[group].reshape(D, D)
        wo[group] = weights[:, 3 * GROUP :]
        for part in range(4):
            rows = slice(272 * part, 272 * part + 272)
            mixed = dot(n1[rows], weights[:, : 3 * GROUP]) + qb[group]
            m[group, rows] = mixed.astype(BF16)

    def look(group, slot):
        rows = slice(PAD * slot, PAD * slot + PAD)
        for head in range(3):
            cols = slice(HEAD_DIM * head, HEAD_DIM * head + HEAD_DIM)
            both = m[group, rows]
            q = both[:, HEAD_DIM * head : HEAD_DIM * (head + 1)] * 0.125
            k = both[:, GROUP + HEAD_DIM * head : GROUP + HEAD_DIM * (head + 1)]
            v = both[:, 2 * GROUP + HEAD_DIM * head : 2 * GROUP + HEAD_DIM * (head + 1)]
            qx = jnp.concatenate((q.astype(BF16), qmask[slot]), axis=1)
            kx = jnp.concatenate((k, kmask[slot]), axis=1)
            scores = dot(qx, kx, NT)
            top = jnp.max(scores, axis=1, keepdims=True)
            terms = jnp.exp(scores - top)
            total = jnp.sum(terms, axis=1, keepdims=True)
            mixed = dot(terms.astype(BF16), v) / total
            att[group, rows, cols] = mixed.astype(BF16)
            lane = lax.broadcasted_iota(jnp.int32, (PAD, 128), 1)
            lacc[slot] = jnp.where(lane == 3 * group + head, top + jnp.log(total), lacc[slot])

    pumps = (
        (b0.third, c0.second, b1.first),
        (),
        (b0.fourth, c0.third, b1.second, c1.first),
        (),
        (b0.last, c0.fourth, b1.third, c1.second),
        (c0.last, b1.fourth, c1.third),
        (b1.last, c1.fourth),
        (),
    )
    for group in range(4):
        project(group)
        put(m.at[group], m_out.at[group])
        for slot in range(2):
            look(group, slot)
            for step in pumps[2 * group + slot]:
                step()
    put(wo, wo_out)
    put(att, att_out)
    row = lax.broadcasted_iota(jnp.int32, (16, 128), 0)
    eye = (row == lax.broadcasted_iota(jnp.int32, (16, 128), 1)).astype(F32)
    for slot in range(2):
        lt[slot] = exact_dot(eye, lacc[slot], NT)
    put(lt, lt_out)
    c1.last()
    sends.finish()
    for copy in outs:
        copy.wait()


def attend(split_at, pa, pb, pc, slab, inputs, cotangent):
    vm = pl.BlockSpec(memory_space=pltpu.VMEM)
    hbm = pl.BlockSpec(memory_space=pl.ANY)
    whole = (4, 4, GROUP, D)
    piece = ((4, 4, GROUP, STEP), BF16)
    shapes = [
        (whole, BF16), piece, piece, piece, piece, ((16, D), F32), ((ROWS, D), BF16),
        ((D, ROWS), BF16), ((ROWS, D), BF16), ((D, ROWS), BF16), ((4, ROWS, 3 * GROUP), BF16),
        ((4, ROWS, GROUP), BF16), ((4, D, GROUP), BF16), ((2, 16, PAD), F32),
    ]
    count = 6 * 26 + 6
    return pl.pallas_call(
        attend_kernel,
        out_shape=tuple(jax.ShapeDtypeStruct(*shape) for shape in shapes),
        in_specs=[pl.BlockSpec(memory_space=pltpu.SMEM)] + [vm] * 6,
        out_specs=[hbm] * len(shapes),
        scratch_shapes=[
            pltpu.VMEM(whole, BF16),
            pltpu.VMEM((4, 4, 16, 128), BF16),
            pltpu.VMEM((ROWS, D), F32),
            pltpu.VMEM((ROWS, D), BF16),
        ]
        + [pltpu.VMEM(*shape) for shape in shapes[5:]]
        + [
            pltpu.VMEM((2, PAD, 128), F32),
            pltpu.VMEM((2, PAD, HEAD_DIM), BF16),
            pltpu.VMEM((2, PAD, HEAD_DIM), BF16),
            pltpu.VMEM((4, 1, 3 * GROUP), F32),
            pltpu.SemaphoreType.DMA((count,)),
            pltpu.SemaphoreType.DMA((count,)),
            pltpu.SemaphoreType.DMA((6,)),
            pltpu.SemaphoreType.DMA((16,)),
        ],
        compiler_params=pltpu.CompilerParams(
            collective_id=0, has_side_effects=True, vmem_limit_bytes=58 * MIB
        ),
    )(split_at, pa, pb, pc, slab, inputs, cotangent)


def gelu_parts(hidden):
    size = jnp.abs(hidden)
    t = 1.0 / (1.0 + 0.3 * size)
    bell = jnp.exp(hidden * hidden * -0.5)
    poly = jnp.full_like(t, TAIL[-1])
    for factor in TAIL[-2::-1]:
        poly = poly * t + factor
    tail = poly * t * bell
    phi = jnp.where(hidden < 0, tail, 1.0 - tail)
    return hidden * phi, phi + hidden * bell * (1.0 / math.sqrt(2 * math.pi))


def feed_kernel(
    e, pb, pc, xp_in, dyp_in, dyt_in, att_in, wo_in, wb0, wc0, wb1, wc1,
    out, gvec, ob, oc, gm_out, gatt_out, gwo_out, gb1, gc1, gb2, gc2,
    xp, dyp, dyt, att, wo, w, middle, acc, back, n2, n2t, act, gh, rcb, rcc, *more,
):
    bufs, (send_sem, recv_sem, send_two, recv_two, in_sem, out_sem, own_sem) = more[:-7], more[-7:]
    dp, aa, ba, half, core, peers = place()
    loads = {}
    for name, source, target in (
        ("xp", xp_in, xp), ("att", att_in, att), ("wo", wo_in, wo), ("dyp", dyp_in, dyp),
        ("wb0", wb0, w.at[0, 0]), ("wc0", wc0, w.at[1, 0]), ("dyt", dyt_in, dyt),
        ("wb1", wb1, w.at[0, 1]), ("wc1", wc1, w.at[1, 1]),
    ):
        loads[name] = pltpu.make_async_copy(source, target, in_sem.at[len(loads)])
        loads[name].start()
    third = (slice(None), slice(2 * STEP, 3 * STEP))
    parts = [part.at[third] for part in (pb, pc)]
    own = [
        pltpu.make_async_copy(part, w.at[i, 2, aa, ba], own_sem.at[i])
        for i, part in enumerate(parts)
    ]
    for copy in own:
        copy.start()
    greet(peers)
    where = (aa, ba, half)
    takes = Sends(send_sem, recv_sem, peers)
    gives = Sends(send_two, recv_two, peers)
    tb, tc = (Gather(f"t{i}", takes, where, parts[i], w.at[i, 2], 0, GROUP) for i in (0, 1))
    made = []
    for i, o in enumerate((ob, oc)):
        held = lambda y, i=i: w.at[i, 0, 2 * y + core]
        for kind, row, count in ((SumY, 0, 64), (SumX, 64, 128)):
            at = 5 * len(made)
            made.append(kind(f"s{len(made)}", gives, where, held, o, row, count, bufs[at : at + 5]))
    by, bx, cy, cx = made
    outs = []

    def put(source, target):
        copy = pltpu.make_async_copy(source, target, out_sem.at[len(outs)])
        copy.start()
        outs.append(copy)

    for name in ("xp", "att", "wo"):
        loads[name].wait()
    gvec[...] = jnp.zeros_like(gvec)
    gvec[7:8] = e[12:13]
    for part in range(4):
        rows = slice(272 * part, 272 * part + 272)
        value = xp[rows].astype(F32) + e[4:5]
        for group in range(4):
            value = value + dot(att[group, rows], wo[group], NT)
        middle[rows] = value
        shifted, rate = norm_parts(value)
        n2[rows] = (shifted * rate * e[5:6] + e[6:7]).astype(BF16)
        acc[rows] = value + e[7:8]
        back[rows] = jnp.zeros((272, D), F32)
        if part == 0:
            meet(peers)
            tb.first()
            tc.first()
    for copy in own:
        copy.wait()
    n2t[...] = n2[...].T
    for name in ("dyp", "wb0", "wc0", "dyt"):
        loads[name].wait()

    def whole_unit(u):
        step, pair, now = min(u, 5) // 2, u % 2, u % 2
        both = ((2 * now, 2 * pair), (2 * now + 1, 2 * pair + 1))
        columns = slice(STEP * step, STEP * step + STEP)

        def weight(kind, group):
            return w[kind, step, group].reshape(D, STEP)

        def up(part):
            rows = slice(272 * part, 272 * part + 272)
            return [
                (
                    dot(n2[rows], weight(0, group)) + e[8 + group : 9 + group, columns],
                    dot(dyp[rows], weight(1, group)),
                )
                for _, group in both
            ]

        def across(part, made, totals):
            rows = slice(272 * part, 272 * part + 272)
            new = []
            for (at, _), (hidden, grad), total in zip(both, made, totals):
                forward, slope = gelu_parts(hidden)
                grad = (grad * slope).astype(BF16)
                act[at, rows] = forward.astype(BF16)
                gh[at, rows] = grad
                new.append(total + jnp.sum(grad.astype(F32), axis=0, keepdims=True))
            return new

        def down(part):
            rows = slice(272 * part, 272 * part + 272)
            for total, values, kind in ((acc, act, 1), (back, gh, 0)):
                more = [dot(values[at, rows], weight(kind, group), NT) for at, group in both]
                total[rows] = total[rows] + more[0] + more[1]

        if u < 6:
            totals = [jnp.zeros((1, STEP), F32)] * 2
            made = up(0)
            for part in range(4):
                ahead = up(part + 1) if part < 3 else None
                totals = across(part, made, totals)
                if part:
                    down(part - 1)
                made = ahead
            down(3)
            for (_, group), total in zip(both, totals):
                gvec[8 + group : 9 + group, columns] = total
        if u > 0:
            step, pair, before = (u - 1) // 2, (u - 1) % 2, (u - 1) % 2
            for i, (turned, values) in enumerate(((n2t, gh), (dyt, act))):
                for j in range(2):
                    grad = dot(turned[...], values[2 * before + j]).astype(BF16)
                    w[i, step, 2 * pair + j] = grad.reshape(4, GROUP, STEP)

    once = 1 + jnp.minimum(dp, 0)

    def unit(u):
        def inside(_, carry):
            whole_unit(u)
            return carry

        lax.fori_loop(0, once, inside, 0)

    tb.second()
    tc.second()
    unit(0)
    tb.third()
    tc.third()
    unit(1)
    tb.fourth()
    tc.fourth()
    for name in ("wb1", "wc1"):
        loads[name].wait()
    unit(2)
    tb.last()
    tc.last()
    for i, rc in enumerate((rcb, rcc)):
        for y in (0, 1):
            gives.start((i, y), w.at[i, 0, 2 * y + 1 - core], rc.at[y], "c")
    unit(3)
    takes.finish()
    gives.arrived((0, 0), (0, 1))
    by.first(rcb)
    bx.first(rcb)
    gives.arrived((1, 0), (1, 1))
    cy.first(rcc)
    cx.first(rcc)
    unit(4)
    put(w.at[0, 1], gb1)
    put(w.at[1, 1], gc1)
    for batch in made:
        batch.second()
    unit(5)
    for batch in made:
        batch.third()
    line = lax.broadcasted_iota(jnp.int32, (16, D), 0)
    out[0:528] = acc[0:528].astype(BF16)
    out[528:544] = jnp.where(line == 0, acc[528:544], acc[543:559]).astype(BF16)
    out[544:1056] = acc[559:1071].astype(BF16)
    out[1056:1058] = acc[1071:1073].astype(BF16)
    unit(6)
    put(w.at[0, 2], gb2)
    put(w.at[1, 2], gc2)
    sums = [jnp.zeros((1, D), F32)] * 3
    for part in range(4):
        rows = slice(272 * part, 272 * part + 272)
        shifted, rate = norm_parts(middle[rows])
        hat = shifted * rate
        grad = back[rows]
        inner = grad * e[5:6]
        mean = jnp.mean(inner, axis=-1, keepdims=True)
        along = jnp.mean(inner * hat, axis=-1, keepdims=True)
        total = dyp[rows].astype(F32) + rate * (inner - mean - hat * along)
        middle[rows] = total
        branch = total.astype(BF16)
        n2[rows] = branch
        for i, value in enumerate((grad * hat, grad, branch.astype(F32))):
            sums[i] = sums[i] + jnp.sum(value, axis=0, keepdims=True)
        for group in range(4):
            act[group, rows, 0:GROUP] = dot(branch, wo[group]).astype(BF16)
        if part == 1:
            for batch in made:
                batch.fourth()
    put(middle, gm_out)
    put(act, gatt_out)
    gvec[5:6] = sums[0]
    gvec[6:7] = sums[1]
    gvec[4:5] = sums[2]
    n2t[...] = n2[...].T
    for group in range(4):
        gh[group, 0:D, 0:GROUP] = dot(n2t[...], att[group]).astype(BF16)
    put(gh.at[:, 0:D], gwo_out)
    for batch in made:
        batch.last()
    gives.finish()
    for copy in outs:
        copy.wait()


def feed(e, pb, pc, xp, dyp, dyt, att, wo, wb0, wc0, wb1, wc1, local):
    vm = pl.BlockSpec(memory_space=pltpu.VMEM)
    hbm = pl.BlockSpec(memory_space=pl.ANY)
    piece = jax.ShapeDtypeStruct((4, 4, GROUP, STEP), BF16)
    own = jax.ShapeDtypeStruct((GROUP, STEP), F32)
    sums = SumY.scratch(64, STEP) + SumX.scratch(128, STEP)
    gives = 4 + 2 * (6 + 10)
    return pl.pallas_call(
        feed_kernel,
        out_shape=(
            jax.ShapeDtypeStruct((local, D), BF16),
            jax.ShapeDtypeStruct((16, D), F32),
            own,
            own,
            jax.ShapeDtypeStruct((ROWS, D), F32),
            jax.ShapeDtypeStruct((4, ROWS, STEP), BF16),
            jax.ShapeDtypeStruct((4, D, STEP), BF16),
            piece,
            piece,
            piece,
            piece,
        ),
        in_specs=[vm] * 3 + [hbm] * 9,
        out_specs=[vm] * 4 + [hbm] * 7,
        scratch_shapes=[
            pltpu.VMEM((ROWS, D), BF16),
            pltpu.VMEM((ROWS, D), BF16),
            pltpu.VMEM((D, ROWS), BF16),
            pltpu.VMEM((4, ROWS, GROUP), BF16),
            pltpu.VMEM((4, D, GROUP), BF16),
            pltpu.VMEM((2, 3, 4, 4, GROUP, STEP), BF16),
            pltpu.VMEM((ROWS, D), F32),
            pltpu.VMEM((ROWS, D), F32),
            pltpu.VMEM((ROWS, D), F32),
            pltpu.VMEM((ROWS, D), BF16),
            pltpu.VMEM((D, ROWS), BF16),
            pltpu.VMEM((4, ROWS, STEP), BF16),
            pltpu.VMEM((4, ROWS, STEP), BF16),
            pltpu.VMEM((2, 4, GROUP, STEP), BF16),
            pltpu.VMEM((2, 4, GROUP, STEP), BF16),
        ]
        + sums * 2
        + [
            pltpu.SemaphoreType.DMA((52,)),
            pltpu.SemaphoreType.DMA((52,)),
            pltpu.SemaphoreType.DMA((gives,)),
            pltpu.SemaphoreType.DMA((gives,)),
            pltpu.SemaphoreType.DMA((9,)),
            pltpu.SemaphoreType.DMA((7,)),
            pltpu.SemaphoreType.DMA((2,)),
        ],
        compiler_params=pltpu.CompilerParams(
            collective_id=2, has_side_effects=True, vmem_limit_bytes=60 * MIB
        ),
    )(e, pb, pc, xp, dyp, dyt, att, wo, wb0, wc0, wb1, wc1)


def unattend_kernel(
    split, e, lt, gvec, ob0, oc0, xp_in, n1t_in, m_in, gatt_in, wa_in, gm_in, gwo_in, gb1, gc1, gb2, gc2,
    gin, oa, ob, oc, ov,
    xp, n1t, m, gatt, ga, gm, gwo, h, rc, rca, rya, gmix, back, sums, gv, qmask, kmask,
    vh, vc, vy, vz, vx, *more,
):
    bufs, (send_sem, recv_sem, own_sem, in_sem) = more[:-4], more[-4:]
    dp, aa, ba, half, core, peers = place()
    greet(peers)
    yy = aa // 2
    order = [2 * (1 - yy) + 1 - core, 2 * (1 - yy) + core, 2 * yy + 1 - core, 2 * yy + core]
    loads = {}

    def load(name, source, target):
        loads[name] = pltpu.make_async_copy(source, target, in_sem.at[len(loads)])
        loads[name].start()

    for k in range(4):
        load(("m", k), m_in.at[order[k]], m.at[order[k]])
        load(("gatt", k), gatt_in.at[order[k]], gatt.at[order[k]])
        if k == 0:
            load("n1t", n1t_in, n1t)
            load("wa", wa_in, ga)
            load("gwo", gwo_in, gwo)
    load("xp", xp_in, xp)
    load("gm", gm_in, gm)
    own = []
    given = (gb1, gc1, gb2, gc2)
    for i, g in enumerate(given):
        for y in (0, 1):
            own.append(pltpu.make_async_copy(g.at[2 * y + core], h.at[i, y], own_sem.at[len(own)]))
            own[-1].start()
    sends = Sends(send_sem, recv_sem, peers)
    where = (aa, ba, half)
    made = []
    for i, o in enumerate((ob, oc, ob, oc)):
        o = o.at[:, STEP * (1 + i // 2) : STEP * (2 + i // 2)]
        held = lambda y, i=i: h.at[i, y]
        for kind, row, count in ((SumY, 0, 64), (SumX, 64, 128)):
            at = 5 * len(made)
            made.append(kind(f"s{len(made)}", sends, where, held, o, row, count, bufs[at : at + 5]))
            made[-1].open = functools.partial(made[-1].first, rc.at[i])
    for i in range(3):
        at = 5 * len(made)
        held = lambda y: ga.at[2 * y + core]
        made.append(SumY(f"a{i}", sends, where, held, oa, 64 * i, 64, bufs[at : at + 5]))
    by1, bx1, cy1, cx1, by2, bx2, cy2, cx2, a0, a1, a2 = made
    for slot in range(2):
        qmask[slot] = mask_columns(split[slot], False)
        kmask[slot] = mask_columns(split[slot], True)
    back[...] = jnp.zeros_like(back)

    def look(group, slot):
        rows = slice(PAD * slot, PAD * slot + PAD)
        for head in range(3):
            both = m[group, rows]
            q = (both[:, HEAD_DIM * head : HEAD_DIM * (head + 1)] * 0.125).astype(BF16)
            k = both[:, GROUP + HEAD_DIM * head : GROUP + HEAD_DIM * (head + 1)]
            v = both[:, 2 * GROUP + HEAD_DIM * head : 2 * GROUP + HEAD_DIM * (head + 1)]
            go = gatt[group, rows][:, HEAD_DIM * head : HEAD_DIM * (head + 1)]
            qx = jnp.concatenate((q, qmask[slot]), axis=1)
            kx = jnp.concatenate((k, kmask[slot]), axis=1)
            scores = dot(kx, qx, NT)
            probs = jnp.exp(scores - lt[slot, pl.ds(3 * group + head, 1)])
            gprobs = dot(v, go, NT)
            both_ = probs * gprobs
            delta = jnp.sum(both_, axis=0, keepdims=True)
            gs = (both_ - probs * delta).astype(BF16)
            gq = dot(gs, k, TN) * 0.125
            gk = dot(gs, q)
            gval = dot(probs.astype(BF16), go)
            for i, value in enumerate((gq, gk, gval)):
                at = GROUP * i + HEAD_DIM * head
                gmix[rows, at : at + HEAD_DIM] = value.astype(BF16)

    def grads(k):
        group = order[k]
        grad = dot(n1t[...], gmix[...]).reshape(4, GROUP, 3 * GROUP)
        rest = gwo[group][:, 0:GROUP].reshape(4, GROUP, GROUP)
        if k in (1, 3):
            rest = rest.astype(F32)
            sends.arrived(("a", k - 1))
            terms = [rca.at[k // 2]]
            if k == 3:
                sends.arrived(("a", 1))
                terms.append(rya)
            for term in terms:
                grad = grad + term[:, :, 0 : 3 * GROUP].astype(F32)
                rest = rest + term[:, :, 3 * GROUP :].astype(F32)
        given = ga.at[group]
        given[:, :, 0 : 3 * GROUP] = grad.astype(BF16)
        given[:, :, 3 * GROUP :] = rest.astype(BF16)

    def fold(group):
        weights = ga[group].reshape(D, D)[:, : 3 * GROUP]
        total = jnp.zeros((1, 3 * GROUP), F32)
        for part in range(4):
            rows = slice(272 * part, 272 * part + 272)
            total = total + jnp.sum(gmix[rows].astype(F32), axis=0, keepdims=True)
            back[rows] = back[rows] + dot(gmix[rows], weights, NT)
        sums[group] = total

    def store(k):
        group = order[k]
        fold(group)
        grads(k)
        if k == 1:
            sends.start(("a", 1), ga.at[group], rya, "y")
        elif k < 3:
            sends.start(("a", k), ga.at[group], rca.at[k // 2], "c")

    def begin():
        meet(peers)
        for i, g in enumerate(given):
            for y in (0, 1):
                sends.start((i, y), g.at[2 * y + 1 - core], rc.at[i, y], "c")

    def settle():
        ob[:, 0:STEP] = ob0[...]
        oc[:, 0:STEP] = oc0[...]
        for copy in own:
            copy.wait()
        for i in range(4):
            sends.arrived((i, 0), (i, 1))
        for name in ("n1t", "wa", "gwo"):
            loads[name].wait()

    pumps = (
        (begin,),
        (settle, by1.open, cy1.open, bx1.open),
        (cx1.open, by2.open, cy2.open),
        (by1.second, cy1.second, bx1.second),
        (cx1.second, bx2.open, by2.second, cy2.second),
        (by1.third, cy1.third, bx1.third, cx2.open),
        (cx1.third, by2.third, cy2.third, bx2.second),
        (by1.fourth, cy1.fourth, bx1.fourth, cx2.second),
    )
    for k in range(4):
        loads[("m", k)].wait()
        loads[("gatt", k)].wait()
        for slot in range(2):
            look(order[k], slot)
            for step in pumps[2 * k + slot]:
                step()
        store(k)
    for batch in (a0, a1, a2):
        mine = batch.held(yy)
        batch.start_x = functools.partial(batch.send, ("x",), mine.at[:, batch.theirs], batch.bufs[3], "x")
    a0.start_x()
    for step in (cx1.fourth, by2.fourth, cy2.fourth, bx2.third, cx2.third):
        step()
    loads["xp"].wait()
    loads["gm"].wait()
    tot_gain, tot_bias = jnp.zeros((1, D), F32), jnp.zeros((1, D), F32)
    for part in range(4):
        rows = slice(272 * part, 272 * part + 272)
        shifted, rate = norm_parts(xp[rows].astype(F32))
        hat = shifted * rate
        grad = back[rows]
        inner = grad * e[0:1]
        mean = jnp.mean(inner, axis=-1, keepdims=True)
        along = jnp.mean(inner * hat, axis=-1, keepdims=True)
        tot_gain = tot_gain + jnp.sum(grad * hat, axis=0, keepdims=True)
        tot_bias = tot_bias + jnp.sum(grad, axis=0, keepdims=True)
        back[rows] = gm[rows] + rate * (inner - mean - hat * along)
        if part == 2:
            a0.third()
            a1.start_x()
    line = lax.broadcasted_iota(jnp.int32, (16, D), 0)
    q_row = jnp.concatenate([sums[i][:, :GROUP] for i in range(4)], axis=1)
    v_row = jnp.concatenate([sums[i][:, 2 * GROUP :] for i in range(4)], axis=1)
    rows = jnp.where(line == 0, tot_gain, jnp.where(line == 1, tot_bias, gvec[...]))
    rows = jnp.where(line == 2, q_row, jnp.where(line == 3, v_row, rows))
    spread, keep, choose = slab_maps()
    wide = exact_dot(choose, rows, TN) * keep
    gv[...] = exact_dot(wide, spread, NT).reshape(4, 4, 16, 128)
    for y in (0, 1):
        sends.start(("v", "c", y), gv.at[2 * y + 1 - core], vc.at[y], "c")
    a1.third()
    a2.start_x()
    for y in (0, 1):
        sends.arrived(("v", "c", y))
        vh[y] = gv[2 * y + core] + vc[y]
    sends.start(("v", "y"), vh.at[1 - yy], vy, "y")
    gin[0:528] = back[0:528].astype(BF16)
    gin[528:544] = jnp.where(line == 0, back[528:544], back[543:559]).astype(BF16)
    gin[544:1056] = back[559:1071].astype(BF16)
    gin[1056:1058] = back[1071:1073].astype(BF16)
    a0.fourth()
    bx2.fourth()
    cx2.fourth()
    sends.arrived(("v", "y"))
    vh[yy] = vh[yy] + vy[...]
    for j in (1, 2, 3):
        sends.start(("v", "z", j), vh.at[yy, lax.rem(ba + j, 4)], vz.at[j - 1], f"z{j}")
    for batch in made[:8]:
        batch.last()
    a2.third()
    a1.fourth()
    sends.arrived(*[("v", "z", j) for j in (1, 2, 3)])
    vh[yy, ba] = vh[yy, ba] + (vz[0] + vz[1] + vz[2])
    sends.start(("v", "x"), vh.at[yy, ba], vx, "x")
    a2.fourth()
    sends.arrived(("v", "x"))
    ov[...] = vh[yy, ba] + vx[...]
    a0.last()
    a1.last()
    a2.last()
    sends.finish()


def unattend(split_at, e, lt, gvec, ob0, oc0, *stored, local):
    vm = pl.BlockSpec(memory_space=pltpu.VMEM)
    hbm = pl.BlockSpec(memory_space=pl.ANY)
    out = jax.ShapeDtypeStruct((GROUP, D), F32)
    count = 8 + 4 * 16 + 3 + 3 * 5 + 7
    return pl.pallas_call(
        unattend_kernel,
        out_shape=(
            jax.ShapeDtypeStruct((local, D), BF16), out, out, out,
            jax.ShapeDtypeStruct((16, 128), F32),
        ),
        in_specs=[pl.BlockSpec(memory_space=pltpu.SMEM)] + [vm] * 5 + [hbm] * 11,
        out_specs=[vm] * 5,
        scratch_shapes=[
            pltpu.VMEM((ROWS, D), BF16),
            pltpu.VMEM((D, ROWS), BF16),
            pltpu.VMEM((4, ROWS, 3 * GROUP), BF16),
            pltpu.VMEM((4, ROWS, STEP), BF16),
            pltpu.VMEM((4, 4, GROUP, D), BF16),
            pltpu.VMEM((ROWS, D), F32),
            pltpu.VMEM((4, D, STEP), BF16),
            pltpu.VMEM((4, 2, 4, GROUP, STEP), BF16),
            pltpu.VMEM((4, 2, 4, GROUP, STEP), BF16),
            pltpu.VMEM((2, 4, GROUP, D), BF16),
            pltpu.VMEM((4, GROUP, D), BF16),
            pltpu.VMEM((ROWS, 3 * GROUP), BF16),
            pltpu.VMEM((ROWS, D), F32),
            pltpu.VMEM((4, 1, 3 * GROUP), F32),
            pltpu.VMEM((4, 4, 16, 128), F32),
            pltpu.VMEM((2, PAD, HEAD_DIM), BF16),
            pltpu.VMEM((2, PAD, HEAD_DIM), BF16),
            pltpu.VMEM((2, 4, 16, 128), F32),
            pltpu.VMEM((2, 4, 16, 128), F32),
            pltpu.VMEM((4, 16, 128), F32),
            pltpu.VMEM((3, 16, 128), F32),
            pltpu.VMEM((16, 128), F32),
        ]
        + (SumY.scratch(64, STEP) + SumX.scratch(128, STEP)) * 4
        + SumY.scratch(64, D) * 3
        + [
            pltpu.SemaphoreType.DMA((count,)),
            pltpu.SemaphoreType.DMA((count,)),
            pltpu.SemaphoreType.DMA((8,)),
            pltpu.SemaphoreType.DMA((13,)),
        ],
        compiler_params=pltpu.CompilerParams(
            collective_id=1, has_side_effects=True, vmem_limit_bytes=62 * MIB
        ),
    )(split_at, e, lt, gvec, ob0, oc0, *stored)


def results_kernel(output, gin, oa, ob, oc, ov, out, gin_out, qkv, wo, up, down, up_bias, *rows):
    out[...] = output[...]
    gin_out[...] = gin[...]
    for kind in range(3):
        qkv[kind] = oa[:, GROUP * kind : GROUP * kind + GROUP]
    wo[...] = oa[:, 3 * GROUP :].T
    up[...] = ob[...]
    down[...] = oc[...]
    up_bias[...] = jnp.concatenate([ov[i : i + 1, :48] for i in range(8, 12)], axis=1)[0]
    for i, row in enumerate(rows):
        row[...] = ov[i, :48]


def results(output, gin, oa, ob, oc, ov):
    shapes = [(3, GROUP, GROUP), (GROUP, GROUP), (GROUP, D), (GROUP, D), (GROUP,)] + [(48,)] * 8
    return pl.pallas_call(
        results_kernel,
        out_shape=[jax.ShapeDtypeStruct(gin.shape, BF16)] * 2
        + [jax.ShapeDtypeStruct(shape, F32) for shape in shapes],
        compiler_params=pltpu.CompilerParams(vmem_limit_bytes=60 * MIB),
    )(output, gin, oa, ob, oc, ov)


def on_device(
    inputs, cotangent, split_at, ln1_gain, ln1_bias, w_qkv, q_bias, v_bias, w_out, o_bias,
    ln2_gain, ln2_bias, w_up, up_bias, w_down, down_bias,
):
    pa = jnp.concatenate((w_qkv.reshape(GROUP, 3 * GROUP), w_out.T), axis=1)
    vectors = jnp.stack(
        (ln1_gain, ln1_bias, q_bias, v_bias, o_bias, ln2_gain, ln2_bias, down_bias)
        + tuple(up_bias[48 * i : 48 * i + 48] for i in range(4))
    )
    slab = jnp.pad(vectors, ((0, 4), (0, 80)))
    pc = w_down.T
    local = inputs.shape[0]
    wa, *pieces, e, xp, n1t, dyp, dyt, m, att, wo, lt = attend(
        split_at, pa, w_up, pc, slab, inputs, cotangent
    )
    output, gvec, ob0, oc0, gm, gatt, gwo, *grads = feed(
        e, w_up, pc, xp, dyp, dyt, att, wo, *pieces, local
    )
    gin, oa, ob, oc, ov = unattend(
        split_at, e, lt, gvec, ob0, oc0, xp, n1t, m, gatt, wa, gm, gwo, *grads, local=local
    )
    if lax.axis_size("dp") > 2:
        oa, ob, oc, ov = (lax.psum(v, "dp") * 0.5 for v in (oa, ob, oc, ov))
    output, gin, qkv, wo, up, down, up_row, *rows = results(output, gin, oa, ob, oc, ov)
    return (
        output,
        gin,
        rows[0],
        rows[1],
        qkv.transpose(1, 0, 2),
        rows[2],
        rows[3],
        wo,
        rows[4],
        rows[5],
        rows[6],
        up,
        up_row,
        down.T,
        rows[7],
    )


def solution(mesh):
    rows = P(("dp", "aa", "ba"), None)
    vec = P(("aa", "ba"))
    grid_qkv, first, second = P("ba", None, "aa"), P("aa", "ba"), P("ba", "aa")
    params = (vec, vec, grid_qkv, vec, vec, first, vec, vec, vec, second, vec, first, vec)
    return jax.shard_map(
        on_device,
        mesh=mesh,
        in_specs=(rows, rows, P(("dp", "aa", "ba"))) + params,
        out_specs=(rows, rows) + params,
        check_vma=False,
    )
```

```python
import functools
import math

import jax
import jax.numpy as jnp
from jax import lax
from jax.experimental import pallas as pl
from jax.experimental.pallas import tpu as pltpu
from jax.sharding import PartitionSpec as P

D = 768
HEADS = 12
HEAD_DIM = 64
SLOT = 529
PAD = 544
ROWS = 2 * PAD
STEP = 256
WIDE = 640
GROUP = 192
BIG = 1e30
MESH = pl.DeviceIdType.MESH
F32 = jnp.float32
BF16 = jnp.bfloat16
MIB = 1 << 20

NT = (((1,), (1,)), ((), ()))
NN = (((1,), (0,)), ((), ()))
TN = (((0,), (0,)), ((), ()))

TAIL = (
    0.11962926248861097,
    0.12075451364069298,
    0.09991001218129214,
    0.12857310923328652,
    -0.0537053561953165,
    0.20637712218096793,
    -0.15721681637037743,
    0.03567808025645831,
)


def dot(left, right, dims=NN):
    return lax.dot_general(left, right, dims, preferred_element_type=F32)


def exact_dot(left, right, dims=NN):
    return lax.dot_general(
        left, right, dims, preferred_element_type=F32, precision=lax.Precision.HIGHEST
    )


def place():
    dp, aa, ba = lax.axis_index("dp"), lax.axis_index("aa"), lax.axis_index("ba")
    half, core = lax.rem(dp, 2), lax.rem(aa, 2)
    peers = {
        "x": (dp + 1 - 2 * half, aa, ba),
        "y": (dp, lax.rem(aa + 2, 4), ba),
        "c": (dp, aa + 1 - 2 * core, ba),
        "z1": (dp, aa, lax.rem(ba + 1, 4)),
        "z2": (dp, aa, lax.rem(ba + 2, 4)),
        "z3": (dp, aa, lax.rem(ba + 3, 4)),
    }
    return dp, aa, ba, half, core, peers


def greet(peers):
    barrier = pltpu.get_barrier_semaphore()
    for peer in peers.values():
        pl.semaphore_signal(barrier, inc=1, device_id=peer, device_id_type=MESH)


def meet(peers):
    pl.semaphore_wait(pltpu.get_barrier_semaphore(), len(peers))


class Sends:
    def __init__(self, send_sem, recv_sem, peers):
        self.send_sem, self.recv_sem, self.peers = send_sem, recv_sem, peers
        self.made = {}

    def start(self, name, src, dst, peer):
        at = len(self.made)
        copy = pltpu.make_async_remote_copy(
            src_ref=src,
            dst_ref=dst,
            send_sem=self.send_sem.at[at],
            recv_sem=self.recv_sem.at[at],
            device_id=self.peers[peer],
            device_id_type=MESH,
        )
        copy.start()
        self.made[name] = copy

    def arrived(self, *names):
        for name in names:
            self.made[name].wait_recv()

    def finish(self):
        for copy in self.made.values():
            copy.wait_send()


def sixteen(value):
    return pl.multiple_of(value, 16)


class Gather:
    def __init__(self, name, sends, where, part, whole, row, count):
        self.name, self.sends, self.part, self.whole = name, sends, part, whole
        self.aa, self.ba, self.half = where
        self.ay = lax.rem(self.aa + 2, 4)
        self.other = [(j, lax.rem(self.ba + j, 4)) for j in (1, 2, 3)]
        big, small = count // 3, count // 6
        self.big = pl.ds(sixteen(row + big * self.half), big)
        self.big_not = pl.ds(sixteen(row + big - big * self.half), big)
        self.small = pl.ds(sixteen(row + 2 * big + small * self.half), small)
        self.rest = pl.ds(row + 2 * big, big)

    def send(self, key, src, dst, peer):
        self.sends.start((self.name,) + key, src, dst, peer)

    def move(self, key, at, peer):
        self.send(key, self.whole.at[at], self.whole.at[at], peer)

    def got(self, *keys):
        self.sends.arrived(*[(self.name,) + key for key in keys])

    def first(self):
        w, aa, ba = self.whole, self.aa, self.ba
        for j in (1, 2, 3):
            self.send(("z", j), self.part.at[self.big], w.at[aa, ba, self.big], f"z{j}")
        self.send(("y",), self.part.at[self.small], w.at[aa, ba, self.small], "y")
        for j in (1, 2, 3):
            self.send(("zs", j), self.part.at[self.small], w.at[aa, ba, self.small], f"z{j}")

    def second(self):
        self.got(("z", 1), ("z", 2), ("z", 3))
        for j, z in self.other:
            self.move(("x", j), (self.aa, z, self.big), "x")
        self.move(("yb",), (self.aa, slice(None), self.big), "y")
        self.got(("y",))
        for j in (1, 2, 3):
            self.move(("zy", j), (self.ay, self.ba, self.small), f"z{j}")
        self.got(("zs", 1), ("zs", 2), ("zs", 3))
        for j, z in self.other:
            self.move(("xs", j), (self.aa, z, self.small), "x")
        self.move(("c0",), (self.aa, slice(None), self.big), "c")

    def third(self):
        every = slice(None)
        self.got(("x", 1), ("x", 2), ("x", 3))
        self.move(("yn",), (self.aa, every, self.big_not), "y")
        self.got(("zy", 1), ("zy", 2), ("zy", 3))
        self.move(("xy",), (self.ay, every, self.small), "x")
        self.got(("yb",))
        self.move(("c1",), (self.aa, every, self.big_not), "c")
        self.move(("c2",), (self.ay, every, self.big), "c")

    def fourth(self):
        every = slice(None)
        self.got(("xs", 1), ("xs", 2), ("xs", 3))
        self.move(("c3",), (self.aa, every, self.rest), "c")
        self.got(("yn",))
        self.move(("c4",), (self.ay, every, self.big_not), "c")
        self.got(("xy",))
        self.move(("c5",), (self.ay, every, self.rest), "c")

    def last(self):
        self.got(*[(f"c{i}",) for i in range(6)])


class Sum:
    def __init__(self, name, sends, where, held, out, row, count, bufs):
        self.name, self.sends, self.held, self.out, self.bufs = name, sends, held, out, bufs
        part = count // 2
        self.aa, self.ba, self.half = where
        self.yy = self.aa // 2
        self.yn = 1 - self.yy
        self.other = [(j, lax.rem(self.ba + j, 4)) for j in (1, 2, 3)]
        self.rows = pl.ds(row, count)
        self.mine = pl.ds(sixteen(row + part * self.half), part)
        self.theirs = pl.ds(sixteen(row + part - part * self.half), part)

    def send(self, key, src, dst, peer):
        self.sends.start((self.name,) + key, src, dst, peer)

    def got(self, *keys):
        self.sends.arrived(*[(self.name,) + key for key in keys])

    def add(self, h, rows, more):
        @pl.loop(0, 4)
        def _(z):
            h[z, rows] = (h[z, rows].astype(F32) + more[z].astype(F32)).astype(BF16)

    def add_core(self, rc):
        for y in (0, 1):
            self.add(self.held(y), self.rows, rc.at[y, :, self.rows])

    def over_z(self, h, key, at):
        for j, z in self.other:
            self.send(key + (j,), h.at[z, self.mine], at(j - 1), f"z{j}")

    def close(self, total, own, far):
        own[...] = total.astype(BF16)
        self.send(("f",), own, far, "x")

    def last(self):
        own, far = self.bufs[:2]
        self.out[self.mine] = own[...].astype(F32)
        self.got(("f",))
        self.out[self.theirs] = far[...].astype(F32)


class SumY(Sum):
    @staticmethod
    def scratch(count, width):
        part = count // 2
        return [
            pltpu.VMEM((part, width), BF16),
            pltpu.VMEM((part, width), BF16),
            pltpu.VMEM((4, count, width), BF16),
            pltpu.VMEM((4, part, width), BF16),
            pltpu.VMEM((3, part, width), BF16),
        ]

    def first(self, rc):
        self.add_core(rc)
        self.send(("y",), self.held(self.yn).at[:, self.rows], self.bufs[2], "y")

    def second(self):
        self.got(("y",))
        h = self.held(self.yy)
        self.add(h, self.rows, self.bufs[2])
        self.send(("x",), h.at[:, self.theirs], self.bufs[3], "x")

    def third(self):
        self.got(("x",))
        h = self.held(self.yy)
        self.add(h, self.mine, self.bufs[3])
        self.over_z(h, ("z",), lambda i: self.bufs[4].at[i])

    def fourth(self):
        self.got(("z", 1), ("z", 2), ("z", 3))
        total = self.held(self.yy)[self.ba, self.mine].astype(F32)
        for i in range(3):
            total = total + self.bufs[4][i].astype(F32)
        self.close(total, self.bufs[0], self.bufs[1])


class SumX(Sum):
    @staticmethod
    def scratch(count, width):
        part = count // 2
        return [
            pltpu.VMEM((part, width), BF16),
            pltpu.VMEM((part, width), BF16),
            pltpu.VMEM((2, 4, part, width), BF16),
            pltpu.VMEM((2, 3, part, width), BF16),
            pltpu.VMEM((part, width), BF16),
        ]

    def first(self, rc):
        self.add_core(rc)
        for y in (0, 1):
            self.send(("x", y), self.held(y).at[:, self.theirs], self.bufs[2].at[y], "x")

    def second(self):
        self.got(("x", 0), ("x", 1))
        for y in (0, 1):
            h = self.held(y)
            self.add(h, self.mine, self.bufs[2].at[y])
            self.over_z(h, ("z", y), lambda i, y=y: self.bufs[3].at[y, i])

    def third(self):
        for y in (0, 1):
            h = self.held(y)
            self.got(("z", y, 1), ("z", y, 2), ("z", y, 3))
            total = h[self.ba, self.mine].astype(F32)
            for i in range(3):
                total = total + self.bufs[3][y, i].astype(F32)
            h[self.ba, self.mine] = total.astype(BF16)
        self.send(("y",), self.held(self.yn).at[self.ba, self.mine], self.bufs[4], "y")

    def fourth(self):
        self.got(("y",))
        total = self.held(self.yy)[self.ba, self.mine].astype(F32) + self.bufs[4][...].astype(F32)
        self.close(total, self.bufs[0], self.bufs[1])


def slab_maps():
    lane = lax.broadcasted_iota(jnp.int32, (128, D), 0)
    column = lax.broadcasted_iota(jnp.int32, (128, D), 1)
    spread = (lax.rem(column, 48) == lane).astype(F32)
    line = lax.broadcasted_iota(jnp.int32, (256, D), 0)
    block = lax.broadcasted_iota(jnp.int32, (256, D), 1) // 48
    device, kind = line // 16, lax.rem(line, 16)
    wanted = jnp.where(kind < 8, device, 4 * lax.rem(device, 4) + kind - 8)
    keep = jnp.where((wanted == block) & (kind < 12), 1.0, 0.0).astype(F32)
    line = lax.broadcasted_iota(jnp.int32, (16, 256), 1)
    out = lax.broadcasted_iota(jnp.int32, (16, 256), 0)
    device, kind = line // 16, lax.rem(line, 16)
    choose = (jnp.where(kind < 8, kind, 8 + device // 4) == out).astype(F32)
    return spread, keep, choose


def norm_parts(value):
    centre = jnp.mean(value, axis=-1, keepdims=True)
    shifted = value - centre
    spread = jnp.mean(shifted * shifted, axis=-1, keepdims=True)
    return shifted, lax.rsqrt(spread + 1e-6)


def mask_columns(split, keys):
    place_ = lax.broadcasted_iota(jnp.int32, (PAD, HEAD_DIM), 0)
    column = lax.broadcasted_iota(jnp.int32, (PAD, HEAD_DIM), 1)
    first = jnp.where(place_ < split, 1.0, 0.0)
    has = jnp.where(column == 0, first, jnp.where(column == 1, 1.0 - first, 0.0))
    if keys:
        allowed = jnp.where(place_ < SLOT, has, 0.0)
        return jnp.where(column < 2, (allowed - 1.0) * BIG, 0.0).astype(BF16)
    return has.astype(BF16)


def shift_in(source, wide):
    wide[0:1056] = source[0:1056].astype(F32)
    wide[1056:ROWS] = jnp.zeros((ROWS - 1056, D), F32)
    wide[1056:1058] = source[1056:1058].astype(F32)


def halves():
    for slot in range(2):
        for part in range(2):
            start = PAD * slot + 272 * part
            yield SLOT * slot + 272 * part, slice(start, start + 272), part


def attend_kernel(
    split, pa, pw, pb, pc, slab, x, dy,
    wa_out, ww, wb0, wc0, wb1, wc1, e_out, xp_out, n1t_out, dyp_out, dyt_out, m_out, att_out, lt_out,
    wa, vv, xs, n1, e, xp, n1t, dyp, dyt, m, att, lt, lacc, qmask, kmask, qb,
    send_sem, recv_sem, own_sem, out_sem,
):
    dp, aa, ba, half, core, peers = place()
    greet(peers)
    meet(peers)
    sends = Sends(send_sem, recv_sem, peers)
    where = (aa, ba, half)
    first, second = (slice(None), slice(0, STEP)), (slice(None), slice(STEP, 2 * STEP))
    parts = (
        (pw, ww), (pb.at[first], wb0), (pc.at[first], wc0), (pb.at[second], wb1), (pc.at[second], wc1),
    )
    own = [
        pltpu.make_async_copy(part, whole.at[aa, ba], own_sem.at[i])
        for i, (part, whole) in enumerate(((pa, wa), (slab, vv)) + parts)
    ]
    for copy in own:
        copy.start()
    for j in (1, 2, 3):
        sends.start(("v", j), slab, vv.at[aa, ba], f"z{j}")
    a0, a1 = (Gather(f"a{i}", sends, where, pa, wa, 96 * i, 96) for i in (0, 1))
    o0, b0, c0, b1, c1 = (
        Gather(f"b{i}", sends, where, part, whole, 0, GROUP)
        for i, (part, whole) in enumerate(parts)
    )
    outs = []

    def put(source, target):
        copy = pltpu.make_async_copy(source, target, out_sem.at[len(outs)])
        copy.start()
        outs.append(copy)

    a0.first()
    shift_in(dy, xs)
    line = lax.broadcasted_iota(jnp.int32, (272, D), 0)
    total = jnp.zeros((1, D), F32)
    for source, target, part in halves():
        value = xs[source : source + 272]
        if part == 1:
            value = jnp.where(line < SLOT - 272, value, 0.0)
        total = total + jnp.sum(value, axis=0, keepdims=True)
        dyp[target] = value.astype(BF16)
    put(dyp, dyp_out)
    for copy in own:
        copy.wait()
    a0.second()
    a1.first()
    sends.arrived(*[("v", j) for j in (1, 2, 3)])
    sends.start(("v", "y"), vv.at[aa], vv.at[aa], "y")
    sends.start(("v", "c"), vv.at[aa], vv.at[aa], "c")
    shift_in(x, xs)
    for source, target, part in halves():
        xp[target] = xs[source : source + 272].astype(BF16)
    put(xp, xp_out)
    sends.arrived(("v", "y"), ("v", "c"))
    sends.start(("v", "cy"), vv.at[lax.rem(aa + 2, 4)], vv.at[lax.rem(aa + 2, 4)], "c")
    a0.third()
    a1.second()
    o0.first()
    dyt[...] = dyp[...].T
    put(dyt, dyt_out)
    sends.arrived(("v", "cy"))
    spread, keep, choose = slab_maps()
    wide = dot(vv[...].reshape(256, 128), spread.astype(BF16))
    e[...] = exact_dot(choose, wide * keep)
    e[12:13] = total
    put(e, e_out)
    gain, offset = e[0:1], e[1:2]
    for source, target, part in halves():
        shifted, rate = norm_parts(xs[source : source + 272])
        n1[target] = (shifted * rate * gain + offset).astype(BF16)
    a0.fourth()
    a1.third()
    o0.second()
    b0.first()
    n1t[...] = n1[...].T
    put(n1t, n1t_out)
    for slot in range(2):
        qmask[slot] = mask_columns(split[slot], False)
        kmask[slot] = mask_columns(split[slot], True)
    zero = jnp.zeros((1, GROUP), F32)
    for group in range(4):
        lanes = slice(GROUP * group, GROUP * group + GROUP)
        qb[group] = jnp.concatenate((e[2:3, lanes], zero, e[3:4, lanes]), axis=1)
    lacc[...] = jnp.zeros_like(lacc)
    a1.fourth()
    a0.last()
    a1.last()
    put(wa, wa_out)

    def project(group):
        weights = wa[group].reshape(D, WIDE)
        for part in range(4):
            rows = slice(272 * part, 272 * part + 272)
            mixed = dot(n1[rows], weights[:, : 3 * GROUP]) + qb[group]
            m[group, rows] = mixed.astype(BF16)

    def look(group, slot):
        rows = slice(PAD * slot, PAD * slot + PAD)
        for head in range(3):
            cols = slice(HEAD_DIM * head, HEAD_DIM * head + HEAD_DIM)
            both = m[group, rows]
            q = both[:, HEAD_DIM * head : HEAD_DIM * (head + 1)] * 0.125
            k = both[:, GROUP + HEAD_DIM * head : GROUP + HEAD_DIM * (head + 1)]
            v = both[:, 2 * GROUP + HEAD_DIM * head : 2 * GROUP + HEAD_DIM * (head + 1)]
            qx = jnp.concatenate((q.astype(BF16), qmask[slot]), axis=1)
            kx = jnp.concatenate((k, kmask[slot]), axis=1)
            scores = dot(qx, kx, NT)
            top = jnp.max(scores, axis=1, keepdims=True)
            terms = jnp.exp(scores - top)
            total = jnp.sum(terms, axis=1, keepdims=True)
            mixed = dot(terms.astype(BF16), v) / total
            att[group, rows, cols] = mixed.astype(BF16)
            lane = lax.broadcasted_iota(jnp.int32, (PAD, 128), 1)
            lacc[slot] = jnp.where(lane == 3 * group + head, top + jnp.log(total), lacc[slot])

    pumps = (
        (o0.third, b0.second, c0.first),
        (b1.first,),
        (o0.fourth, b0.third, c0.second),
        (b1.second, c1.first),
        (o0.last, b0.fourth, c0.third),
        (b0.last, b1.third, c1.second),
        (c0.fourth, b1.fourth, c1.third),
        (c0.last, b1.last, c1.fourth),
    )
    for group in range(4):
        project(group)
        put(m.at[group], m_out.at[group])
        for slot in range(2):
            look(group, slot)
            for step in pumps[2 * group + slot]:
                step()
    put(att, att_out)
    row = lax.broadcasted_iota(jnp.int32, (16, 128), 0)
    eye = (row == lax.broadcasted_iota(jnp.int32, (16, 128), 1)).astype(F32)
    for slot in range(2):
        lt[slot] = exact_dot(eye, lacc[slot], NT)
    put(lt, lt_out)
    c1.last()
    sends.finish()
    for copy in outs:
        copy.wait()


def attend(split_at, pa, pw, pb, pc, slab, inputs, cotangent):
    vm = pl.BlockSpec(memory_space=pltpu.VMEM)
    hbm = pl.BlockSpec(memory_space=pl.ANY)
    whole = (4, 4, GROUP, WIDE)
    piece = ((4, 4, GROUP, STEP), BF16)
    shapes = [
        (whole, BF16), piece, piece, piece, piece, piece, ((16, D), F32), ((ROWS, D), BF16),
        ((D, ROWS), BF16), ((ROWS, D), BF16), ((D, ROWS), BF16), ((4, ROWS, 3 * GROUP), BF16),
        ((4, ROWS, GROUP), BF16), ((2, 16, PAD), F32),
    ]
    count = 7 * 26 + 6
    return pl.pallas_call(
        attend_kernel,
        out_shape=tuple(jax.ShapeDtypeStruct(*shape) for shape in shapes),
        in_specs=[pl.BlockSpec(memory_space=pltpu.SMEM)] + [vm] * 7,
        out_specs=[hbm] * len(shapes),
        scratch_shapes=[
            pltpu.VMEM(whole, BF16),
            pltpu.VMEM((4, 4, 16, 128), BF16),
            pltpu.VMEM((ROWS, D), F32),
            pltpu.VMEM((ROWS, D), BF16),
        ]
        + [pltpu.VMEM(*shape) for shape in shapes[6:]]
        + [
            pltpu.VMEM((2, PAD, 128), F32),
            pltpu.VMEM((2, PAD, HEAD_DIM), BF16),
            pltpu.VMEM((2, PAD, HEAD_DIM), BF16),
            pltpu.VMEM((4, 1, 3 * GROUP), F32),
            pltpu.SemaphoreType.DMA((count,)),
            pltpu.SemaphoreType.DMA((count,)),
            pltpu.SemaphoreType.DMA((7,)),
            pltpu.SemaphoreType.DMA((16,)),
        ],
        compiler_params=pltpu.CompilerParams(
            collective_id=0, has_side_effects=True, vmem_limit_bytes=58 * MIB
        ),
    )(split_at, pa, pw, pb, pc, slab, inputs, cotangent)


def gelu_parts(hidden):
    size = jnp.abs(hidden)
    t = 1.0 / (1.0 + 0.3 * size)
    bell = jnp.exp(hidden * hidden * -0.5)
    poly = jnp.full_like(t, TAIL[-1])
    for factor in TAIL[-2::-1]:
        poly = poly * t + factor
    tail = poly * t * bell
    phi = jnp.where(hidden < 0, tail, 1.0 - tail)
    return hidden * phi, phi + hidden * bell * (1.0 / math.sqrt(2 * math.pi))


def feed_kernel(
    e, pb, pc, xp_in, dyp_in, dyt_in, att_in, wo_in, wb0, wc0, wb1, wc1,
    out, gvec, ob, oc, gm_out, gatt_out, gwo_out, gb1, gc1, gb2, gc2,
    xp, dyp, dyt, att, wo, w, middle, acc, back, n2, n2t, act, gh, rcb, rcc, *more,
):
    bufs, (send_sem, recv_sem, send_two, recv_two, in_sem, out_sem, own_sem) = more[:-7], more[-7:]
    dp, aa, ba, half, core, peers = place()
    loads = {}
    for name, source, target in (
        ("xp", xp_in, xp), ("att", att_in, att), ("wo", wo_in, wo), ("dyp", dyp_in, dyp),
        ("wb0", wb0, w.at[0, 0]), ("wc0", wc0, w.at[1, 0]), ("dyt", dyt_in, dyt),
        ("wb1", wb1, w.at[0, 1]), ("wc1", wc1, w.at[1, 1]),
    ):
        loads[name] = pltpu.make_async_copy(source, target, in_sem.at[len(loads)])
        loads[name].start()
    third = (slice(None), slice(2 * STEP, 3 * STEP))
    parts = [part.at[third] for part in (pb, pc)]
    own = [
        pltpu.make_async_copy(part, w.at[i, 2, aa, ba], own_sem.at[i])
        for i, part in enumerate(parts)
    ]
    for copy in own:
        copy.start()
    greet(peers)
    where = (aa, ba, half)
    takes = Sends(send_sem, recv_sem, peers)
    gives = Sends(send_two, recv_two, peers)
    tb, tc = (Gather(f"t{i}", takes, where, parts[i], w.at[i, 2], 0, GROUP) for i in (0, 1))
    made = []
    for i, o in enumerate((ob, oc)):
        held = lambda y, i=i: w.at[i, 0, 2 * y + core]
        for kind, row, count in ((SumY, 0, 128), (SumX, 128, 64)):
            at = 5 * len(made)
            made.append(kind(f"s{len(made)}", gives, where, held, o, row, count, bufs[at : at + 5]))
    by, bx, cy, cx = made
    outs = []

    def put(source, target):
        copy = pltpu.make_async_copy(source, target, out_sem.at[len(outs)])
        copy.start()
        outs.append(copy)

    for name in ("xp", "att", "wo"):
        loads[name].wait()
    gvec[...] = jnp.zeros_like(gvec)
    gvec[7:8] = e[12:13]
    for part in range(4):
        rows = slice(272 * part, 272 * part + 272)
        value = xp[rows].astype(F32) + e[4:5]
        for group in range(4):
            value = value + dot(att[group, rows], wo[group, :, 0:GROUP], NT)
        middle[rows] = value
        shifted, rate = norm_parts(value)
        n2[rows] = (shifted * rate * e[5:6] + e[6:7]).astype(BF16)
        acc[rows] = value + e[7:8]
        back[rows] = jnp.zeros((272, D), F32)
        if part == 0:
            meet(peers)
            tb.first()
            tc.first()
    for copy in own:
        copy.wait()
    n2t[...] = n2[...].T
    for name in ("dyp", "wb0", "wc0", "dyt"):
        loads[name].wait()

    def whole_unit(u, forward):
        step, pair, now = u // 2, u % 2, u % 2
        both = ((2 * now, 2 * pair), (2 * now + 1, 2 * pair + 1))
        columns = slice(STEP * step, STEP * step + STEP)

        def weight(kind, group):
            return w[kind, step, group].reshape(D, STEP)

        def up(part):
            rows = slice(272 * part, 272 * part + 272)
            return [
                (
                    dot(n2[rows], weight(0, group)) + e[8 + group : 9 + group, columns],
                    dot(dyp[rows], weight(1, group)),
                )
                for _, group in both
            ]

        def across(part, made, totals):
            rows = slice(272 * part, 272 * part + 272)
            new = []
            for (at, _), (hidden, grad), total in zip(both, made, totals):
                forward, slope = gelu_parts(hidden)
                grad = (grad * slope).astype(BF16)
                act[at, rows] = forward.astype(BF16)
                gh[at, rows] = grad
                new.append(total + jnp.sum(grad.astype(F32), axis=0, keepdims=True))
            return new

        def down(part):
            rows = slice(272 * part, 272 * part + 272)
            for total, values, kind in ((acc, act, 1), (back, gh, 0)):
                more = [dot(values[at, rows], weight(kind, group), NT) for at, group in both]
                total[rows] = total[rows] + more[0] + more[1]

        if forward:
            totals = [jnp.zeros((1, STEP), F32)] * 2
            made = up(0)
            for part in range(4):
                ahead = up(part + 1) if part < 3 else None
                totals = across(part, made, totals)
                if part:
                    down(part - 1)
                made = ahead
            down(3)
            for (_, group), total in zip(both, totals):
                gvec[8 + group : 9 + group, columns] = total
        else:
            for i, (turned, values) in enumerate(((n2t, gh), (dyt, act))):
                for j in range(2):
                    grad = dot(turned[...], values[2 * now + j]).astype(BF16)
                    w[i, step, 2 * pair + j] = grad.reshape(4, GROUP, STEP)

    once = 1 + jnp.minimum(dp, 0)

    def unit(u, forward):
        def inside(_, carry):
            whole_unit(u, forward)
            return carry

        lax.fori_loop(0, once, inside, 0)

    unit(0, True)
    tb.second()
    tc.second()
    unit(0, False)
    unit(1, True)
    tb.third()
    tc.third()
    unit(1, False)
    for i, rc in enumerate((rcb, rcc)):
        for y in (0, 1):
            gives.start((i, y), w.at[i, 0, 2 * y + 1 - core], rc.at[y], "c")
    for name in ("wb1", "wc1"):
        loads[name].wait()
    unit(2, True)
    tb.fourth()
    tc.fourth()
    gives.arrived((0, 0), (0, 1))
    by.first(rcb)
    bx.first(rcb)
    gives.arrived((1, 0), (1, 1))
    cy.first(rcc)
    cx.first(rcc)
    unit(2, False)
    unit(3, True)
    tb.last()
    tc.last()
    takes.finish()
    unit(3, False)
    put(w.at[0, 1], gb1)
    put(w.at[1, 1], gc1)
    unit(4, True)
    for batch in made:
        batch.second()
    unit(4, False)
    unit(5, True)
    for batch in made:
        batch.third()
    line = lax.broadcasted_iota(jnp.int32, (16, D), 0)
    out[0:528] = acc[0:528].astype(BF16)
    out[528:544] = jnp.where(line == 0, acc[528:544], acc[543:559]).astype(BF16)
    out[544:1056] = acc[559:1071].astype(BF16)
    out[1056:1058] = acc[1071:1073].astype(BF16)
    unit(5, False)
    put(w.at[0, 2], gb2)
    put(w.at[1, 2], gc2)
    sums = [jnp.zeros((1, D), F32)] * 3
    for part in range(4):
        rows = slice(272 * part, 272 * part + 272)
        shifted, rate = norm_parts(middle[rows])
        hat = shifted * rate
        grad = back[rows]
        inner = grad * e[5:6]
        mean = jnp.mean(inner, axis=-1, keepdims=True)
        along = jnp.mean(inner * hat, axis=-1, keepdims=True)
        total = dyp[rows].astype(F32) + rate * (inner - mean - hat * along)
        middle[rows] = total
        branch = total.astype(BF16)
        n2[rows] = branch
        for i, value in enumerate((grad * hat, grad, branch.astype(F32))):
            sums[i] = sums[i] + jnp.sum(value, axis=0, keepdims=True)
        for group in range(4):
            act[group, rows, 0:GROUP] = dot(branch, wo[group, :, 0:GROUP]).astype(BF16)
        if part == 1:
            for batch in made:
                batch.fourth()
    put(middle, gm_out)
    put(act, gatt_out)
    gvec[5:6] = sums[0]
    gvec[6:7] = sums[1]
    gvec[4:5] = sums[2]
    n2t[...] = n2[...].T
    for group in range(4):
        gh[group, 0:D, 0:GROUP] = dot(n2t[...], att[group]).astype(BF16)
    put(gh.at[:, 0:D], gwo_out)
    for batch in made:
        batch.last()
    gives.finish()
    for copy in outs:
        copy.wait()


def feed(e, pb, pc, xp, dyp, dyt, att, wo, wb0, wc0, wb1, wc1, local):
    vm = pl.BlockSpec(memory_space=pltpu.VMEM)
    hbm = pl.BlockSpec(memory_space=pl.ANY)
    piece = jax.ShapeDtypeStruct((4, 4, GROUP, STEP), BF16)
    own = jax.ShapeDtypeStruct((GROUP, STEP), F32)
    sums = SumY.scratch(128, STEP) + SumX.scratch(64, STEP)
    gives = 4 + 2 * (6 + 10)
    return pl.pallas_call(
        feed_kernel,
        out_shape=(
            jax.ShapeDtypeStruct((local, D), BF16),
            jax.ShapeDtypeStruct((16, D), F32),
            own,
            own,
            jax.ShapeDtypeStruct((ROWS, D), F32),
            jax.ShapeDtypeStruct((4, ROWS, STEP), BF16),
            jax.ShapeDtypeStruct((4, D, STEP), BF16),
            piece,
            piece,
            piece,
            piece,
        ),
        in_specs=[vm] * 3 + [hbm] * 9,
        out_specs=[vm] * 4 + [hbm] * 7,
        scratch_shapes=[
            pltpu.VMEM((ROWS, D), BF16),
            pltpu.VMEM((ROWS, D), BF16),
            pltpu.VMEM((D, ROWS), BF16),
            pltpu.VMEM((4, ROWS, GROUP), BF16),
            pltpu.VMEM((4, D, STEP), BF16),
            pltpu.VMEM((2, 3, 4, 4, GROUP, STEP), BF16),
            pltpu.VMEM((ROWS, D), F32),
            pltpu.VMEM((ROWS, D), F32),
            pltpu.VMEM((ROWS, D), F32),
            pltpu.VMEM((ROWS, D), BF16),
            pltpu.VMEM((D, ROWS), BF16),
            pltpu.VMEM((4, ROWS, STEP), BF16),
            pltpu.VMEM((4, ROWS, STEP), BF16),
            pltpu.VMEM((2, 4, GROUP, STEP), BF16),
            pltpu.VMEM((2, 4, GROUP, STEP), BF16),
        ]
        + sums * 2
        + [
            pltpu.SemaphoreType.DMA((52,)),
            pltpu.SemaphoreType.DMA((52,)),
            pltpu.SemaphoreType.DMA((gives,)),
            pltpu.SemaphoreType.DMA((gives,)),
            pltpu.SemaphoreType.DMA((9,)),
            pltpu.SemaphoreType.DMA((7,)),
            pltpu.SemaphoreType.DMA((2,)),
        ],
        compiler_params=pltpu.CompilerParams(
            collective_id=2, has_side_effects=True, vmem_limit_bytes=60 * MIB
        ),
    )(e, pb, pc, xp, dyp, dyt, att, wo, wb0, wc0, wb1, wc1)


def unattend_kernel(
    split, e, lt, gvec, ob0, oc0, xp_in, n1t_in, m_in, gatt_in, wa_in, gm_in, gwo, gb1, gc1, gb2, gc2,
    gin, oa, ow, ob, oc, ov,
    xp, n1t, m, gatt, ga, gm, h, rc, rca, rya, gmix, back, sums, gv, qmask, kmask,
    vh, vc, vy, vz, vx, *more,
):
    bufs, (send_sem, recv_sem, own_sem, in_sem) = more[:-4], more[-4:]
    dp, aa, ba, half, core, peers = place()
    greet(peers)
    yy = aa // 2
    order = [2 * (1 - yy) + 1 - core, 2 * (1 - yy) + core, 2 * yy + 1 - core, 2 * yy + core]
    loads = {}

    def load(name, source, target):
        loads[name] = pltpu.make_async_copy(source, target, in_sem.at[len(loads)])
        loads[name].start()

    for k in range(4):
        load(("m", k), m_in.at[order[k]], m.at[order[k]])
        load(("gatt", k), gatt_in.at[order[k]], gatt.at[order[k]])
        if k == 0:
            load("n1t", n1t_in, n1t)
            load("wa", wa_in, ga)
    load("xp", xp_in, xp)
    load("gm", gm_in, gm)
    own = []
    given = (gb1, gc1, gb2, gc2, gwo)
    for i, g in enumerate(given):
        for y in (0, 1):
            own.append(pltpu.make_async_copy(g.at[2 * y + core], h.at[i, y], own_sem.at[len(own)]))
            own[-1].start()
    sends = Sends(send_sem, recv_sem, peers)
    where = (aa, ba, half)
    made = []
    for i, o in enumerate((ob, oc, ob, oc, ow)):
        if i < 4:
            o = o.at[:, STEP * (1 + i // 2) : STEP * (2 + i // 2)]
        held = lambda y, i=i: h.at[i, y]
        for kind, row, count in ((SumY, 0, 64), (SumX, 64, 128)):
            at = 5 * len(made)
            made.append(kind(f"s{len(made)}", sends, where, held, o, row, count, bufs[at : at + 5]))
            made[-1].open = functools.partial(made[-1].first, rc.at[i])
    for i in range(3):
        at = 5 * len(made)
        held = lambda y: ga.at[2 * y + core]
        made.append(SumY(f"a{i}", sends, where, held, oa, 64 * i, 64, bufs[at : at + 5]))
    by1, bx1, cy1, cx1, by2, bx2, cy2, cx2, wy, wx, a0, a1, a2 = made
    for slot in range(2):
        qmask[slot] = mask_columns(split[slot], False)
        kmask[slot] = mask_columns(split[slot], True)
    back[...] = jnp.zeros_like(back)

    def look(group, slot):
        rows = slice(PAD * slot, PAD * slot + PAD)
        for head in range(3):
            both = m[group, rows]
            q = (both[:, HEAD_DIM * head : HEAD_DIM * (head + 1)] * 0.125).astype(BF16)
            k = both[:, GROUP + HEAD_DIM * head : GROUP + HEAD_DIM * (head + 1)]
            v = both[:, 2 * GROUP + HEAD_DIM * head : 2 * GROUP + HEAD_DIM * (head + 1)]
            go = gatt[group, rows][:, HEAD_DIM * head : HEAD_DIM * (head + 1)]
            qx = jnp.concatenate((q, qmask[slot]), axis=1)
            kx = jnp.concatenate((k, kmask[slot]), axis=1)
            scores = dot(kx, qx, NT)
            probs = jnp.exp(scores - lt[slot, pl.ds(3 * group + head, 1)])
            gprobs = dot(v, go, NT)
            both_ = probs * gprobs
            delta = jnp.sum(both_, axis=0, keepdims=True)
            gs = (both_ - probs * delta).astype(BF16)
            gq = dot(gs, k, TN) * 0.125
            gk = dot(gs, q)
            gval = dot(probs.astype(BF16), go)
            for i, value in enumerate((gq, gk, gval)):
                at = GROUP * i + HEAD_DIM * head
                gmix[rows, at : at + HEAD_DIM] = value.astype(BF16)

    def grads(k):
        group = order[k]
        grad = dot(n1t[...], gmix[...]).reshape(4, GROUP, 3 * GROUP)
        if k in (1, 3):
            sends.arrived(("a", k - 1))
            terms = [rca.at[k // 2]]
            if k == 3:
                sends.arrived(("a", 1))
                terms.append(rya)
            for term in terms:
                grad = grad + term[:, :, 0 : 3 * GROUP].astype(F32)
        ga[group, :, :, 0 : 3 * GROUP] = grad.astype(BF16)

    def fold(group):
        weights = ga[group].reshape(D, WIDE)[:, : 3 * GROUP]
        total = jnp.zeros((1, 3 * GROUP), F32)
        for part in range(4):
            rows = slice(272 * part, 272 * part + 272)
            total = total + jnp.sum(gmix[rows].astype(F32), axis=0, keepdims=True)
            back[rows] = back[rows] + dot(gmix[rows], weights, NT)
        sums[group] = total

    def store(k):
        group = order[k]
        fold(group)
        grads(k)
        if k == 1:
            sends.start(("a", 1), ga.at[group], rya, "y")
        elif k < 3:
            sends.start(("a", k), ga.at[group], rca.at[k // 2], "c")

    def begin():
        meet(peers)
        for i, g in enumerate(given):
            for y in (0, 1):
                sends.start((i, y), g.at[2 * y + 1 - core], rc.at[i, y], "c")

    def settle():
        ob[:, 0:STEP] = ob0[...]
        oc[:, 0:STEP] = oc0[...]
        for copy in own:
            copy.wait()
        for i in range(5):
            sends.arrived((i, 0), (i, 1))
        for name in ("n1t", "wa"):
            loads[name].wait()

    pumps = (
        (begin,),
        (settle, by1.open, cy1.open, bx1.open),
        (cx1.open, by2.open, cy2.open, wy.open),
        (by1.second, cy1.second, bx1.second, wx.open),
        (cx1.second, bx2.open, by2.second, cy2.second, wy.second),
        (by1.third, cy1.third, bx1.third, wx.second, cx2.open),
        (cx1.third, by2.third, cy2.third, wy.third, bx2.second),
        (by1.fourth, cy1.fourth, bx1.fourth, wx.third, cx2.second),
    )
    for k in range(4):
        loads[("m", k)].wait()
        loads[("gatt", k)].wait()
        for slot in range(2):
            look(order[k], slot)
            for step in pumps[2 * k + slot]:
                step()
        store(k)
    for batch in (a0, a1, a2):
        mine = batch.held(yy)
        batch.start_x = functools.partial(batch.send, ("x",), mine.at[:, batch.theirs], batch.bufs[3], "x")
    a0.start_x()
    for step in (cx1.fourth, by2.fourth, cy2.fourth, wy.fourth, wx.fourth, bx2.third, cx2.third):
        step()
    loads["xp"].wait()
    loads["gm"].wait()
    tot_gain, tot_bias = jnp.zeros((1, D), F32), jnp.zeros((1, D), F32)
    for part in range(4):
        rows = slice(272 * part, 272 * part + 272)
        shifted, rate = norm_parts(xp[rows].astype(F32))
        hat = shifted * rate
        grad = back[rows]
        inner = grad * e[0:1]
        mean = jnp.mean(inner, axis=-1, keepdims=True)
        along = jnp.mean(inner * hat, axis=-1, keepdims=True)
        tot_gain = tot_gain + jnp.sum(grad * hat, axis=0, keepdims=True)
        tot_bias = tot_bias + jnp.sum(grad, axis=0, keepdims=True)
        back[rows] = gm[rows] + rate * (inner - mean - hat * along)
        if part == 2:
            a0.third()
            a1.start_x()
    line = lax.broadcasted_iota(jnp.int32, (16, D), 0)
    q_row = jnp.concatenate([sums[i][:, :GROUP] for i in range(4)], axis=1)
    v_row = jnp.concatenate([sums[i][:, 2 * GROUP :] for i in range(4)], axis=1)
    rows = jnp.where(line == 0, tot_gain, jnp.where(line == 1, tot_bias, gvec[...]))
    rows = jnp.where(line == 2, q_row, jnp.where(line == 3, v_row, rows))
    spread, keep, choose = slab_maps()
    wide = exact_dot(choose, rows, TN) * keep
    gv[...] = exact_dot(wide, spread, NT).reshape(4, 4, 16, 128)
    for y in (0, 1):
        sends.start(("v", "c", y), gv.at[2 * y + 1 - core], vc.at[y], "c")
    a1.third()
    a2.start_x()
    for y in (0, 1):
        sends.arrived(("v", "c", y))
        vh[y] = gv[2 * y + core] + vc[y]
    sends.start(("v", "y"), vh.at[1 - yy], vy, "y")
    gin[0:528] = back[0:528].astype(BF16)
    gin[528:544] = jnp.where(line == 0, back[528:544], back[543:559]).astype(BF16)
    gin[544:1056] = back[559:1071].astype(BF16)
    gin[1056:1058] = back[1071:1073].astype(BF16)
    a0.fourth()
    bx2.fourth()
    cx2.fourth()
    sends.arrived(("v", "y"))
    vh[yy] = vh[yy] + vy[...]
    for j in (1, 2, 3):
        sends.start(("v", "z", j), vh.at[yy, lax.rem(ba + j, 4)], vz.at[j - 1], f"z{j}")
    for batch in made[:10]:
        batch.last()
    a2.third()
    a1.fourth()
    sends.arrived(*[("v", "z", j) for j in (1, 2, 3)])
    vh[yy, ba] = vh[yy, ba] + (vz[0] + vz[1] + vz[2])
    sends.start(("v", "x"), vh.at[yy, ba], vx, "x")
    a2.fourth()
    sends.arrived(("v", "x"))
    ov[...] = vh[yy, ba] + vx[...]
    a0.last()
    a1.last()
    a2.last()
    sends.finish()


def unattend(split_at, e, lt, gvec, ob0, oc0, *stored, local):
    vm = pl.BlockSpec(memory_space=pltpu.VMEM)
    hbm = pl.BlockSpec(memory_space=pl.ANY)
    out = jax.ShapeDtypeStruct((GROUP, D), F32)
    count = 10 + 5 * 16 + 3 + 3 * 5 + 7
    return pl.pallas_call(
        unattend_kernel,
        out_shape=(
            jax.ShapeDtypeStruct((local, D), BF16),
            jax.ShapeDtypeStruct((GROUP, WIDE), F32),
            jax.ShapeDtypeStruct((GROUP, STEP), F32),
            out, out,
            jax.ShapeDtypeStruct((16, 128), F32),
        ),
        in_specs=[pl.BlockSpec(memory_space=pltpu.SMEM)] + [vm] * 5 + [hbm] * 11,
        out_specs=[vm] * 6,
        scratch_shapes=[
            pltpu.VMEM((ROWS, D), BF16),
            pltpu.VMEM((D, ROWS), BF16),
            pltpu.VMEM((4, ROWS, 3 * GROUP), BF16),
            pltpu.VMEM((4, ROWS, STEP), BF16),
            pltpu.VMEM((4, 4, GROUP, WIDE), BF16),
            pltpu.VMEM((ROWS, D), F32),
            pltpu.VMEM((5, 2, 4, GROUP, STEP), BF16),
            pltpu.VMEM((5, 2, 4, GROUP, STEP), BF16),
            pltpu.VMEM((2, 4, GROUP, WIDE), BF16),
            pltpu.VMEM((4, GROUP, WIDE), BF16),
            pltpu.VMEM((ROWS, 3 * GROUP), BF16),
            pltpu.VMEM((ROWS, D), F32),
            pltpu.VMEM((4, 1, 3 * GROUP), F32),
            pltpu.VMEM((4, 4, 16, 128), F32),
            pltpu.VMEM((2, PAD, HEAD_DIM), BF16),
            pltpu.VMEM((2, PAD, HEAD_DIM), BF16),
            pltpu.VMEM((2, 4, 16, 128), F32),
            pltpu.VMEM((2, 4, 16, 128), F32),
            pltpu.VMEM((4, 16, 128), F32),
            pltpu.VMEM((3, 16, 128), F32),
            pltpu.VMEM((16, 128), F32),
        ]
        + (SumY.scratch(64, STEP) + SumX.scratch(128, STEP)) * 5
        + SumY.scratch(64, WIDE) * 3
        + [
            pltpu.SemaphoreType.DMA((count,)),
            pltpu.SemaphoreType.DMA((count,)),
            pltpu.SemaphoreType.DMA((10,)),
            pltpu.SemaphoreType.DMA((13,)),
        ],
        compiler_params=pltpu.CompilerParams(
            collective_id=1, has_side_effects=True, vmem_limit_bytes=62 * MIB
        ),
    )(split_at, e, lt, gvec, ob0, oc0, *stored)


def results_kernel(output, gin, oa, ow, ob, oc, ov, out, gin_out, qkv, wo, up, down, up_bias, *rows):
    out[...] = output[...]
    gin_out[...] = gin[...]
    for kind in range(3):
        qkv[kind] = oa[:, GROUP * kind : GROUP * kind + GROUP]
    wo[...] = ow[...].T[:GROUP]
    up[...] = ob[...]
    down[...] = oc[...]
    up_bias[...] = jnp.concatenate([ov[i : i + 1, :48] for i in range(8, 12)], axis=1)[0]
    for i, row in enumerate(rows):
        row[...] = ov[i, :48]


def results(output, gin, oa, ow, ob, oc, ov):
    shapes = [(3, GROUP, GROUP), (GROUP, GROUP), (GROUP, D), (GROUP, D), (GROUP,)] + [(48,)] * 8
    return pl.pallas_call(
        results_kernel,
        out_shape=[jax.ShapeDtypeStruct(gin.shape, BF16)] * 2
        + [jax.ShapeDtypeStruct(shape, F32) for shape in shapes],
        compiler_params=pltpu.CompilerParams(vmem_limit_bytes=60 * MIB),
    )(output, gin, oa, ow, ob, oc, ov)


def on_device(
    inputs, cotangent, split_at, ln1_gain, ln1_bias, w_qkv, q_bias, v_bias, w_out, o_bias,
    ln2_gain, ln2_bias, w_up, up_bias, w_down, down_bias,
):
    pa = jnp.pad(w_qkv.reshape(GROUP, 3 * GROUP), ((0, 0), (0, WIDE - 3 * GROUP)))
    pw = jnp.pad(w_out.T, ((0, 0), (0, STEP - GROUP)))
    vectors = jnp.stack(
        (ln1_gain, ln1_bias, q_bias, v_bias, o_bias, ln2_gain, ln2_bias, down_bias)
        + tuple(up_bias[48 * i : 48 * i + 48] for i in range(4))
    )
    slab = jnp.pad(vectors, ((0, 4), (0, 80)))
    pc = w_down.T
    local = inputs.shape[0]
    wa, ww, *pieces, e, xp, n1t, dyp, dyt, m, att, lt = attend(
        split_at, pa, pw, w_up, pc, slab, inputs, cotangent
    )
    output, gvec, ob0, oc0, gm, gatt, gwo, *grads = feed(
        e, w_up, pc, xp, dyp, dyt, att, ww.reshape(4, D, STEP), *pieces, local
    )
    gwo = gwo.reshape(4, 4, GROUP, STEP)
    gin, oa, ow, ob, oc, ov = unattend(
        split_at, e, lt, gvec, ob0, oc0, xp, n1t, m, gatt, wa, gm, gwo, *grads, local=local
    )
    if lax.axis_size("dp") > 2:
        oa, ow, ob, oc, ov = (lax.psum(v, "dp") * 0.5 for v in (oa, ow, ob, oc, ov))
    output, gin, qkv, wo, up, down, up_row, *rows = results(output, gin, oa, ow, ob, oc, ov)
    return (
        output,
        gin,
        rows[0],
        rows[1],
        qkv.transpose(1, 0, 2),
        rows[2],
        rows[3],
        wo,
        rows[4],
        rows[5],
        rows[6],
        up,
        up_row,
        down.T,
        rows[7],
    )


def solution(mesh):
    rows = P(("dp", "aa", "ba"), None)
    vec = P(("aa", "ba"))
    grid_qkv, first, second = P("ba", None, "aa"), P("aa", "ba"), P("ba", "aa")
    params = (vec, vec, grid_qkv, vec, vec, first, vec, vec, vec, second, vec, first, vec)
    return jax.shard_map(
        on_device,
        mesh=mesh,
        in_specs=(rows, rows, P(("dp", "aa", "ba"))) + params,
        out_specs=(rows, rows) + params,
        check_vma=False,
    )
```

```python
import functools
import math

import jax
import jax.numpy as jnp
from jax import lax
from jax.experimental import pallas as pl
from jax.experimental.pallas import tpu as pltpu
from jax.sharding import PartitionSpec as P

D = 768
HEADS = 12
HEAD_DIM = 64
SLOT = 529
PAD = 544
ROWS = 2 * PAD
STEP = 256
WIDE = 640
GROUP = 192
BIG = 1e30
MESH = pl.DeviceIdType.MESH
F32 = jnp.float32
BF16 = jnp.bfloat16
MIB = 1 << 20

NT = (((1,), (1,)), ((), ()))
NN = (((1,), (0,)), ((), ()))
TN = (((0,), (0,)), ((), ()))

TAIL = (
    0.11962926248861097,
    0.12075451364069298,
    0.09991001218129214,
    0.12857310923328652,
    -0.0537053561953165,
    0.20637712218096793,
    -0.15721681637037743,
    0.03567808025645831,
)


def dot(left, right, dims=NN):
    return lax.dot_general(left, right, dims, preferred_element_type=F32)


def exact_dot(left, right, dims=NN):
    return lax.dot_general(
        left, right, dims, preferred_element_type=F32, precision=lax.Precision.HIGHEST
    )


def place():
    dp, aa, ba = lax.axis_index("dp"), lax.axis_index("aa"), lax.axis_index("ba")
    half, core = lax.rem(dp, 2), lax.rem(aa, 2)
    peers = {
        "x": (dp + 1 - 2 * half, aa, ba),
        "y": (dp, lax.rem(aa + 2, 4), ba),
        "c": (dp, aa + 1 - 2 * core, ba),
        "z1": (dp, aa, lax.rem(ba + 1, 4)),
        "z2": (dp, aa, lax.rem(ba + 2, 4)),
        "z3": (dp, aa, lax.rem(ba + 3, 4)),
    }
    return dp, aa, ba, half, core, peers


def greet(peers):
    barrier = pltpu.get_barrier_semaphore()
    for peer in peers.values():
        pl.semaphore_signal(barrier, inc=1, device_id=peer, device_id_type=MESH)


def meet(peers):
    pl.semaphore_wait(pltpu.get_barrier_semaphore(), len(peers))


class Sends:
    def __init__(self, send_sem, recv_sem, peers):
        self.send_sem, self.recv_sem, self.peers = send_sem, recv_sem, peers
        self.made = {}

    def start(self, name, src, dst, peer):
        at = len(self.made)
        copy = pltpu.make_async_remote_copy(
            src_ref=src,
            dst_ref=dst,
            send_sem=self.send_sem.at[at],
            recv_sem=self.recv_sem.at[at],
            device_id=self.peers[peer],
            device_id_type=MESH,
        )
        copy.start()
        self.made[name] = copy

    def arrived(self, *names):
        for name in names:
            self.made[name].wait_recv()

    def finish(self):
        for copy in self.made.values():
            copy.wait_send()


def sixteen(value):
    return pl.multiple_of(value, 16)


class Gather:
    def __init__(self, name, sends, where, part, whole, row, count):
        self.name, self.sends, self.part, self.whole = name, sends, part, whole
        self.aa, self.ba, self.half = where
        self.ay = lax.rem(self.aa + 2, 4)
        self.other = [(j, lax.rem(self.ba + j, 4)) for j in (1, 2, 3)]
        big, small = count // 3, count // 6
        self.big = pl.ds(sixteen(row + big * self.half), big)
        self.big_not = pl.ds(sixteen(row + big - big * self.half), big)
        self.small = pl.ds(sixteen(row + 2 * big + small * self.half), small)
        self.rest = pl.ds(row + 2 * big, big)

    def send(self, key, src, dst, peer):
        self.sends.start((self.name,) + key, src, dst, peer)

    def move(self, key, at, peer):
        self.send(key, self.whole.at[at], self.whole.at[at], peer)

    def got(self, *keys):
        self.sends.arrived(*[(self.name,) + key for key in keys])

    def first(self):
        w, aa, ba = self.whole, self.aa, self.ba
        for j in (1, 2, 3):
            self.send(("z", j), self.part.at[self.big], w.at[aa, ba, self.big], f"z{j}")
        self.send(("y",), self.part.at[self.small], w.at[aa, ba, self.small], "y")
        for j in (1, 2, 3):
            self.send(("zs", j), self.part.at[self.small], w.at[aa, ba, self.small], f"z{j}")

    def second(self):
        self.got(("z", 1), ("z", 2), ("z", 3))
        for j, z in self.other:
            self.move(("x", j), (self.aa, z, self.big), "x")
        self.move(("yb",), (self.aa, slice(None), self.big), "y")
        self.got(("y",))
        for j in (1, 2, 3):
            self.move(("zy", j), (self.ay, self.ba, self.small), f"z{j}")
        self.got(("zs", 1), ("zs", 2), ("zs", 3))
        for j, z in self.other:
            self.move(("xs", j), (self.aa, z, self.small), "x")
        self.move(("c0",), (self.aa, slice(None), self.big), "c")

    def third(self):
        every = slice(None)
        self.got(("x", 1), ("x", 2), ("x", 3))
        self.move(("yn",), (self.aa, every, self.big_not), "y")
        self.got(("zy", 1), ("zy", 2), ("zy", 3))
        self.move(("xy",), (self.ay, every, self.small), "x")
        self.got(("yb",))
        self.move(("c1",), (self.aa, every, self.big_not), "c")
        self.move(("c2",), (self.ay, every, self.big), "c")

    def fourth(self):
        every = slice(None)
        self.got(("xs", 1), ("xs", 2), ("xs", 3))
        self.move(("c3",), (self.aa, every, self.rest), "c")
        self.got(("yn",))
        self.move(("c4",), (self.ay, every, self.big_not), "c")
        self.got(("xy",))
        self.move(("c5",), (self.ay, every, self.rest), "c")

    def last(self):
        self.got(*[(f"c{i}",) for i in range(6)])


class Sum:
    def __init__(self, name, sends, where, held, out, row, count, bufs):
        self.name, self.sends, self.held, self.out, self.bufs = name, sends, held, out, bufs
        part = count // 2
        self.aa, self.ba, self.half = where
        self.yy = self.aa // 2
        self.yn = 1 - self.yy
        self.other = [(j, lax.rem(self.ba + j, 4)) for j in (1, 2, 3)]
        self.rows = pl.ds(row, count)
        self.mine = pl.ds(sixteen(row + part * self.half), part)
        self.theirs = pl.ds(sixteen(row + part - part * self.half), part)

    def send(self, key, src, dst, peer):
        self.sends.start((self.name,) + key, src, dst, peer)

    def got(self, *keys):
        self.sends.arrived(*[(self.name,) + key for key in keys])

    def add(self, h, rows, more):
        @pl.loop(0, 4)
        def _(z):
            h[z, rows] = (h[z, rows].astype(F32) + more[z].astype(F32)).astype(BF16)

    def add_core(self, rc):
        for y in (0, 1):
            self.add(self.held(y), self.rows, rc.at[y, :, self.rows])

    def over_z(self, h, key, at):
        for j, z in self.other:
            self.send(key + (j,), h.at[z, self.mine], at(j - 1), f"z{j}")

    def close(self, total, own, far):
        own[...] = total.astype(BF16)
        self.send(("f",), own, far, "x")

    def last(self):
        own, far = self.bufs[:2]
        self.out[self.mine] = own[...].astype(F32)
        self.got(("f",))
        self.out[self.theirs] = far[...].astype(F32)


class SumY(Sum):
    @staticmethod
    def scratch(count, width):
        part = count // 2
        return [
            pltpu.VMEM((part, width), BF16),
            pltpu.VMEM((part, width), BF16),
            pltpu.VMEM((4, count, width), BF16),
            pltpu.VMEM((4, part, width), BF16),
            pltpu.VMEM((3, part, width), BF16),
        ]

    def first(self, rc):
        self.add_core(rc)
        self.send(("y",), self.held(self.yn).at[:, self.rows], self.bufs[2], "y")

    def second(self):
        self.got(("y",))
        h = self.held(self.yy)
        self.add(h, self.rows, self.bufs[2])
        self.send(("x",), h.at[:, self.theirs], self.bufs[3], "x")

    def third(self):
        self.got(("x",))
        h = self.held(self.yy)
        self.add(h, self.mine, self.bufs[3])
        self.over_z(h, ("z",), lambda i: self.bufs[4].at[i])

    def fourth(self):
        self.got(("z", 1), ("z", 2), ("z", 3))
        total = self.held(self.yy)[self.ba, self.mine].astype(F32)
        for i in range(3):
            total = total + self.bufs[4][i].astype(F32)
        self.close(total, self.bufs[0], self.bufs[1])


class SumX(Sum):
    @staticmethod
    def scratch(count, width):
        part = count // 2
        return [
            pltpu.VMEM((part, width), BF16),
            pltpu.VMEM((part, width), BF16),
            pltpu.VMEM((2, 4, part, width), BF16),
            pltpu.VMEM((2, 3, part, width), BF16),
            pltpu.VMEM((part, width), BF16),
        ]

    def first(self, rc):
        self.add_core(rc)
        for y in (0, 1):
            self.send(("x", y), self.held(y).at[:, self.theirs], self.bufs[2].at[y], "x")

    def second(self):
        self.got(("x", 0), ("x", 1))
        for y in (0, 1):
            h = self.held(y)
            self.add(h, self.mine, self.bufs[2].at[y])
            self.over_z(h, ("z", y), lambda i, y=y: self.bufs[3].at[y, i])

    def third(self):
        for y in (0, 1):
            h = self.held(y)
            self.got(("z", y, 1), ("z", y, 2), ("z", y, 3))
            total = h[self.ba, self.mine].astype(F32)
            for i in range(3):
                total = total + self.bufs[3][y, i].astype(F32)
            h[self.ba, self.mine] = total.astype(BF16)
        self.send(("y",), self.held(self.yn).at[self.ba, self.mine], self.bufs[4], "y")

    def fourth(self):
        self.got(("y",))
        total = self.held(self.yy)[self.ba, self.mine].astype(F32) + self.bufs[4][...].astype(F32)
        self.close(total, self.bufs[0], self.bufs[1])


def slab_maps():
    lane = lax.broadcasted_iota(jnp.int32, (128, D), 0)
    column = lax.broadcasted_iota(jnp.int32, (128, D), 1)
    spread = (lax.rem(column, 48) == lane).astype(F32)
    line = lax.broadcasted_iota(jnp.int32, (256, D), 0)
    block = lax.broadcasted_iota(jnp.int32, (256, D), 1) // 48
    device, kind = line // 16, lax.rem(line, 16)
    wanted = jnp.where(kind < 8, device, 4 * lax.rem(device, 4) + kind - 8)
    keep = jnp.where((wanted == block) & (kind < 12), 1.0, 0.0).astype(F32)
    line = lax.broadcasted_iota(jnp.int32, (16, 256), 1)
    out = lax.broadcasted_iota(jnp.int32, (16, 256), 0)
    device, kind = line // 16, lax.rem(line, 16)
    choose = (jnp.where(kind < 8, kind, 8 + device // 4) == out).astype(F32)
    return spread, keep, choose


def norm_parts(value):
    centre = jnp.mean(value, axis=-1, keepdims=True)
    shifted = value - centre
    spread = jnp.mean(shifted * shifted, axis=-1, keepdims=True)
    return shifted, lax.rsqrt(spread + 1e-6)


def mask_columns(split, keys):
    place_ = lax.broadcasted_iota(jnp.int32, (PAD, HEAD_DIM), 0)
    column = lax.broadcasted_iota(jnp.int32, (PAD, HEAD_DIM), 1)
    first = jnp.where(place_ < split, 1.0, 0.0)
    has = jnp.where(column == 0, first, jnp.where(column == 1, 1.0 - first, 0.0))
    if keys:
        allowed = jnp.where(place_ < SLOT, has, 0.0)
        return jnp.where(column < 2, (allowed - 1.0) * BIG, 0.0).astype(BF16)
    return has.astype(BF16)


def shift_in(source, wide):
    wide[0:1056] = source[0:1056].astype(F32)
    wide[1056:ROWS] = jnp.zeros((ROWS - 1056, D), F32)
    wide[1056:1058] = source[1056:1058].astype(F32)


def halves():
    for slot in range(2):
        for part in range(2):
            start = PAD * slot + 272 * part
            yield SLOT * slot + 272 * part, slice(start, start + 272), part


def attend_kernel(
    split, wq, w_out, pb, pc, up_bias, v0, v1, v2, v3, v4, v5, v6, v7, x, dy,
    wa_out, ww, wb0, wc0, wb1, wc1, e_out, xp_out, n1t_out, dyp_out, dyt_out, m_out, att_out, lt_out,
    wa, vv, xs, n1, e, xp, n1t, dyp, dyt, m, att, lt, lacc, qmask, kmask, qb, pa, pw, slab,
    send_sem, recv_sem, own_sem, out_sem,
):
    dp, aa, ba, half, core, peers = place()
    greet(peers)
    for kind in range(3):
        pa[:, GROUP * kind : GROUP * kind + GROUP] = wq[kind]
    pa[:, 3 * GROUP :] = jnp.zeros((GROUP, WIDE - 3 * GROUP), BF16)
    pw[:, :GROUP] = w_out[...].T
    pw[:, GROUP:] = jnp.zeros((GROUP, STEP - GROUP), BF16)
    lines = [v[...].astype(F32) for v in (v0, v1, v2, v3, v4, v5, v6, v7)]
    lines += [up_bias[:, 48 * i : 48 * i + 48].astype(F32) for i in range(4)]
    slab[...] = jnp.zeros((16, 128), BF16)
    slab[:, :48] = jnp.concatenate(lines + [jnp.zeros((4, 48), F32)], axis=0).astype(BF16)
    meet(peers)
    sends = Sends(send_sem, recv_sem, peers)
    where = (aa, ba, half)
    first, second = (slice(None), slice(0, STEP)), (slice(None), slice(STEP, 2 * STEP))
    parts = (
        (pw, ww), (pb.at[first], wb0), (pc.at[first], wc0), (pb.at[second], wb1), (pc.at[second], wc1),
    )
    own = [
        pltpu.make_async_copy(part, whole.at[aa, ba], own_sem.at[i])
        for i, (part, whole) in enumerate(((pa, wa), (slab, vv)) + parts)
    ]
    for copy in own:
        copy.start()
    for j in (1, 2, 3):
        sends.start(("v", j), slab, vv.at[aa, ba], f"z{j}")
    a0, a1 = (Gather(f"a{i}", sends, where, pa, wa, 96 * i, 96) for i in (0, 1))
    o0, b0, c0, b1, c1 = (
        Gather(f"b{i}", sends, where, part, whole, 0, GROUP)
        for i, (part, whole) in enumerate(parts)
    )
    outs = []

    def put(source, target):
        copy = pltpu.make_async_copy(source, target, out_sem.at[len(outs)])
        copy.start()
        outs.append(copy)

    a0.first()
    shift_in(dy, xs)
    line = lax.broadcasted_iota(jnp.int32, (272, D), 0)
    total = jnp.zeros((1, D), F32)
    for source, target, part in halves():
        value = xs[source : source + 272]
        if part == 1:
            value = jnp.where(line < SLOT - 272, value, 0.0)
        total = total + jnp.sum(value, axis=0, keepdims=True)
        dyp[target] = value.astype(BF16)
    put(dyp, dyp_out)
    for copy in own:
        copy.wait()
    a0.second()
    a1.first()
    sends.arrived(*[("v", j) for j in (1, 2, 3)])
    sends.start(("v", "y"), vv.at[aa], vv.at[aa], "y")
    sends.start(("v", "c"), vv.at[aa], vv.at[aa], "c")
    shift_in(x, xs)
    for source, target, part in halves():
        xp[target] = xs[source : source + 272].astype(BF16)
    put(xp, xp_out)
    sends.arrived(("v", "y"), ("v", "c"))
    sends.start(("v", "cy"), vv.at[lax.rem(aa + 2, 4)], vv.at[lax.rem(aa + 2, 4)], "c")
    a0.third()
    a1.second()
    o0.first()
    dyt[...] = dyp[...].T
    put(dyt, dyt_out)
    sends.arrived(("v", "cy"))
    spread, keep, choose = slab_maps()
    wide = dot(vv[...].reshape(256, 128), spread.astype(BF16))
    e[...] = exact_dot(choose, wide * keep)
    e[12:13] = total
    put(e, e_out)
    gain, offset = e[0:1], e[1:2]
    for source, target, part in halves():
        shifted, rate = norm_parts(xs[source : source + 272])
        n1[target] = (shifted * rate * gain + offset).astype(BF16)
    a0.fourth()
    a1.third()
    o0.second()
    b0.first()
    n1t[...] = n1[...].T
    put(n1t, n1t_out)
    for slot in range(2):
        qmask[slot] = mask_columns(split[slot], False)
        kmask[slot] = mask_columns(split[slot], True)
    zero = jnp.zeros((1, GROUP), F32)
    for group in range(4):
        lanes = slice(GROUP * group, GROUP * group + GROUP)
        qb[group] = jnp.concatenate((e[2:3, lanes], zero, e[3:4, lanes]), axis=1)
    lacc[...] = jnp.zeros_like(lacc)
    a1.fourth()
    a0.last()
    a1.last()
    put(wa, wa_out)

    def project(group):
        weights = wa[group].reshape(D, WIDE)
        for part in range(4):
            rows = slice(272 * part, 272 * part + 272)
            mixed = dot(n1[rows], weights[:, : 3 * GROUP]) + qb[group]
            m[group, rows] = mixed.astype(BF16)

    def look(group, slot):
        rows = slice(PAD * slot, PAD * slot + PAD)
        for head in range(3):
            cols = slice(HEAD_DIM * head, HEAD_DIM * head + HEAD_DIM)
            both = m[group, rows]
            q = both[:, HEAD_DIM * head : HEAD_DIM * (head + 1)] * 0.125
            k = both[:, GROUP + HEAD_DIM * head : GROUP + HEAD_DIM * (head + 1)]
            v = both[:, 2 * GROUP + HEAD_DIM * head : 2 * GROUP + HEAD_DIM * (head + 1)]
            qx = jnp.concatenate((q.astype(BF16), qmask[slot]), axis=1)
            kx = jnp.concatenate((k, kmask[slot]), axis=1)
            scores = dot(qx, kx, NT)
            top = jnp.max(scores, axis=1, keepdims=True)
            terms = jnp.exp(scores - top)
            total = jnp.sum(terms, axis=1, keepdims=True)
            mixed = dot(terms.astype(BF16), v) / total
            att[group, rows, cols] = mixed.astype(BF16)
            lane = lax.broadcasted_iota(jnp.int32, (PAD, 128), 1)
            lacc[slot] = jnp.where(lane == 3 * group + head, top + jnp.log(total), lacc[slot])

    pumps = (
        (o0.third, b0.second, c0.first),
        (b1.first,),
        (o0.fourth, b0.third, c0.second),
        (b1.second, c1.first),
        (o0.last, b0.fourth, c0.third),
        (b0.last, b1.third, c1.second),
        (c0.fourth, b1.fourth, c1.third),
        (c0.last, b1.last, c1.fourth),
    )
    for group in range(4):
        project(group)
        put(m.at[group], m_out.at[group])
        for slot in range(2):
            look(group, slot)
            for step in pumps[2 * group + slot]:
                step()
    put(att, att_out)
    row = lax.broadcasted_iota(jnp.int32, (16, 128), 0)
    eye = (row == lax.broadcasted_iota(jnp.int32, (16, 128), 1)).astype(F32)
    for slot in range(2):
        lt[slot] = exact_dot(eye, lacc[slot], NT)
    put(lt, lt_out)
    c1.last()
    sends.finish()
    for copy in outs:
        copy.wait()


def attend(split_at, wq, w_out, pb, pc, up_bias, vectors, inputs, cotangent):
    vm = pl.BlockSpec(memory_space=pltpu.VMEM)
    hbm = pl.BlockSpec(memory_space=pl.ANY)
    whole = (4, 4, GROUP, WIDE)
    piece = ((4, 4, GROUP, STEP), BF16)
    shapes = [
        (whole, BF16), piece, piece, piece, piece, piece, ((16, D), F32), ((ROWS, D), BF16),
        ((D, ROWS), BF16), ((ROWS, D), BF16), ((D, ROWS), BF16), ((4, ROWS, 3 * GROUP), BF16),
        ((4, ROWS, GROUP), BF16), ((2, 16, PAD), F32),
    ]
    count = 7 * 26 + 6
    return pl.pallas_call(
        attend_kernel,
        out_shape=tuple(jax.ShapeDtypeStruct(*shape) for shape in shapes),
        in_specs=[pl.BlockSpec(memory_space=pltpu.SMEM)] + [vm] * 15,
        out_specs=[hbm] * len(shapes),
        scratch_shapes=[
            pltpu.VMEM(whole, BF16),
            pltpu.VMEM((4, 4, 16, 128), BF16),
            pltpu.VMEM((ROWS, D), F32),
            pltpu.VMEM((ROWS, D), BF16),
        ]
        + [pltpu.VMEM(*shape) for shape in shapes[6:]]
        + [
            pltpu.VMEM((2, PAD, 128), F32),
            pltpu.VMEM((2, PAD, HEAD_DIM), BF16),
            pltpu.VMEM((2, PAD, HEAD_DIM), BF16),
            pltpu.VMEM((4, 1, 3 * GROUP), F32),
            pltpu.VMEM((GROUP, WIDE), BF16),
            pltpu.VMEM((GROUP, STEP), BF16),
            pltpu.VMEM((16, 128), BF16),
            pltpu.SemaphoreType.DMA((count,)),
            pltpu.SemaphoreType.DMA((count,)),
            pltpu.SemaphoreType.DMA((7,)),
            pltpu.SemaphoreType.DMA((16,)),
        ],
        compiler_params=pltpu.CompilerParams(
            collective_id=0, has_side_effects=True, vmem_limit_bytes=58 * MIB
        ),
    )(split_at, wq, w_out, pb, pc, up_bias, *vectors, inputs, cotangent)


def gelu_parts(hidden):
    size = jnp.abs(hidden)
    t = 1.0 / (1.0 + 0.3 * size)
    bell = jnp.exp(hidden * hidden * -0.5)
    poly = jnp.full_like(t, TAIL[-1])
    for factor in TAIL[-2::-1]:
        poly = poly * t + factor
    tail = poly * t * bell
    phi = jnp.where(hidden < 0, tail, 1.0 - tail)
    return hidden * phi, phi + hidden * bell * (1.0 / math.sqrt(2 * math.pi))


def feed_kernel(
    e, pb, pc, xp_in, dyp_in, dyt_in, att_in, wo_in, wb0, wc0, wb1, wc1,
    out, gvec, ob, oc, gm_out, gatt_out, gwo_out, gb1, gc1, gb2, gc2,
    xp, dyp, dyt, att, wo, w, middle, acc, back, n2, n2t, act, gh, rcb, rcc, *more,
):
    bufs, (send_sem, recv_sem, send_two, recv_two, in_sem, out_sem, own_sem) = more[:-7], more[-7:]
    dp, aa, ba, half, core, peers = place()
    loads = {}
    for name, source, target in (
        ("xp", xp_in, xp), ("att", att_in, att), ("wo", wo_in, wo), ("dyp", dyp_in, dyp),
        ("wb0", wb0, w.at[0, 0]), ("wc0", wc0, w.at[1, 0]), ("dyt", dyt_in, dyt),
        ("wb1", wb1, w.at[0, 1]), ("wc1", wc1, w.at[1, 1]),
    ):
        loads[name] = pltpu.make_async_copy(source, target, in_sem.at[len(loads)])
        loads[name].start()
    third = (slice(None), slice(2 * STEP, 3 * STEP))
    parts = [part.at[third] for part in (pb, pc)]
    own = [
        pltpu.make_async_copy(part, w.at[i, 2, aa, ba], own_sem.at[i])
        for i, part in enumerate(parts)
    ]
    for copy in own:
        copy.start()
    greet(peers)
    where = (aa, ba, half)
    takes = Sends(send_sem, recv_sem, peers)
    gives = Sends(send_two, recv_two, peers)
    tb, tc = (Gather(f"t{i}", takes, where, parts[i], w.at[i, 2], 0, GROUP) for i in (0, 1))
    made = []
    for i, o in enumerate((ob, oc)):
        held = lambda y, i=i: w.at[i, 0, 2 * y + core]
        for kind, row, count in ((SumY, 0, 128), (SumX, 128, 64)):
            at = 5 * len(made)
            made.append(kind(f"s{len(made)}", gives, where, held, o, row, count, bufs[at : at + 5]))
    by, bx, cy, cx = made
    outs = []

    def put(source, target):
        copy = pltpu.make_async_copy(source, target, out_sem.at[len(outs)])
        copy.start()
        outs.append(copy)

    for name in ("xp", "att", "wo"):
        loads[name].wait()
    gvec[...] = jnp.zeros_like(gvec)
    gvec[7:8] = e[12:13]
    for part in range(4):
        rows = slice(272 * part, 272 * part + 272)
        value = xp[rows].astype(F32) + e[4:5]
        for group in range(4):
            value = value + dot(att[group, rows], wo[group, :, 0:GROUP], NT)
        middle[rows] = value
        shifted, rate = norm_parts(value)
        n2[rows] = (shifted * rate * e[5:6] + e[6:7]).astype(BF16)
        acc[rows] = value + e[7:8]
        back[rows] = jnp.zeros((272, D), F32)
        if part == 0:
            meet(peers)
            tb.first()
            tc.first()
    for copy in own:
        copy.wait()
    n2t[...] = n2[...].T
    for name in ("dyp", "wb0", "wc0", "dyt"):
        loads[name].wait()

    def whole_unit(u, forward):
        step, pair, now = u // 2, u % 2, u % 2
        both = ((2 * now, 2 * pair), (2 * now + 1, 2 * pair + 1))
        columns = slice(STEP * step, STEP * step + STEP)

        def weight(kind, group):
            return w[kind, step, group].reshape(D, STEP)

        def up(part):
            rows = slice(272 * part, 272 * part + 272)
            return [
                (
                    dot(n2[rows], weight(0, group)) + e[8 + group : 9 + group, columns],
                    dot(dyp[rows], weight(1, group)),
                )
                for _, group in both
            ]

        def across(part, made, totals):
            rows = slice(272 * part, 272 * part + 272)
            new = []
            for (at, _), (hidden, grad), total in zip(both, made, totals):
                forward, slope = gelu_parts(hidden)
                grad = (grad * slope).astype(BF16)
                act[at, rows] = forward.astype(BF16)
                gh[at, rows] = grad
                new.append(total + jnp.sum(grad.astype(F32), axis=0, keepdims=True))
            return new

        def down(part):
            rows = slice(272 * part, 272 * part + 272)
            for total, values, kind in ((acc, act, 1), (back, gh, 0)):
                more = [dot(values[at, rows], weight(kind, group), NT) for at, group in both]
                total[rows] = total[rows] + more[0] + more[1]

        if forward:
            totals = [jnp.zeros((1, STEP), F32)] * 2
            made = up(0)
            for part in range(4):
                ahead = up(part + 1) if part < 3 else None
                totals = across(part, made, totals)
                if part:
                    down(part - 1)
                made = ahead
            down(3)
            for (_, group), total in zip(both, totals):
                gvec[8 + group : 9 + group, columns] = total
        else:
            for i, (turned, values) in enumerate(((n2t, gh), (dyt, act))):
                for j in range(2):
                    grad = dot(turned[...], values[2 * now + j]).astype(BF16)
                    w[i, step, 2 * pair + j] = grad.reshape(4, GROUP, STEP)

    once = 1 + jnp.minimum(dp, 0)

    def unit(u, forward):
        def inside(_, carry):
            whole_unit(u, forward)
            return carry

        lax.fori_loop(0, once, inside, 0)

    unit(0, True)
    tb.second()
    tc.second()
    unit(0, False)
    unit(1, True)
    tb.third()
    tc.third()
    unit(1, False)
    for i, rc in enumerate((rcb, rcc)):
        for y in (0, 1):
            gives.start((i, y), w.at[i, 0, 2 * y + 1 - core], rc.at[y], "c")
    for name in ("wb1", "wc1"):
        loads[name].wait()
    unit(2, True)
    tb.fourth()
    tc.fourth()
    gives.arrived((0, 0), (0, 1))
    by.first(rcb)
    bx.first(rcb)
    gives.arrived((1, 0), (1, 1))
    cy.first(rcc)
    cx.first(rcc)
    unit(2, False)
    unit(3, True)
    tb.last()
    tc.last()
    takes.finish()
    unit(3, False)
    put(w.at[0, 1], gb1)
    put(w.at[1, 1], gc1)
    unit(4, True)
    for batch in made:
        batch.second()
    unit(4, False)
    unit(5, True)
    for batch in made:
        batch.third()
    line = lax.broadcasted_iota(jnp.int32, (16, D), 0)
    out[0:528] = acc[0:528].astype(BF16)
    out[528:544] = jnp.where(line == 0, acc[528:544], acc[543:559]).astype(BF16)
    out[544:1056] = acc[559:1071].astype(BF16)
    out[1056:1058] = acc[1071:1073].astype(BF16)
    unit(5, False)
    put(w.at[0, 2], gb2)
    put(w.at[1, 2], gc2)
    sums = [jnp.zeros((1, D), F32)] * 3
    for part in range(4):
        rows = slice(272 * part, 272 * part + 272)
        shifted, rate = norm_parts(middle[rows])
        hat = shifted * rate
        grad = back[rows]
        inner = grad * e[5:6]
        mean = jnp.mean(inner, axis=-1, keepdims=True)
        along = jnp.mean(inner * hat, axis=-1, keepdims=True)
        total = dyp[rows].astype(F32) + rate * (inner - mean - hat * along)
        middle[rows] = total
        branch = total.astype(BF16)
        n2[rows] = branch
        for i, value in enumerate((grad * hat, grad, branch.astype(F32))):
            sums[i] = sums[i] + jnp.sum(value, axis=0, keepdims=True)
        for group in range(4):
            act[group, rows, 0:GROUP] = dot(branch, wo[group, :, 0:GROUP]).astype(BF16)
        if part == 1:
            for batch in made:
                batch.fourth()
    put(middle, gm_out)
    put(act, gatt_out)
    gvec[5:6] = sums[0]
    gvec[6:7] = sums[1]
    gvec[4:5] = sums[2]
    n2t[...] = n2[...].T
    for group in range(4):
        gh[group, 0:D, 0:GROUP] = dot(n2t[...], att[group]).astype(BF16)
    put(gh.at[:, 0:D], gwo_out)
    for batch in made:
        batch.last()
    gives.finish()
    for copy in outs:
        copy.wait()


def feed(e, pb, pc, xp, dyp, dyt, att, wo, wb0, wc0, wb1, wc1, local):
    vm = pl.BlockSpec(memory_space=pltpu.VMEM)
    hbm = pl.BlockSpec(memory_space=pl.ANY)
    piece = jax.ShapeDtypeStruct((4, 4, GROUP, STEP), BF16)
    own = jax.ShapeDtypeStruct((GROUP, STEP), F32)
    sums = SumY.scratch(128, STEP) + SumX.scratch(64, STEP)
    gives = 4 + 2 * (6 + 10)
    return pl.pallas_call(
        feed_kernel,
        out_shape=(
            jax.ShapeDtypeStruct((local, D), BF16),
            jax.ShapeDtypeStruct((16, D), F32),
            own,
            own,
            jax.ShapeDtypeStruct((ROWS, D), F32),
            jax.ShapeDtypeStruct((4, ROWS, STEP), BF16),
            jax.ShapeDtypeStruct((4, D, STEP), BF16),
            piece,
            piece,
            piece,
            piece,
        ),
        in_specs=[vm] * 3 + [hbm] * 9,
        out_specs=[vm] * 4 + [hbm] * 7,
        scratch_shapes=[
            pltpu.VMEM((ROWS, D), BF16),
            pltpu.VMEM((ROWS, D), BF16),
            pltpu.VMEM((D, ROWS), BF16),
            pltpu.VMEM((4, ROWS, GROUP), BF16),
            pltpu.VMEM((4, D, STEP), BF16),
            pltpu.VMEM((2, 3, 4, 4, GROUP, STEP), BF16),
            pltpu.VMEM((ROWS, D), F32),
            pltpu.VMEM((ROWS, D), F32),
            pltpu.VMEM((ROWS, D), F32),
            pltpu.VMEM((ROWS, D), BF16),
            pltpu.VMEM((D, ROWS), BF16),
            pltpu.VMEM((4, ROWS, STEP), BF16),
            pltpu.VMEM((4, ROWS, STEP), BF16),
            pltpu.VMEM((2, 4, GROUP, STEP), BF16),
            pltpu.VMEM((2, 4, GROUP, STEP), BF16),
        ]
        + sums * 2
        + [
            pltpu.SemaphoreType.DMA((52,)),
            pltpu.SemaphoreType.DMA((52,)),
            pltpu.SemaphoreType.DMA((gives,)),
            pltpu.SemaphoreType.DMA((gives,)),
            pltpu.SemaphoreType.DMA((9,)),
            pltpu.SemaphoreType.DMA((7,)),
            pltpu.SemaphoreType.DMA((2,)),
        ],
        compiler_params=pltpu.CompilerParams(
            collective_id=2, has_side_effects=True, vmem_limit_bytes=60 * MIB
        ),
    )(e, pb, pc, xp, dyp, dyt, att, wo, wb0, wc0, wb1, wc1)


def unattend_kernel(
    split, e, lt, gvec, ob0, oc0, xp_in, n1t_in, m_in, gatt_in, wa_in, gm_in, gwo, gb1, gc1, gb2, gc2,
    gin, oa, ow, ob, oc, ov,
    xp, n1t, m, gatt, ga, gm, h, rc, rca, rya, fin, gmix, back, sums, gv, qmask, kmask,
    vh, vc, vy, vz, vx, *more,
):
    bufs, (send_sem, recv_sem, own_sem, in_sem) = more[:-4], more[-4:]
    dp, aa, ba, half, core, peers = place()
    greet(peers)
    yy = aa // 2
    order = [2 * (1 - yy) + 1 - core, 2 * (1 - yy) + core, 2 * yy + 1 - core, 2 * yy + core]
    loads = {}

    def load(name, source, target):
        loads[name] = pltpu.make_async_copy(source, target, in_sem.at[len(loads)])
        loads[name].start()

    for k in range(4):
        load(("m", k), m_in.at[order[k]], m.at[order[k]])
        load(("gatt", k), gatt_in.at[order[k]], gatt.at[order[k]])
        if k == 0:
            load("n1t", n1t_in, n1t)
            load("wa", wa_in, ga)
    load("xp", xp_in, xp)
    load("gm", gm_in, gm)
    own = []
    given = (gb1, gc1, gb2, gc2, gwo)
    for i, g in enumerate(given):
        for y in (0, 1):
            own.append(pltpu.make_async_copy(g.at[2 * y + core], h.at[i, y], own_sem.at[len(own)]))
            own[-1].start()
    sends = Sends(send_sem, recv_sem, peers)
    where = (aa, ba, half)
    made = []
    for i, o in enumerate((ob, oc, ob, oc, ow)):
        if i < 4:
            o = o.at[:, STEP * (1 + i // 2) : STEP * (2 + i // 2)]
        held = lambda y, i=i: h.at[i, y]
        for kind, row, count in ((SumY, 0, 64), (SumX, 64, 128)):
            at = 5 * len(made)
            made.append(kind(f"s{len(made)}", sends, where, held, o, row, count, bufs[at : at + 5]))
            made[-1].open = functools.partial(made[-1].first, rc.at[i])
    for i in range(3):
        at = 5 * len(made)
        held = lambda y: fin
        made.append(SumY(f"a{i}", sends, where, held, oa, 64 * i, 64, bufs[at : at + 5]))
    by1, bx1, cy1, cx1, by2, bx2, cy2, cx2, wy, wx, a0, a1, a2 = made
    for slot in range(2):
        qmask[slot] = mask_columns(split[slot], False)
        kmask[slot] = mask_columns(split[slot], True)
    back[...] = jnp.zeros_like(back)

    def look(group, slot):
        rows = slice(PAD * slot, PAD * slot + PAD)
        for head in range(3):
            both = m[group, rows]
            q = (both[:, HEAD_DIM * head : HEAD_DIM * (head + 1)] * 0.125).astype(BF16)
            k = both[:, GROUP + HEAD_DIM * head : GROUP + HEAD_DIM * (head + 1)]
            v = both[:, 2 * GROUP + HEAD_DIM * head : 2 * GROUP + HEAD_DIM * (head + 1)]
            go = gatt[group, rows][:, HEAD_DIM * head : HEAD_DIM * (head + 1)]
            qx = jnp.concatenate((q, qmask[slot]), axis=1)
            kx = jnp.concatenate((k, kmask[slot]), axis=1)
            scores = dot(kx, qx, NT)
            probs = jnp.exp(scores - lt[slot, pl.ds(3 * group + head, 1)])
            gprobs = dot(v, go, NT)
            both_ = probs * gprobs
            delta = jnp.sum(both_, axis=0, keepdims=True)
            gs = (both_ - probs * delta).astype(BF16)
            gq = dot(gs, k, TN) * 0.125
            gk = dot(gs, q)
            gval = dot(probs.astype(BF16), go)
            for i, value in enumerate((gq, gk, gval)):
                at = GROUP * i + HEAD_DIM * head
                gmix[rows, at : at + HEAD_DIM] = value.astype(BF16)

    def grads(k):
        group = order[k]
        grad = dot(n1t[...], gmix[...]).reshape(4, GROUP, 3 * GROUP)
        if k in (1, 3):
            sends.arrived(("a", k - 1))
            terms = [rca.at[k // 2]]
            if k == 3:
                sends.arrived(("a", 1))
                terms.append(rya)
            for term in terms:
                grad = grad + term[:, :, 0 : 3 * GROUP].astype(F32)
        given = fin if k == 3 else ga.at[group]
        given[:, :, 0 : 3 * GROUP] = grad.astype(BF16)
        if k == 3:
            given[:, :, 3 * GROUP :] = jnp.zeros((4, GROUP, WIDE - 3 * GROUP), BF16)

    def fold(group):
        weights = ga[group].reshape(D, WIDE)[:, : 3 * GROUP]
        total = jnp.zeros((1, 3 * GROUP), F32)
        for part in range(4):
            rows = slice(272 * part, 272 * part + 272)
            total = total + jnp.sum(gmix[rows].astype(F32), axis=0, keepdims=True)
            back[rows] = back[rows] + dot(gmix[rows], weights, NT)
        sums[group] = total

    def store(k):
        group = order[k]
        fold(group)
        grads(k)
        if k == 1:
            sends.start(("a", 1), ga.at[group], rya, "y")
        elif k < 3:
            sends.start(("a", k), ga.at[group], rca.at[k // 2], "c")

    def begin():
        meet(peers)
        for i, g in enumerate(given):
            for y in (0, 1):
                sends.start((i, y), g.at[2 * y + 1 - core], rc.at[i, y], "c")

    def settle():
        ob[:, 0:STEP] = ob0[...]
        oc[:, 0:STEP] = oc0[...]
        for copy in own:
            copy.wait()
        for i in range(5):
            sends.arrived((i, 0), (i, 1))
        for name in ("n1t", "wa"):
            loads[name].wait()

    pumps = (
        (begin,),
        (settle, by1.open, cy1.open, bx1.open),
        (cx1.open, by2.open, cy2.open, wy.open),
        (by1.second, cy1.second, bx1.second, wx.open),
        (cx1.second, bx2.open, by2.second, cy2.second, wy.second),
        (by1.third, cy1.third, bx1.third, wx.second, cx2.open),
        (cx1.third, by2.third, cy2.third, wy.third, bx2.second),
        (by1.fourth, cy1.fourth, bx1.fourth, wx.third, cx2.second),
    )
    for k in range(4):
        loads[("m", k)].wait()
        loads[("gatt", k)].wait()
        for slot in range(2):
            look(order[k], slot)
            for step in pumps[2 * k + slot]:
                step()
        if k < 3:
            store(k)
    grads(3)
    for batch in (a0, a1, a2):
        mine = batch.held(yy)
        batch.start_x = functools.partial(batch.send, ("x",), mine.at[:, batch.theirs], batch.bufs[3], "x")
    a0.start_x()
    fold(order[3])
    for step in (cx1.fourth, by2.fourth, cy2.fourth, wy.fourth, wx.fourth, bx2.third, cx2.third):
        step()
    loads["xp"].wait()
    loads["gm"].wait()
    tot_gain, tot_bias = jnp.zeros((1, D), F32), jnp.zeros((1, D), F32)
    for part in range(4):
        rows = slice(272 * part, 272 * part + 272)
        shifted, rate = norm_parts(xp[rows].astype(F32))
        hat = shifted * rate
        grad = back[rows]
        inner = grad * e[0:1]
        mean = jnp.mean(inner, axis=-1, keepdims=True)
        along = jnp.mean(inner * hat, axis=-1, keepdims=True)
        tot_gain = tot_gain + jnp.sum(grad * hat, axis=0, keepdims=True)
        tot_bias = tot_bias + jnp.sum(grad, axis=0, keepdims=True)
        back[rows] = gm[rows] + rate * (inner - mean - hat * along)
        if part == 2:
            a0.third()
            a1.start_x()
    line = lax.broadcasted_iota(jnp.int32, (16, D), 0)
    q_row = jnp.concatenate([sums[i][:, :GROUP] for i in range(4)], axis=1)
    v_row = jnp.concatenate([sums[i][:, 2 * GROUP :] for i in range(4)], axis=1)
    rows = jnp.where(line == 0, tot_gain, jnp.where(line == 1, tot_bias, gvec[...]))
    rows = jnp.where(line == 2, q_row, jnp.where(line == 3, v_row, rows))
    spread, keep, choose = slab_maps()
    wide = exact_dot(choose, rows, TN) * keep
    gv[...] = exact_dot(wide, spread, NT).reshape(4, 4, 16, 128)
    for y in (0, 1):
        sends.start(("v", "c", y), gv.at[2 * y + 1 - core], vc.at[y], "c")
    a1.third()
    a2.start_x()
    for y in (0, 1):
        sends.arrived(("v", "c", y))
        vh[y] = gv[2 * y + core] + vc[y]
    sends.start(("v", "y"), vh.at[1 - yy], vy, "y")
    gin[0:528] = back[0:528].astype(BF16)
    gin[528:544] = jnp.where(line == 0, back[528:544], back[543:559]).astype(BF16)
    gin[544:1056] = back[559:1071].astype(BF16)
    gin[1056:1058] = back[1071:1073].astype(BF16)
    a0.fourth()
    bx2.fourth()
    cx2.fourth()
    sends.arrived(("v", "y"))
    vh[yy] = vh[yy] + vy[...]
    for j in (1, 2, 3):
        sends.start(("v", "z", j), vh.at[yy, lax.rem(ba + j, 4)], vz.at[j - 1], f"z{j}")
    for batch in made[:10]:
        batch.last()
    a2.third()
    a1.fourth()
    sends.arrived(*[("v", "z", j) for j in (1, 2, 3)])
    vh[yy, ba] = vh[yy, ba] + (vz[0] + vz[1] + vz[2])
    sends.start(("v", "x"), vh.at[yy, ba], vx, "x")
    a2.fourth()
    sends.arrived(("v", "x"))
    ov[...] = vh[yy, ba] + vx[...]
    a0.last()
    a1.last()
    a2.last()
    sends.finish()


def unattend(split_at, e, lt, gvec, ob0, oc0, *stored, local):
    vm = pl.BlockSpec(memory_space=pltpu.VMEM)
    hbm = pl.BlockSpec(memory_space=pl.ANY)
    out = jax.ShapeDtypeStruct((GROUP, D), F32)
    count = 10 + 5 * 16 + 3 + 3 * 5 + 7
    return pl.pallas_call(
        unattend_kernel,
        out_shape=(
            jax.ShapeDtypeStruct((local, D), BF16),
            jax.ShapeDtypeStruct((GROUP, WIDE), F32),
            jax.ShapeDtypeStruct((GROUP, STEP), F32),
            out, out,
            jax.ShapeDtypeStruct((16, 128), F32),
        ),
        in_specs=[pl.BlockSpec(memory_space=pltpu.SMEM)] + [vm] * 5 + [hbm] * 11,
        out_specs=[vm] * 6,
        scratch_shapes=[
            pltpu.VMEM((ROWS, D), BF16),
            pltpu.VMEM((D, ROWS), BF16),
            pltpu.VMEM((4, ROWS, 3 * GROUP), BF16),
            pltpu.VMEM((4, ROWS, STEP), BF16),
            pltpu.VMEM((4, 4, GROUP, WIDE), BF16),
            pltpu.VMEM((ROWS, D), F32),
            pltpu.VMEM((5, 2, 4, GROUP, STEP), BF16),
            pltpu.VMEM((5, 2, 4, GROUP, STEP), BF16),
            pltpu.VMEM((2, 4, GROUP, WIDE), BF16),
            pltpu.VMEM((4, GROUP, WIDE), BF16),
            pltpu.VMEM((4, GROUP, WIDE), BF16),
            pltpu.VMEM((ROWS, 3 * GROUP), BF16),
            pltpu.VMEM((ROWS, D), F32),
            pltpu.VMEM((4, 1, 3 * GROUP), F32),
            pltpu.VMEM((4, 4, 16, 128), F32),
            pltpu.VMEM((2, PAD, HEAD_DIM), BF16),
            pltpu.VMEM((2, PAD, HEAD_DIM), BF16),
            pltpu.VMEM((2, 4, 16, 128), F32),
            pltpu.VMEM((2, 4, 16, 128), F32),
            pltpu.VMEM((4, 16, 128), F32),
            pltpu.VMEM((3, 16, 128), F32),
            pltpu.VMEM((16, 128), F32),
        ]
        + (SumY.scratch(64, STEP) + SumX.scratch(128, STEP)) * 5
        + SumY.scratch(64, WIDE) * 3
        + [
            pltpu.SemaphoreType.DMA((count,)),
            pltpu.SemaphoreType.DMA((count,)),
            pltpu.SemaphoreType.DMA((10,)),
            pltpu.SemaphoreType.DMA((13,)),
        ],
        compiler_params=pltpu.CompilerParams(
            collective_id=1, has_side_effects=True, vmem_limit_bytes=62 * MIB
        ),
    )(split_at, e, lt, gvec, ob0, oc0, *stored)


def results_kernel(output, gin, oa, ow, ob, oc, ov, out, gin_out, qkv, wo, up, down, up_bias, *rows):
    out[...] = output[...]
    gin_out[...] = gin[...]
    for kind in range(3):
        qkv[kind] = oa[:, GROUP * kind : GROUP * kind + GROUP]
    wo[...] = ow[...].T[:GROUP]
    up[...] = ob[...]
    down[...] = oc[...]
    up_bias[...] = jnp.concatenate([ov[i : i + 1, :48] for i in range(8, 12)], axis=1)[0]
    for i, row in enumerate(rows):
        row[...] = ov[i, :48]


def results(output, gin, oa, ow, ob, oc, ov):
    shapes = [(3, GROUP, GROUP), (GROUP, GROUP), (GROUP, D), (GROUP, D), (GROUP,)] + [(48,)] * 8
    return pl.pallas_call(
        results_kernel,
        out_shape=[jax.ShapeDtypeStruct(gin.shape, BF16)] * 2
        + [jax.ShapeDtypeStruct(shape, F32) for shape in shapes],
        compiler_params=pltpu.CompilerParams(vmem_limit_bytes=60 * MIB),
    )(output, gin, oa, ow, ob, oc, ov)


def on_device(
    inputs, cotangent, split_at, ln1_gain, ln1_bias, w_qkv, q_bias, v_bias, w_out, o_bias,
    ln2_gain, ln2_bias, w_up, up_bias, w_down, down_bias,
):
    vectors = [
        v.reshape(1, 48)
        for v in (ln1_gain, ln1_bias, q_bias, v_bias, o_bias, ln2_gain, ln2_bias, down_bias)
    ]
    wq = w_qkv.transpose(1, 0, 2)
    pc = w_down.T
    local = inputs.shape[0]
    wa, ww, *pieces, e, xp, n1t, dyp, dyt, m, att, lt = attend(
        split_at, wq, w_out, w_up, pc, up_bias.reshape(1, 192), vectors, inputs, cotangent
    )
    output, gvec, ob0, oc0, gm, gatt, gwo, *grads = feed(
        e, w_up, pc, xp, dyp, dyt, att, ww.reshape(4, D, STEP), *pieces, local
    )
    gwo = gwo.reshape(4, 4, GROUP, STEP)
    gin, oa, ow, ob, oc, ov = unattend(
        split_at, e, lt, gvec, ob0, oc0, xp, n1t, m, gatt, wa, gm, gwo, *grads, local=local
    )
    if lax.axis_size("dp") > 2:
        oa, ow, ob, oc, ov = (lax.psum(v, "dp") * 0.5 for v in (oa, ow, ob, oc, ov))
    output, gin, qkv, wo, up, down, up_row, *rows = results(output, gin, oa, ow, ob, oc, ov)
    return (
        output,
        gin,
        rows[0],
        rows[1],
        qkv.transpose(1, 0, 2),
        rows[2],
        rows[3],
        wo,
        rows[4],
        rows[5],
        rows[6],
        up,
        up_row,
        down.T,
        rows[7],
    )


def solution(mesh):
    rows = P(("dp", "aa", "ba"), None)
    vec = P(("aa", "ba"))
    grid_qkv, first, second = P("ba", None, "aa"), P("aa", "ba"), P("ba", "aa")
    params = (vec, vec, grid_qkv, vec, vec, first, vec, vec, vec, second, vec, first, vec)
    return jax.shard_map(
        on_device,
        mesh=mesh,
        in_specs=(rows, rows, P(("dp", "aa", "ba"))) + params,
        out_specs=(rows, rows) + params,
        check_vma=False,
    )
```

```python
import functools
import math

import jax
import jax.numpy as jnp
from jax import lax
from jax.experimental import pallas as pl
from jax.experimental.pallas import tpu as pltpu
from jax.sharding import PartitionSpec as P

D = 768
HEADS = 12
HEAD_DIM = 64
SLOT = 529
PAD = 544
ROWS = 2 * PAD
STEP = 256
WIDE = 640
GROUP = 192
BIG = 1e30
MESH = pl.DeviceIdType.MESH
F32 = jnp.float32
BF16 = jnp.bfloat16
MIB = 1 << 20

NT = (((1,), (1,)), ((), ()))
NN = (((1,), (0,)), ((), ()))
TN = (((0,), (0,)), ((), ()))

TAIL = (
    0.11962926248861097,
    0.12075451364069298,
    0.09991001218129214,
    0.12857310923328652,
    -0.0537053561953165,
    0.20637712218096793,
    -0.15721681637037743,
    0.03567808025645831,
)


def dot(left, right, dims=NN):
    return lax.dot_general(left, right, dims, preferred_element_type=F32)


def exact_dot(left, right, dims=NN):
    return lax.dot_general(
        left, right, dims, preferred_element_type=F32, precision=lax.Precision.HIGHEST
    )


def place():
    dp, aa, ba = lax.axis_index("dp"), lax.axis_index("aa"), lax.axis_index("ba")
    half, core = lax.rem(dp, 2), lax.rem(aa, 2)
    peers = {
        "x": (dp + 1 - 2 * half, aa, ba),
        "y": (dp, lax.rem(aa + 2, 4), ba),
        "c": (dp, aa + 1 - 2 * core, ba),
        "z1": (dp, aa, lax.rem(ba + 1, 4)),
        "z2": (dp, aa, lax.rem(ba + 2, 4)),
        "z3": (dp, aa, lax.rem(ba + 3, 4)),
    }
    return dp, aa, ba, half, core, peers


def greet(peers):
    barrier = pltpu.get_barrier_semaphore()
    for peer in peers.values():
        pl.semaphore_signal(barrier, inc=1, device_id=peer, device_id_type=MESH)


def meet(peers):
    pl.semaphore_wait(pltpu.get_barrier_semaphore(), len(peers))


class Sends:
    def __init__(self, send_sem, recv_sem, peers):
        self.send_sem, self.recv_sem, self.peers = send_sem, recv_sem, peers
        self.made = {}

    def start(self, name, src, dst, peer):
        at = len(self.made)
        copy = pltpu.make_async_remote_copy(
            src_ref=src,
            dst_ref=dst,
            send_sem=self.send_sem.at[at],
            recv_sem=self.recv_sem.at[at],
            device_id=self.peers[peer],
            device_id_type=MESH,
        )
        copy.start()
        self.made[name] = copy

    def arrived(self, *names):
        for name in names:
            self.made[name].wait_recv()

    def finish(self):
        for copy in self.made.values():
            copy.wait_send()


def sixteen(value):
    return pl.multiple_of(value, 16)


class Gather:
    def __init__(self, name, sends, where, part, whole, row, count):
        self.name, self.sends, self.part, self.whole = name, sends, part, whole
        self.aa, self.ba, self.half = where
        self.ay = lax.rem(self.aa + 2, 4)
        self.other = [(j, lax.rem(self.ba + j, 4)) for j in (1, 2, 3)]
        big, small = count // 3, count // 6
        self.big = pl.ds(sixteen(row + big * self.half), big)
        self.big_not = pl.ds(sixteen(row + big - big * self.half), big)
        self.small = pl.ds(sixteen(row + 2 * big + small * self.half), small)
        self.rest = pl.ds(row + 2 * big, big)

    def send(self, key, src, dst, peer):
        self.sends.start((self.name,) + key, src, dst, peer)

    def move(self, key, at, peer):
        self.send(key, self.whole.at[at], self.whole.at[at], peer)

    def got(self, *keys):
        self.sends.arrived(*[(self.name,) + key for key in keys])

    def first(self):
        w, aa, ba = self.whole, self.aa, self.ba
        for j in (1, 2, 3):
            self.send(("z", j), self.part.at[self.big], w.at[aa, ba, self.big], f"z{j}")
        self.send(("y",), self.part.at[self.small], w.at[aa, ba, self.small], "y")
        for j in (1, 2, 3):
            self.send(("zs", j), self.part.at[self.small], w.at[aa, ba, self.small], f"z{j}")

    def second(self):
        self.got(("z", 1), ("z", 2), ("z", 3))
        for j, z in self.other:
            self.move(("x", j), (self.aa, z, self.big), "x")
        self.move(("yb",), (self.aa, slice(None), self.big), "y")
        self.got(("y",))
        for j in (1, 2, 3):
            self.move(("zy", j), (self.ay, self.ba, self.small), f"z{j}")
        self.got(("zs", 1), ("zs", 2), ("zs", 3))
        for j, z in self.other:
            self.move(("xs", j), (self.aa, z, self.small), "x")
        self.move(("c0",), (self.aa, slice(None), self.big), "c")

    def third(self):
        every = slice(None)
        self.got(("x", 1), ("x", 2), ("x", 3))
        self.move(("yn",), (self.aa, every, self.big_not), "y")
        self.got(("zy", 1), ("zy", 2), ("zy", 3))
        self.move(("xy",), (self.ay, every, self.small), "x")
        self.got(("yb",))
        self.move(("c1",), (self.aa, every, self.big_not), "c")
        self.move(("c2",), (self.ay, every, self.big), "c")

    def fourth(self):
        every = slice(None)
        self.got(("xs", 1), ("xs", 2), ("xs", 3))
        self.move(("c3",), (self.aa, every, self.rest), "c")
        self.got(("yn",))
        self.move(("c4",), (self.ay, every, self.big_not), "c")
        self.got(("xy",))
        self.move(("c5",), (self.ay, every, self.rest), "c")

    def last(self):
        self.got(*[(f"c{i}",) for i in range(6)])


class Sum:
    def __init__(self, name, sends, where, held, out, row, count, bufs):
        self.name, self.sends, self.held, self.out, self.bufs = name, sends, held, out, bufs
        part = count // 2
        self.aa, self.ba, self.half = where
        self.yy = self.aa // 2
        self.yn = 1 - self.yy
        self.other = [(j, lax.rem(self.ba + j, 4)) for j in (1, 2, 3)]
        self.rows = pl.ds(row, count)
        self.mine = pl.ds(sixteen(row + part * self.half), part)
        self.theirs = pl.ds(sixteen(row + part - part * self.half), part)

    def send(self, key, src, dst, peer):
        self.sends.start((self.name,) + key, src, dst, peer)

    def got(self, *keys):
        self.sends.arrived(*[(self.name,) + key for key in keys])

    def add(self, h, rows, more):
        @pl.loop(0, 4)
        def _(z):
            h[z, rows] = (h[z, rows].astype(F32) + more[z].astype(F32)).astype(BF16)

    def add_core(self, rc):
        for y in (0, 1):
            self.add(self.held(y), self.rows, rc.at[y, :, self.rows])

    def over_z(self, h, key, at):
        for j, z in self.other:
            self.send(key + (j,), h.at[z, self.mine], at(j - 1), f"z{j}")

    def close(self, total, own, far):
        own[...] = total.astype(BF16)
        self.send(("f",), own, far, "x")

    def last(self):
        own, far = self.bufs[:2]
        self.out[self.mine] = own[...].astype(F32)
        self.got(("f",))
        self.out[self.theirs] = far[...].astype(F32)


class SumY(Sum):
    @staticmethod
    def scratch(count, width):
        part = count // 2
        return [
            pltpu.VMEM((part, width), BF16),
            pltpu.VMEM((part, width), BF16),
            pltpu.VMEM((4, count, width), BF16),
            pltpu.VMEM((4, part, width), BF16),
            pltpu.VMEM((3, part, width), BF16),
        ]

    def first(self, rc):
        self.add_core(rc)
        self.send(("y",), self.held(self.yn).at[:, self.rows], self.bufs[2], "y")

    def second(self):
        self.got(("y",))
        h = self.held(self.yy)
        self.add(h, self.rows, self.bufs[2])
        self.send(("x",), h.at[:, self.theirs], self.bufs[3], "x")

    def third(self):
        self.got(("x",))
        h = self.held(self.yy)
        self.add(h, self.mine, self.bufs[3])
        self.over_z(h, ("z",), lambda i: self.bufs[4].at[i])

    def fourth(self):
        self.got(("z", 1), ("z", 2), ("z", 3))
        total = self.held(self.yy)[self.ba, self.mine].astype(F32)
        for i in range(3):
            total = total + self.bufs[4][i].astype(F32)
        self.close(total, self.bufs[0], self.bufs[1])


class SumX(Sum):
    @staticmethod
    def scratch(count, width):
        part = count // 2
        return [
            pltpu.VMEM((part, width), BF16),
            pltpu.VMEM((part, width), BF16),
            pltpu.VMEM((2, 4, part, width), BF16),
            pltpu.VMEM((2, 3, part, width), BF16),
            pltpu.VMEM((part, width), BF16),
        ]

    def first(self, rc):
        self.add_core(rc)
        for y in (0, 1):
            self.send(("x", y), self.held(y).at[:, self.theirs], self.bufs[2].at[y], "x")

    def second(self):
        self.got(("x", 0), ("x", 1))
        for y in (0, 1):
            h = self.held(y)
            self.add(h, self.mine, self.bufs[2].at[y])
            self.over_z(h, ("z", y), lambda i, y=y: self.bufs[3].at[y, i])

    def third(self):
        for y in (0, 1):
            h = self.held(y)
            self.got(("z", y, 1), ("z", y, 2), ("z", y, 3))
            total = h[self.ba, self.mine].astype(F32)
            for i in range(3):
                total = total + self.bufs[3][y, i].astype(F32)
            h[self.ba, self.mine] = total.astype(BF16)
        self.send(("y",), self.held(self.yn).at[self.ba, self.mine], self.bufs[4], "y")

    def fourth(self):
        self.got(("y",))
        total = self.held(self.yy)[self.ba, self.mine].astype(F32) + self.bufs[4][...].astype(F32)
        self.close(total, self.bufs[0], self.bufs[1])


def slab_maps():
    lane = lax.broadcasted_iota(jnp.int32, (128, D), 0)
    column = lax.broadcasted_iota(jnp.int32, (128, D), 1)
    spread = (lax.rem(column, 48) == lane).astype(F32)
    line = lax.broadcasted_iota(jnp.int32, (256, D), 0)
    block = lax.broadcasted_iota(jnp.int32, (256, D), 1) // 48
    device, kind = line // 16, lax.rem(line, 16)
    wanted = jnp.where(kind < 8, device, 4 * lax.rem(device, 4) + kind - 8)
    keep = jnp.where((wanted == block) & (kind < 12), 1.0, 0.0).astype(F32)
    line = lax.broadcasted_iota(jnp.int32, (16, 256), 1)
    out = lax.broadcasted_iota(jnp.int32, (16, 256), 0)
    device, kind = line // 16, lax.rem(line, 16)
    choose = (jnp.where(kind < 8, kind, 8 + device // 4) == out).astype(F32)
    return spread, keep, choose


def norm_parts(value):
    centre = jnp.mean(value, axis=-1, keepdims=True)
    shifted = value - centre
    spread = jnp.mean(shifted * shifted, axis=-1, keepdims=True)
    return shifted, lax.rsqrt(spread + 1e-6)


def mask_columns(split, keys):
    place_ = lax.broadcasted_iota(jnp.int32, (PAD, HEAD_DIM), 0)
    column = lax.broadcasted_iota(jnp.int32, (PAD, HEAD_DIM), 1)
    first = jnp.where(place_ < split, 1.0, 0.0)
    has = jnp.where(column == 0, first, jnp.where(column == 1, 1.0 - first, 0.0))
    if keys:
        allowed = jnp.where(place_ < SLOT, has, 0.0)
        return jnp.where(column < 2, (allowed - 1.0) * BIG, 0.0).astype(BF16)
    return has.astype(BF16)


def shift_in(source, wide):
    wide[0:1056] = source[0:1056].astype(F32)
    wide[1056:ROWS] = jnp.zeros((ROWS - 1056, D), F32)
    wide[1056:1058] = source[1056:1058].astype(F32)


def halves():
    for slot in range(2):
        for part in range(2):
            start = PAD * slot + 272 * part
            yield SLOT * slot + 272 * part, slice(start, start + 272), part


def attend_kernel(
    split, wq, w_out, pb, pc, up_bias, v0, v1, v2, v3, v4, v5, v6, v7, x, dy,
    wa_out, ww, wb0, wc0, wb1, wc1, e_out, xp_out, n1t_out, dyp_out, dyt_out, m_out, att_out, lt_out,
    wa, vv, xs, n1, e, xp, n1t, dyp, dyt, m, att, lt, lacc, qmask, kmask, qb, pa, pw, slab,
    send_sem, recv_sem, own_sem, out_sem,
):
    dp, aa, ba, half, core, peers = place()
    greet(peers)
    for kind in range(3):
        pa[:, GROUP * kind : GROUP * kind + GROUP] = wq[kind]
    pa[:, 3 * GROUP :] = jnp.zeros((GROUP, WIDE - 3 * GROUP), BF16)
    pw[:, :GROUP] = w_out[...].T
    pw[:, GROUP:] = jnp.zeros((GROUP, STEP - GROUP), BF16)
    lines = [v[...].astype(F32) for v in (v0, v1, v2, v3, v4, v5, v6, v7)]
    wide = up_bias[...].astype(F32).reshape(1, 192)
    lines += [wide[:, 48 * i : 48 * i + 48] for i in range(4)]
    slab[...] = jnp.zeros((16, 128), BF16)
    slab[:, :48] = jnp.concatenate(lines + [jnp.zeros((4, 48), F32)], axis=0).astype(BF16)
    meet(peers)
    sends = Sends(send_sem, recv_sem, peers)
    where = (aa, ba, half)
    first, second = (slice(None), slice(0, STEP)), (slice(None), slice(STEP, 2 * STEP))
    parts = (
        (pw, ww), (pb.at[first], wb0), (pc.at[first], wc0), (pb.at[second], wb1), (pc.at[second], wc1),
    )
    own = [
        pltpu.make_async_copy(part, whole.at[aa, ba], own_sem.at[i])
        for i, (part, whole) in enumerate(((pa, wa), (slab, vv)) + parts)
    ]
    for copy in own:
        copy.start()
    for j in (1, 2, 3):
        sends.start(("v", j), slab, vv.at[aa, ba], f"z{j}")
    a0, a1 = (Gather(f"a{i}", sends, where, pa, wa, 96 * i, 96) for i in (0, 1))
    o0, b0, c0, b1, c1 = (
        Gather(f"b{i}", sends, where, part, whole, 0, GROUP)
        for i, (part, whole) in enumerate(parts)
    )
    outs = []

    def put(source, target):
        copy = pltpu.make_async_copy(source, target, out_sem.at[len(outs)])
        copy.start()
        outs.append(copy)

    a0.first()
    shift_in(dy, xs)
    line = lax.broadcasted_iota(jnp.int32, (272, D), 0)
    total = jnp.zeros((1, D), F32)
    for source, target, part in halves():
        value = xs[source : source + 272]
        if part == 1:
            value = jnp.where(line < SLOT - 272, value, 0.0)
        total = total + jnp.sum(value, axis=0, keepdims=True)
        dyp[target] = value.astype(BF16)
    put(dyp, dyp_out)
    for copy in own:
        copy.wait()
    a0.second()
    a1.first()
    sends.arrived(*[("v", j) for j in (1, 2, 3)])
    sends.start(("v", "y"), vv.at[aa], vv.at[aa], "y")
    sends.start(("v", "c"), vv.at[aa], vv.at[aa], "c")
    shift_in(x, xs)
    for source, target, part in halves():
        xp[target] = xs[source : source + 272].astype(BF16)
    put(xp, xp_out)
    sends.arrived(("v", "y"), ("v", "c"))
    sends.start(("v", "cy"), vv.at[lax.rem(aa + 2, 4)], vv.at[lax.rem(aa + 2, 4)], "c")
    a0.third()
    a1.second()
    o0.first()
    dyt[...] = dyp[...].T
    put(dyt, dyt_out)
    sends.arrived(("v", "cy"))
    spread, keep, choose = slab_maps()
    wide = dot(vv[...].reshape(256, 128), spread.astype(BF16))
    e[...] = exact_dot(choose, wide * keep)
    e[12:13] = total
    put(e, e_out)
    gain, offset = e[0:1], e[1:2]
    for source, target, part in halves():
        shifted, rate = norm_parts(xs[source : source + 272])
        n1[target] = (shifted * rate * gain + offset).astype(BF16)
    a0.fourth()
    a1.third()
    o0.second()
    b0.first()
    n1t[...] = n1[...].T
    put(n1t, n1t_out)
    for slot in range(2):
        qmask[slot] = mask_columns(split[slot], False)
        kmask[slot] = mask_columns(split[slot], True)
    zero = jnp.zeros((1, GROUP), F32)
    for group in range(4):
        lanes = slice(GROUP * group, GROUP * group + GROUP)
        qb[group] = jnp.concatenate((e[2:3, lanes], zero, e[3:4, lanes]), axis=1)
    lacc[...] = jnp.zeros_like(lacc)
    a1.fourth()
    a0.last()
    a1.last()
    put(wa, wa_out)

    def project(group):
        weights = wa[group].reshape(D, WIDE)
        for part in range(4):
            rows = slice(272 * part, 272 * part + 272)
            mixed = dot(n1[rows], weights[:, : 3 * GROUP]) + qb[group]
            m[group, rows] = mixed.astype(BF16)

    def look(group, slot):
        rows = slice(PAD * slot, PAD * slot + PAD)
        for head in range(3):
            cols = slice(HEAD_DIM * head, HEAD_DIM * head + HEAD_DIM)
            both = m[group, rows]
            q = both[:, HEAD_DIM * head : HEAD_DIM * (head + 1)] * 0.125
            k = both[:, GROUP + HEAD_DIM * head : GROUP + HEAD_DIM * (head + 1)]
            v = both[:, 2 * GROUP + HEAD_DIM * head : 2 * GROUP + HEAD_DIM * (head + 1)]
            qx = jnp.concatenate((q.astype(BF16), qmask[slot]), axis=1)
            kx = jnp.concatenate((k, kmask[slot]), axis=1)
            scores = dot(qx, kx, NT)
            top = jnp.max(scores, axis=1, keepdims=True)
            terms = jnp.exp(scores - top)
            total = jnp.sum(terms, axis=1, keepdims=True)
            mixed = dot(terms.astype(BF16), v) / total
            att[group, rows, cols] = mixed.astype(BF16)
            lane = lax.broadcasted_iota(jnp.int32, (PAD, 128), 1)
            lacc[slot] = jnp.where(lane == 3 * group + head, top + jnp.log(total), lacc[slot])

    pumps = (
        (o0.third, b0.second, c0.first),
        (b1.first,),
        (o0.fourth, b0.third, c0.second),
        (b1.second, c1.first),
        (o0.last, b0.fourth, c0.third),
        (b0.last, b1.third, c1.second),
        (c0.fourth, b1.fourth, c1.third),
        (c0.last, b1.last, c1.fourth),
    )
    for group in range(4):
        project(group)
        put(m.at[group], m_out.at[group])
        for slot in range(2):
            look(group, slot)
            for step in pumps[2 * group + slot]:
                step()
    put(att, att_out)
    row = lax.broadcasted_iota(jnp.int32, (16, 128), 0)
    eye = (row == lax.broadcasted_iota(jnp.int32, (16, 128), 1)).astype(F32)
    for slot in range(2):
        lt[slot] = exact_dot(eye, lacc[slot], NT)
    put(lt, lt_out)
    c1.last()
    sends.finish()
    for copy in outs:
        copy.wait()


def attend(split_at, wq, w_out, pb, pc, up_bias, vectors, inputs, cotangent):
    vm = pl.BlockSpec(memory_space=pltpu.VMEM)
    hbm = pl.BlockSpec(memory_space=pl.ANY)
    whole = (4, 4, GROUP, WIDE)
    piece = ((4, 4, GROUP, STEP), BF16)
    shapes = [
        (whole, BF16), piece, piece, piece, piece, piece, ((16, D), F32), ((ROWS, D), BF16),
        ((D, ROWS), BF16), ((ROWS, D), BF16), ((D, ROWS), BF16), ((4, ROWS, 3 * GROUP), BF16),
        ((4, ROWS, GROUP), BF16), ((2, 16, PAD), F32),
    ]
    count = 7 * 26 + 6
    return pl.pallas_call(
        attend_kernel,
        out_shape=tuple(jax.ShapeDtypeStruct(*shape) for shape in shapes),
        in_specs=[pl.BlockSpec(memory_space=pltpu.SMEM)] + [vm] * 15,
        out_specs=[hbm] * len(shapes),
        scratch_shapes=[
            pltpu.VMEM(whole, BF16),
            pltpu.VMEM((4, 4, 16, 128), BF16),
            pltpu.VMEM((ROWS, D), F32),
            pltpu.VMEM((ROWS, D), BF16),
        ]
        + [pltpu.VMEM(*shape) for shape in shapes[6:]]
        + [
            pltpu.VMEM((2, PAD, 128), F32),
            pltpu.VMEM((2, PAD, HEAD_DIM), BF16),
            pltpu.VMEM((2, PAD, HEAD_DIM), BF16),
            pltpu.VMEM((4, 1, 3 * GROUP), F32),
            pltpu.VMEM((GROUP, WIDE), BF16),
            pltpu.VMEM((GROUP, STEP), BF16),
            pltpu.VMEM((16, 128), BF16),
            pltpu.SemaphoreType.DMA((count,)),
            pltpu.SemaphoreType.DMA((count,)),
            pltpu.SemaphoreType.DMA((7,)),
            pltpu.SemaphoreType.DMA((16,)),
        ],
        compiler_params=pltpu.CompilerParams(
            collective_id=0, has_side_effects=True, vmem_limit_bytes=58 * MIB
        ),
    )(split_at, wq, w_out, pb, pc, up_bias, *vectors, inputs, cotangent)


def gelu_parts(hidden):
    size = jnp.abs(hidden)
    t = 1.0 / (1.0 + 0.3 * size)
    bell = jnp.exp(hidden * hidden * -0.5)
    poly = jnp.full_like(t, TAIL[-1])
    for factor in TAIL[-2::-1]:
        poly = poly * t + factor
    tail = poly * t * bell
    phi = jnp.where(hidden < 0, tail, 1.0 - tail)
    return hidden * phi, phi + hidden * bell * (1.0 / math.sqrt(2 * math.pi))


def feed_kernel(
    e, pb, pc, xp_in, dyp_in, dyt_in, att_in, wo_in, wb0, wc0, wb1, wc1,
    out, gvec, ob, oc, gm_out, gatt_out, gwo_out, gb1, gc1, gb2, gc2,
    xp, dyp, dyt, att, wo, w, middle, acc, back, n2, n2t, act, gh, rcb, rcc, *more,
):
    bufs, (send_sem, recv_sem, send_two, recv_two, in_sem, out_sem, own_sem) = more[:-7], more[-7:]
    dp, aa, ba, half, core, peers = place()
    loads = {}
    for name, source, target in (
        ("xp", xp_in, xp), ("att", att_in, att), ("wo", wo_in, wo), ("dyp", dyp_in, dyp),
        ("wb0", wb0, w.at[0, 0]), ("wc0", wc0, w.at[1, 0]), ("dyt", dyt_in, dyt),
        ("wb1", wb1, w.at[0, 1]), ("wc1", wc1, w.at[1, 1]),
    ):
        loads[name] = pltpu.make_async_copy(source, target, in_sem.at[len(loads)])
        loads[name].start()
    third = (slice(None), slice(2 * STEP, 3 * STEP))
    parts = [part.at[third] for part in (pb, pc)]
    own = [
        pltpu.make_async_copy(part, w.at[i, 2, aa, ba], own_sem.at[i])
        for i, part in enumerate(parts)
    ]
    for copy in own:
        copy.start()
    greet(peers)
    where = (aa, ba, half)
    takes = Sends(send_sem, recv_sem, peers)
    gives = Sends(send_two, recv_two, peers)
    tb, tc = (Gather(f"t{i}", takes, where, parts[i], w.at[i, 2], 0, GROUP) for i in (0, 1))
    made = []
    for i, o in enumerate((ob, oc)):
        held = lambda y, i=i: w.at[i, 0, 2 * y + core]
        for kind, row, count in ((SumY, 0, 128), (SumX, 128, 64)):
            at = 5 * len(made)
            made.append(kind(f"s{len(made)}", gives, where, held, o, row, count, bufs[at : at + 5]))
    by, bx, cy, cx = made
    outs = []

    def put(source, target):
        copy = pltpu.make_async_copy(source, target, out_sem.at[len(outs)])
        copy.start()
        outs.append(copy)

    for name in ("xp", "att", "wo"):
        loads[name].wait()
    gvec[...] = jnp.zeros_like(gvec)
    gvec[7:8] = e[12:13]
    for part in range(4):
        rows = slice(272 * part, 272 * part + 272)
        value = xp[rows].astype(F32) + e[4:5]
        for group in range(4):
            value = value + dot(att[group, rows], wo[group, :, 0:GROUP], NT)
        middle[rows] = value
        shifted, rate = norm_parts(value)
        n2[rows] = (shifted * rate * e[5:6] + e[6:7]).astype(BF16)
        acc[rows] = value + e[7:8]
        back[rows] = jnp.zeros((272, D), F32)
        if part == 0:
            meet(peers)
            tb.first()
            tc.first()
    for copy in own:
        copy.wait()
    n2t[...] = n2[...].T
    for name in ("dyp", "wb0", "wc0", "dyt"):
        loads[name].wait()

    def whole_unit(u, forward):
        step, pair, now = u // 2, u % 2, u % 2
        both = ((2 * now, 2 * pair), (2 * now + 1, 2 * pair + 1))
        columns = slice(STEP * step, STEP * step + STEP)

        def weight(kind, group):
            return w[kind, step, group].reshape(D, STEP)

        def up(part):
            rows = slice(272 * part, 272 * part + 272)
            return [
                (
                    dot(n2[rows], weight(0, group)) + e[8 + group : 9 + group, columns],
                    dot(dyp[rows], weight(1, group)),
                )
                for _, group in both
            ]

        def across(part, made, totals):
            rows = slice(272 * part, 272 * part + 272)
            new = []
            for (at, _), (hidden, grad), total in zip(both, made, totals):
                forward, slope = gelu_parts(hidden)
                grad = (grad * slope).astype(BF16)
                act[at, rows] = forward.astype(BF16)
                gh[at, rows] = grad
                new.append(total + jnp.sum(grad.astype(F32), axis=0, keepdims=True))
            return new

        def down(part):
            rows = slice(272 * part, 272 * part + 272)
            for total, values, kind in ((acc, act, 1), (back, gh, 0)):
                more = [dot(values[at, rows], weight(kind, group), NT) for at, group in both]
                total[rows] = total[rows] + more[0] + more[1]

        if forward:
            totals = [jnp.zeros((1, STEP), F32)] * 2
            made = up(0)
            for part in range(4):
                ahead = up(part + 1) if part < 3 else None
                totals = across(part, made, totals)
                if part:
                    down(part - 1)
                made = ahead
            down(3)
            for (_, group), total in zip(both, totals):
                gvec[8 + group : 9 + group, columns] = total
        else:
            for i, (turned, values) in enumerate(((n2t, gh), (dyt, act))):
                for j in range(2):
                    grad = dot(turned[...], values[2 * now + j]).astype(BF16)
                    w[i, step, 2 * pair + j] = grad.reshape(4, GROUP, STEP)

    once = 1 + jnp.minimum(dp, 0)

    def unit(u, forward):
        def inside(_, carry):
            whole_unit(u, forward)
            return carry

        lax.fori_loop(0, once, inside, 0)

    unit(0, True)
    tb.second()
    tc.second()
    unit(0, False)
    unit(1, True)
    tb.third()
    tc.third()
    unit(1, False)
    for i, rc in enumerate((rcb, rcc)):
        for y in (0, 1):
            gives.start((i, y), w.at[i, 0, 2 * y + 1 - core], rc.at[y], "c")
    for name in ("wb1", "wc1"):
        loads[name].wait()
    unit(2, True)
    tb.fourth()
    tc.fourth()
    gives.arrived((0, 0), (0, 1))
    by.first(rcb)
    bx.first(rcb)
    gives.arrived((1, 0), (1, 1))
    cy.first(rcc)
    cx.first(rcc)
    unit(2, False)
    unit(3, True)
    tb.last()
    tc.last()
    takes.finish()
    unit(3, False)
    put(w.at[0, 1], gb1)
    put(w.at[1, 1], gc1)
    unit(4, True)
    for batch in made:
        batch.second()
    unit(4, False)
    unit(5, True)
    for batch in made:
        batch.third()
    line = lax.broadcasted_iota(jnp.int32, (16, D), 0)
    out[0:528] = acc[0:528].astype(BF16)
    out[528:544] = jnp.where(line == 0, acc[528:544], acc[543:559]).astype(BF16)
    out[544:1056] = acc[559:1071].astype(BF16)
    out[1056:1058] = acc[1071:1073].astype(BF16)
    unit(5, False)
    put(w.at[0, 2], gb2)
    put(w.at[1, 2], gc2)
    sums = [jnp.zeros((1, D), F32)] * 3
    for part in range(4):
        rows = slice(272 * part, 272 * part + 272)
        shifted, rate = norm_parts(middle[rows])
        hat = shifted * rate
        grad = back[rows]
        inner = grad * e[5:6]
        mean = jnp.mean(inner, axis=-1, keepdims=True)
        along = jnp.mean(inner * hat, axis=-1, keepdims=True)
        total = dyp[rows].astype(F32) + rate * (inner - mean - hat * along)
        middle[rows] = total
        branch = total.astype(BF16)
        n2[rows] = branch
        for i, value in enumerate((grad * hat, grad, branch.astype(F32))):
            sums[i] = sums[i] + jnp.sum(value, axis=0, keepdims=True)
        for group in range(4):
            act[group, rows, 0:GROUP] = dot(branch, wo[group, :, 0:GROUP]).astype(BF16)
        if part == 1:
            for batch in made:
                batch.fourth()
    put(middle, gm_out)
    put(act, gatt_out)
    gvec[5:6] = sums[0]
    gvec[6:7] = sums[1]
    gvec[4:5] = sums[2]
    n2t[...] = n2[...].T
    for group in range(4):
        gh[group, 0:D, 0:GROUP] = dot(n2t[...], att[group]).astype(BF16)
    put(gh.at[:, 0:D], gwo_out)
    for batch in made:
        batch.last()
    gives.finish()
    for copy in outs:
        copy.wait()


def feed(e, pb, pc, xp, dyp, dyt, att, wo, wb0, wc0, wb1, wc1, local):
    vm = pl.BlockSpec(memory_space=pltpu.VMEM)
    hbm = pl.BlockSpec(memory_space=pl.ANY)
    piece = jax.ShapeDtypeStruct((4, 4, GROUP, STEP), BF16)
    own = jax.ShapeDtypeStruct((GROUP, STEP), F32)
    sums = SumY.scratch(128, STEP) + SumX.scratch(64, STEP)
    gives = 4 + 2 * (6 + 10)
    return pl.pallas_call(
        feed_kernel,
        out_shape=(
            jax.ShapeDtypeStruct((local, D), BF16),
            jax.ShapeDtypeStruct((16, D), F32),
            own,
            own,
            jax.ShapeDtypeStruct((ROWS, D), F32),
            jax.ShapeDtypeStruct((4, ROWS, STEP), BF16),
            jax.ShapeDtypeStruct((4, D, STEP), BF16),
            piece,
            piece,
            piece,
            piece,
        ),
        in_specs=[vm] * 3 + [hbm] * 9,
        out_specs=[vm] * 4 + [hbm] * 7,
        scratch_shapes=[
            pltpu.VMEM((ROWS, D), BF16),
            pltpu.VMEM((ROWS, D), BF16),
            pltpu.VMEM((D, ROWS), BF16),
            pltpu.VMEM((4, ROWS, GROUP), BF16),
            pltpu.VMEM((4, D, STEP), BF16),
            pltpu.VMEM((2, 3, 4, 4, GROUP, STEP), BF16),
            pltpu.VMEM((ROWS, D), F32),
            pltpu.VMEM((ROWS, D), F32),
            pltpu.VMEM((ROWS, D), F32),
            pltpu.VMEM((ROWS, D), BF16),
            pltpu.VMEM((D, ROWS), BF16),
            pltpu.VMEM((4, ROWS, STEP), BF16),
            pltpu.VMEM((4, ROWS, STEP), BF16),
            pltpu.VMEM((2, 4, GROUP, STEP), BF16),
            pltpu.VMEM((2, 4, GROUP, STEP), BF16),
        ]
        + sums * 2
        + [
            pltpu.SemaphoreType.DMA((52,)),
            pltpu.SemaphoreType.DMA((52,)),
            pltpu.SemaphoreType.DMA((gives,)),
            pltpu.SemaphoreType.DMA((gives,)),
            pltpu.SemaphoreType.DMA((9,)),
            pltpu.SemaphoreType.DMA((7,)),
            pltpu.SemaphoreType.DMA((2,)),
        ],
        compiler_params=pltpu.CompilerParams(
            collective_id=2, has_side_effects=True, vmem_limit_bytes=60 * MIB
        ),
    )(e, pb, pc, xp, dyp, dyt, att, wo, wb0, wc0, wb1, wc1)


def unattend_kernel(
    split, e, lt, gvec, ob0, oc0, xp_in, n1t_in, m_in, gatt_in, wa_in, gm_in, gwo, gb1, gc1, gb2, gc2,
    gin, oa, ow, ob, oc, ov,
    xp, n1t, m, gatt, ga, gm, h, rc, rca, rya, fin, gmix, back, sums, gv, qmask, kmask,
    vh, vc, vy, vz, vx, *more,
):
    bufs, (send_sem, recv_sem, own_sem, in_sem) = more[:-4], more[-4:]
    dp, aa, ba, half, core, peers = place()
    greet(peers)
    yy = aa // 2
    order = [2 * (1 - yy) + 1 - core, 2 * (1 - yy) + core, 2 * yy + 1 - core, 2 * yy + core]
    loads = {}

    def load(name, source, target):
        loads[name] = pltpu.make_async_copy(source, target, in_sem.at[len(loads)])
        loads[name].start()

    for k in range(4):
        load(("m", k), m_in.at[order[k]], m.at[order[k]])
        load(("gatt", k), gatt_in.at[order[k]], gatt.at[order[k]])
        if k == 0:
            load("n1t", n1t_in, n1t)
            load("wa", wa_in, ga)
    load("xp", xp_in, xp)
    load("gm", gm_in, gm)
    own = []
    given = (gb1, gc1, gb2, gc2, gwo)
    for i, g in enumerate(given):
        for y in (0, 1):
            own.append(pltpu.make_async_copy(g.at[2 * y + core], h.at[i, y], own_sem.at[len(own)]))
            own[-1].start()
    sends = Sends(send_sem, recv_sem, peers)
    where = (aa, ba, half)
    made = []
    for i, o in enumerate((ob, oc, ob, oc, ow)):
        if i < 4:
            o = o.at[:, STEP * (1 + i // 2) : STEP * (2 + i // 2)]
        held = lambda y, i=i: h.at[i, y]
        for kind, row, count in ((SumY, 0, 64), (SumX, 64, 128)):
            at = 5 * len(made)
            made.append(kind(f"s{len(made)}", sends, where, held, o, row, count, bufs[at : at + 5]))
            made[-1].open = functools.partial(made[-1].first, rc.at[i])
    for i in range(3):
        at = 5 * len(made)
        held = lambda y: fin
        made.append(SumY(f"a{i}", sends, where, held, oa, 64 * i, 64, bufs[at : at + 5]))
    by1, bx1, cy1, cx1, by2, bx2, cy2, cx2, wy, wx, a0, a1, a2 = made
    for slot in range(2):
        qmask[slot] = mask_columns(split[slot], False)
        kmask[slot] = mask_columns(split[slot], True)
    back[...] = jnp.zeros_like(back)

    def look(group, slot):
        rows = slice(PAD * slot, PAD * slot + PAD)
        for head in range(3):
            both = m[group, rows]
            q = (both[:, HEAD_DIM * head : HEAD_DIM * (head + 1)] * 0.125).astype(BF16)
            k = both[:, GROUP + HEAD_DIM * head : GROUP + HEAD_DIM * (head + 1)]
            v = both[:, 2 * GROUP + HEAD_DIM * head : 2 * GROUP + HEAD_DIM * (head + 1)]
            go = gatt[group, rows][:, HEAD_DIM * head : HEAD_DIM * (head + 1)]
            qx = jnp.concatenate((q, qmask[slot]), axis=1)
            kx = jnp.concatenate((k, kmask[slot]), axis=1)
            scores = dot(kx, qx, NT)
            probs = jnp.exp(scores - lt[slot, pl.ds(3 * group + head, 1)])
            gprobs = dot(v, go, NT)
            both_ = probs * gprobs
            delta = jnp.sum(both_, axis=0, keepdims=True)
            gs = (both_ - probs * delta).astype(BF16)
            gq = dot(gs, k, TN) * 0.125
            gk = dot(gs, q)
            gval = dot(probs.astype(BF16), go)
            for i, value in enumerate((gq, gk, gval)):
                at = GROUP * i + HEAD_DIM * head
                gmix[rows, at : at + HEAD_DIM] = value.astype(BF16)

    def grads(k):
        group = order[k]
        grad = dot(n1t[...], gmix[...]).reshape(4, GROUP, 3 * GROUP)
        if k in (1, 3):
            sends.arrived(("a", k - 1))
            terms = [rca.at[k // 2]]
            if k == 3:
                sends.arrived(("a", 1))
                terms.append(rya)
            for term in terms:
                grad = grad + term[:, :, 0 : 3 * GROUP].astype(F32)
        given = fin if k == 3 else ga.at[group]
        given[:, :, 0 : 3 * GROUP] = grad.astype(BF16)
        if k == 3:
            given[:, :, 3 * GROUP :] = jnp.zeros((4, GROUP, WIDE - 3 * GROUP), BF16)

    def fold(group):
        weights = ga[group].reshape(D, WIDE)[:, : 3 * GROUP]
        total = jnp.zeros((1, 3 * GROUP), F32)
        for part in range(4):
            rows = slice(272 * part, 272 * part + 272)
            total = total + jnp.sum(gmix[rows].astype(F32), axis=0, keepdims=True)
            back[rows] = back[rows] + dot(gmix[rows], weights, NT)
        sums[group] = total

    def store(k):
        group = order[k]
        fold(group)
        grads(k)
        if k == 1:
            sends.start(("a", 1), ga.at[group], rya, "y")
        elif k < 3:
            sends.start(("a", k), ga.at[group], rca.at[k // 2], "c")

    def begin():
        meet(peers)
        for i, g in enumerate(given):
            for y in (0, 1):
                sends.start((i, y), g.at[2 * y + 1 - core], rc.at[i, y], "c")

    def settle():
        ob[:, 0:STEP] = ob0[...]
        oc[:, 0:STEP] = oc0[...]
        for copy in own:
            copy.wait()
        for i in range(5):
            sends.arrived((i, 0), (i, 1))
        for name in ("n1t", "wa"):
            loads[name].wait()

    pumps = (
        (begin,),
        (settle, by1.open, cy1.open, bx1.open),
        (cx1.open, by2.open, cy2.open, wy.open),
        (by1.second, cy1.second, bx1.second, wx.open),
        (cx1.second, bx2.open, by2.second, cy2.second, wy.second),
        (by1.third, cy1.third, bx1.third, wx.second, cx2.open),
        (cx1.third, by2.third, cy2.third, wy.third, bx2.second),
        (by1.fourth, cy1.fourth, bx1.fourth, wx.third, cx2.second),
    )
    for k in range(4):
        loads[("m", k)].wait()
        loads[("gatt", k)].wait()
        for slot in range(2):
            look(order[k], slot)
            for step in pumps[2 * k + slot]:
                step()
        if k < 3:
            store(k)
    grads(3)
    for batch in (a0, a1, a2):
        mine = batch.held(yy)
        batch.start_x = functools.partial(batch.send, ("x",), mine.at[:, batch.theirs], batch.bufs[3], "x")
    a0.start_x()
    fold(order[3])
    for step in (cx1.fourth, by2.fourth, cy2.fourth, wy.fourth, wx.fourth, bx2.third, cx2.third):
        step()
    loads["xp"].wait()
    loads["gm"].wait()
    tot_gain, tot_bias = jnp.zeros((1, D), F32), jnp.zeros((1, D), F32)
    for part in range(4):
        rows = slice(272 * part, 272 * part + 272)
        shifted, rate = norm_parts(xp[rows].astype(F32))
        hat = shifted * rate
        grad = back[rows]
        inner = grad * e[0:1]
        mean = jnp.mean(inner, axis=-1, keepdims=True)
        along = jnp.mean(inner * hat, axis=-1, keepdims=True)
        tot_gain = tot_gain + jnp.sum(grad * hat, axis=0, keepdims=True)
        tot_bias = tot_bias + jnp.sum(grad, axis=0, keepdims=True)
        back[rows] = gm[rows] + rate * (inner - mean - hat * along)
        if part == 2:
            a0.third()
            a1.start_x()
    line = lax.broadcasted_iota(jnp.int32, (16, D), 0)
    q_row = jnp.concatenate([sums[i][:, :GROUP] for i in range(4)], axis=1)
    v_row = jnp.concatenate([sums[i][:, 2 * GROUP :] for i in range(4)], axis=1)
    rows = jnp.where(line == 0, tot_gain, jnp.where(line == 1, tot_bias, gvec[...]))
    rows = jnp.where(line == 2, q_row, jnp.where(line == 3, v_row, rows))
    spread, keep, choose = slab_maps()
    wide = exact_dot(choose, rows, TN) * keep
    gv[...] = exact_dot(wide, spread, NT).reshape(4, 4, 16, 128)
    for y in (0, 1):
        sends.start(("v", "c", y), gv.at[2 * y + 1 - core], vc.at[y], "c")
    a1.third()
    a2.start_x()
    for y in (0, 1):
        sends.arrived(("v", "c", y))
        vh[y] = gv[2 * y + core] + vc[y]
    sends.start(("v", "y"), vh.at[1 - yy], vy, "y")
    gin[0:528] = back[0:528].astype(BF16)
    gin[528:544] = jnp.where(line == 0, back[528:544], back[543:559]).astype(BF16)
    gin[544:1056] = back[559:1071].astype(BF16)
    gin[1056:1058] = back[1071:1073].astype(BF16)
    a0.fourth()
    bx2.fourth()
    cx2.fourth()
    sends.arrived(("v", "y"))
    vh[yy] = vh[yy] + vy[...]
    for j in (1, 2, 3):
        sends.start(("v", "z", j), vh.at[yy, lax.rem(ba + j, 4)], vz.at[j - 1], f"z{j}")
    for batch in made[:10]:
        batch.last()
    a2.third()
    a1.fourth()
    sends.arrived(*[("v", "z", j) for j in (1, 2, 3)])
    vh[yy, ba] = vh[yy, ba] + (vz[0] + vz[1] + vz[2])
    sends.start(("v", "x"), vh.at[yy, ba], vx, "x")
    a2.fourth()
    sends.arrived(("v", "x"))
    ov[...] = vh[yy, ba] + vx[...]
    a0.last()
    a1.last()
    a2.last()
    sends.finish()


def unattend(split_at, e, lt, gvec, ob0, oc0, *stored, local):
    vm = pl.BlockSpec(memory_space=pltpu.VMEM)
    hbm = pl.BlockSpec(memory_space=pl.ANY)
    out = jax.ShapeDtypeStruct((GROUP, D), F32)
    count = 10 + 5 * 16 + 3 + 3 * 5 + 7
    return pl.pallas_call(
        unattend_kernel,
        out_shape=(
            jax.ShapeDtypeStruct((local, D), BF16),
            jax.ShapeDtypeStruct((GROUP, WIDE), F32),
            jax.ShapeDtypeStruct((GROUP, STEP), F32),
            out, out,
            jax.ShapeDtypeStruct((16, 128), F32),
        ),
        in_specs=[pl.BlockSpec(memory_space=pltpu.SMEM)] + [vm] * 5 + [hbm] * 11,
        out_specs=[vm] * 6,
        scratch_shapes=[
            pltpu.VMEM((ROWS, D), BF16),
            pltpu.VMEM((D, ROWS), BF16),
            pltpu.VMEM((4, ROWS, 3 * GROUP), BF16),
            pltpu.VMEM((4, ROWS, STEP), BF16),
            pltpu.VMEM((4, 4, GROUP, WIDE), BF16),
            pltpu.VMEM((ROWS, D), F32),
            pltpu.VMEM((5, 2, 4, GROUP, STEP), BF16),
            pltpu.VMEM((5, 2, 4, GROUP, STEP), BF16),
            pltpu.VMEM((2, 4, GROUP, WIDE), BF16),
            pltpu.VMEM((4, GROUP, WIDE), BF16),
            pltpu.VMEM((4, GROUP, WIDE), BF16),
            pltpu.VMEM((ROWS, 3 * GROUP), BF16),
            pltpu.VMEM((ROWS, D), F32),
            pltpu.VMEM((4, 1, 3 * GROUP), F32),
            pltpu.VMEM((4, 4, 16, 128), F32),
            pltpu.VMEM((2, PAD, HEAD_DIM), BF16),
            pltpu.VMEM((2, PAD, HEAD_DIM), BF16),
            pltpu.VMEM((2, 4, 16, 128), F32),
            pltpu.VMEM((2, 4, 16, 128), F32),
            pltpu.VMEM((4, 16, 128), F32),
            pltpu.VMEM((3, 16, 128), F32),
            pltpu.VMEM((16, 128), F32),
        ]
        + (SumY.scratch(64, STEP) + SumX.scratch(128, STEP)) * 5
        + SumY.scratch(64, WIDE) * 3
        + [
            pltpu.SemaphoreType.DMA((count,)),
            pltpu.SemaphoreType.DMA((count,)),
            pltpu.SemaphoreType.DMA((10,)),
            pltpu.SemaphoreType.DMA((13,)),
        ],
        compiler_params=pltpu.CompilerParams(
            collective_id=1, has_side_effects=True, vmem_limit_bytes=62 * MIB
        ),
    )(split_at, e, lt, gvec, ob0, oc0, *stored)


def results_kernel(output, gin, oa, ow, ob, oc, ov, out, gin_out, qkv, wo, up, down, up_bias, *more):
    rows, (one, two, sem) = more[:-3], more[-3:]
    moves = []
    for i, (source, held, target) in enumerate(((output, one, out), (gin, two, gin_out))):
        into = pltpu.make_async_copy(source, held, sem.at[i])
        into.start()
        moves.append((into, pltpu.make_async_copy(held, target, sem.at[2 + i])))
    for into, away in moves:
        into.wait()
        away.start()
    for kind in range(3):
        qkv[kind] = oa[:, GROUP * kind : GROUP * kind + GROUP]
    wo[...] = ow[...].T[:GROUP]
    up[...] = ob[...]
    down[...] = oc[...]
    up_bias[...] = jnp.concatenate([ov[i : i + 1, :48] for i in range(8, 12)], axis=1)[0]
    for i, row in enumerate(rows):
        row[...] = ov[i, :48]
    for _, away in moves:
        away.wait()


def results(output, gin, oa, ow, ob, oc, ov):
    vm = pl.BlockSpec(memory_space=pltpu.VMEM)
    hbm = pl.BlockSpec(memory_space=pl.ANY)
    shapes = [(3, GROUP, GROUP), (GROUP, GROUP), (GROUP, D), (GROUP, D), (GROUP,)] + [(48,)] * 8
    return pl.pallas_call(
        results_kernel,
        out_shape=[jax.ShapeDtypeStruct(gin.shape, BF16)] * 2
        + [jax.ShapeDtypeStruct(shape, F32) for shape in shapes],
        in_specs=[hbm] * 2 + [vm] * 5,
        out_specs=[hbm] * 2 + [vm] * 13,
        scratch_shapes=[
            pltpu.VMEM(gin.shape, BF16),
            pltpu.VMEM(gin.shape, BF16),
            pltpu.SemaphoreType.DMA((4,)),
        ],
        compiler_params=pltpu.CompilerParams(vmem_limit_bytes=60 * MIB),
    )(output, gin, oa, ow, ob, oc, ov)


def on_device(
    inputs, cotangent, split_at, ln1_gain, ln1_bias, w_qkv, q_bias, v_bias, w_out, o_bias,
    ln2_gain, ln2_bias, w_up, up_bias, w_down, down_bias,
):
    vectors = [
        v.reshape(1, 48)
        for v in (ln1_gain, ln1_bias, q_bias, v_bias, o_bias, ln2_gain, ln2_bias, down_bias)
    ]
    wq = w_qkv.transpose(1, 0, 2)
    pc = w_down.T
    local = inputs.shape[0]
    wa, ww, *pieces, e, xp, n1t, dyp, dyt, m, att, lt = attend(
        split_at, wq, w_out, w_up, pc, up_bias, vectors, inputs, cotangent
    )
    output, gvec, ob0, oc0, gm, gatt, gwo, *grads = feed(
        e, w_up, pc, xp, dyp, dyt, att, ww.reshape(4, D, STEP), *pieces, local
    )
    gwo = gwo.reshape(4, 4, GROUP, STEP)
    gin, oa, ow, ob, oc, ov = unattend(
        split_at, e, lt, gvec, ob0, oc0, xp, n1t, m, gatt, wa, gm, gwo, *grads, local=local
    )
    if lax.axis_size("dp") > 2:
        oa, ow, ob, oc, ov = (lax.psum(v, "dp") * 0.5 for v in (oa, ow, ob, oc, ov))
    output, gin, qkv, wo, up, down, up_row, *rows = results(output, gin, oa, ow, ob, oc, ov)
    return (
        output,
        gin,
        rows[0],
        rows[1],
        qkv.transpose(1, 0, 2),
        rows[2],
        rows[3],
        wo,
        rows[4],
        rows[5],
        rows[6],
        up,
        up_row,
        down.T,
        rows[7],
    )


def solution(mesh):
    rows = P(("dp", "aa", "ba"), None)
    vec = P(("aa", "ba"))
    grid_qkv, first, second = P("ba", None, "aa"), P("aa", "ba"), P("ba", "aa")
    params = (vec, vec, grid_qkv, vec, vec, first, vec, vec, vec, second, vec, first, vec)
    return jax.shard_map(
        on_device,
        mesh=mesh,
        in_specs=(rows, rows, P(("dp", "aa", "ba"))) + params,
        out_specs=(rows, rows) + params,
        check_vma=False,
    )
```
